32 devices in a mesh: win: 8 (over z, y), lat: 4 (over x, core).
Axes of the slice: x: 2, y: 2, z: 4, core: 2. Of those that a mesh axis runs over, the one named last changes fastest.
Arguments:
- model_rhs: float32 [8, 3, 32, 1536], P('win', None, 'lat'), may hold values from -6 to 6
- obs_rhs: float32 [8, 3, 32, 1536], P('win', None, 'lat'), may hold values from -6 to 6
- model_var: float32 [8, 3, 32, 1536], P('win', None, 'lat'), may hold values from 0.3 to 3
- obs_var: float32 [8, 3, 32, 1536], P('win', None, 'lat'), may hold values from 0.3 to 3
- obs_weight: float32 [8, 3, 32, 1536], P('win', None, 'lat'), may hold values from 0.2 to 1.5
- depth: float32 [8, 32, 1536], P('win', 'lat'), may hold values from 0.5 to 1.5
Outputs:
- dual_model: float32 [8, 3, 32, 1536], P('win', None, 'lat')
- dual_obs: float32 [8, 3, 32, 1536], P('win', None, 'lat')
- increment: float32 [8, 3, 32, 1536], P('win', None, 'lat')
The draws below stay inside these ranges and needn't reach their ends.
All inputs are finite; a program needn't handle non-finite values.
Results may differ from the reference program's by a relative error of at most 0.0001.
Values sent between devices are 32-bit elements; how exact they have to be, the bound alone decides.
No kernel may reach another device: no remote copies, remote signals or barrier semaphores. Data moves between devices by JAX's collectives and lax.ppermute only.
A program may use at most 64 MiB of HBM per device.

```python
import math
import jax
import jax.numpy as jnp

NLON = 1536
GRID_ROWS = 768
STEPS = 4
ITERS = 2
NLAT = 32
BAND_START = 368
WINDOWS = 8


def steps_of(stream_key, dims, split, low, high):
    loudness = 1.0
    for axis_at, blocks in split:
        draws = jax.random.uniform(jax.random.fold_in(jax.random.fold_in(stream_key, 6), axis_at), (blocks,), jnp.float32, low / len(split), high / len(split))
        loudness = loudness * jnp.repeat(jnp.exp(draws), dims[axis_at] // blocks).reshape((-1,) + (1,) * (len(dims) - 1 - axis_at))
    return loudness


def normal_values(key, dims, deviation, limit, shards=(), held_as=jnp.bfloat16):
    drawn = jax.random.normal(key, dims, jnp.float32) * deviation
    if len(shards) > 0:
        drawn = steps_of(key, dims, shards, -0.22, 0.18) * drawn
    return jnp.clip(drawn, min=-limit, max=limit).astype(held_as)


def setup_inputs(seed: int = 0) -> dict:
    streams_of = jax.random.split(jax.random.key(seed), 7)
    return {
        "model_rhs": normal_values(streams_of[0], (WINDOWS, 3, NLAT, NLON), 1.0, 6.0, ((0, 8), (2, 4)), jnp.float32),
        "obs_rhs": normal_values(streams_of[1], (WINDOWS, 3, NLAT, NLON), 1.0, 6.0, ((0, 8), (2, 4)), jnp.float32),
        "model_var": jnp.clip(jnp.exp(math.log(3.0) - 2.3025851 * jax.random.uniform(streams_of[2], (WINDOWS, 3, NLAT, NLON), jnp.float32) ** steps_of(streams_of[2], (WINDOWS, 3, NLAT, NLON), ((0, 8), (2, 4)), -0.2, 0.2)), 0.3, 3.0),
        "obs_var": jnp.clip(jnp.exp(math.log(3.0) - 2.3025851 * jax.random.uniform(streams_of[3], (WINDOWS, 3, NLAT, NLON), jnp.float32) ** steps_of(streams_of[3], (WINDOWS, 3, NLAT, NLON), ((0, 8), (2, 4)), -0.2, 0.2)), 0.3, 3.0),
        "obs_weight": jnp.clip(0.2 + 1.3 * jax.random.uniform(streams_of[4], (WINDOWS, 3, NLAT, NLON), jnp.float32) ** steps_of(streams_of[4], (WINDOWS, 3, NLAT, NLON), ((0, 8), (2, 4)), -0.2, 0.2), 0.2, 1.5),
        "depth": jnp.clip(0.5 + 1.0 * jax.random.uniform(streams_of[5], (WINDOWS, NLAT, NLON), jnp.float32) ** steps_of(streams_of[5], (WINDOWS, NLAT, NLON), ((0, 8), (1, 4)), -0.2, 0.2), 0.5, 1.5),
    }


mass_rate = 0.5
press_rate = 0.5
spin_rate = 0.4

def along_lon(field):
    return 0.5 * (jnp.roll(field, -1, axis=-1) - jnp.roll(field, 1, axis=-1))

def along_lat(field):
    widths = [(0, 0)] * (field.ndim - 2) + [(1, 1), (0, 0)]
    padded = jnp.pad(field, widths)
    return 0.5 * (padded[..., 2:, :] - padded[..., :-2, :])

def model_step(state, depth, spin):
    height, east, north = (state[:, 0], state[:, 1], state[:, 2])
    height = height - mass_rate * (along_lon(depth * east) + along_lat(depth * north))
    east = east + mass_rate * spin * north - press_rate * along_lon(height)
    north = north - mass_rate * spin * east - press_rate * along_lat(height)
    return jnp.stack([height, east, north], axis=1)

def inner(left, right):
    return jnp.sum(left[0] * right[0]) + jnp.sum(left[1] * right[1]) + jnp.sum(left[2] * right[2])

def least_squares(beta, columns):
    count = len(columns)
    cosines, sines, upper_cols = ([], [], [])
    target = [beta]
    for index, (proj, tail) in enumerate(columns):
        column = list(proj)
        for prior in range(index):
            top = cosines[prior] * column[prior] + sines[prior] * column[prior + 1]
            bottom = -sines[prior] * column[prior] + cosines[prior] * column[prior + 1]
            column[prior] = top
            column[prior + 1] = bottom
        radius = jnp.sqrt(column[index] * column[index] + tail * tail)
        cosine = column[index] / radius
        sine = tail / radius
        column[index] = radius
        cosines.append(cosine)
        sines.append(sine)
        target.append(-sine * target[index])
        target[index] = cosine * target[index]
        upper_cols.append(column)
    coeffs = [None] * count
    for row in reversed(range(count)):
        accum = target[row]
        for later in range(row + 1, count):
            accum = accum - upper_cols[later][row] * coeffs[later]
        coeffs[row] = accum / upper_cols[row][row]
    return coeffs

def reference(model_rhs, obs_rhs, model_var, obs_var, obs_weight, depth):
    rows_idx = jnp.arange(NLAT, dtype=jnp.float32)
    latitude = -jnp.pi / 2 + (rows_idx + BAND_START + 0.5) * (jnp.pi / GRID_ROWS)
    spin = (spin_rate * jnp.sin(latitude))[:, None]

    def propagate(state):
        for step in range(STEPS):
            state = model_step(state, depth, spin)
        return state

    def apply(vector):
        dual_model, dual_obs, increment = vector
        carried = propagate(increment)
        carried = jnp.concatenate([jnp.zeros_like(carried[:1]), carried[:-1]], axis=0)
        upcoming = jnp.concatenate([dual_model[1:], jnp.zeros_like(dual_model[:1])], axis=0)
        _, pullback = jax.vjp(propagate, jnp.zeros_like(upcoming))
        back = pullback(upcoming)[0]
        return (model_var * dual_model + increment - carried, obs_var * dual_obs + obs_weight * increment, dual_model - back + obs_weight * dual_obs)
    first = (model_rhs, obs_rhs, jnp.zeros_like(model_rhs))
    beta = jnp.sqrt(inner(first, first))
    basis = [tuple((part / beta for part in first))]
    columns = []
    for index in range(ITERS):
        image = apply(basis[index])
        proj = [inner(image, vec) for vec in basis]
        for factor, vec in zip(proj, basis):
            image = tuple((a - factor * b for a, b in zip(image, vec)))
        tail = jnp.sqrt(inner(image, image))
        columns.append((proj, tail))
        if index + 1 < ITERS:
            basis.append(tuple((part / tail for part in image)))
    coeffs = least_squares(beta, columns)
    result = [jnp.zeros_like(model_rhs) for part in range(3)]
    for factor, vec in zip(coeffs, basis):
        result = [acc + factor * part for acc, part in zip(result, vec)]
    return (result[0], result[1], result[2])
```

```python
import jax
import jax.numpy as jnp
from jax import lax
from jax.sharding import PartitionSpec as P

GRID_ROWS = 768
STEPS = 4
REACH = 2 * STEPS

mass_rate = 0.5
press_rate = 0.5
spin_rate = 0.4


def halo(block):
    count = lax.axis_size("lat")
    forward = [(i, i + 1) for i in range(count - 1)]
    backward = [(j, i) for i, j in forward]
    rows = block.shape[-2]
    low = lax.ppermute(block[..., rows - REACH:, :], "lat", forward)
    high = lax.ppermute(block[..., :REACH, :], "lat", backward)
    return jnp.concatenate([low, block, high], axis=-2)


def shifted(value, axis, steps):
    count = lax.axis_size(axis)
    initial, last = (max(0, -steps), min(count, count - steps))
    return lax.ppermute(value, axis, [(source, source + steps) for source in range(initial, last)])


def along_lon(field):
    return 0.5 * (jnp.roll(field, -1, axis=-1) - jnp.roll(field, 1, axis=-1))


def along_lat(field):
    padded = jnp.pad(field, [(0, 0)] * (field.ndim - 2) + [(1, 1), (0, 0)])
    return 0.5 * (padded[..., 2:, :] - padded[..., :-2, :])


def adjoint(adj_height, adj_east, adj_north, depth, spin, inside):
    for step in range(STEPS):
        adj_mid = adj_east - mass_rate * spin * adj_north
        adj_rest = inside * (adj_height + press_rate * (along_lat(adj_north) + along_lon(adj_mid)))
        adj_height = adj_rest
        adj_north = inside * (adj_north + mass_rate * spin * adj_mid + mass_rate * depth * along_lat(adj_rest))
        adj_east = adj_mid + mass_rate * depth * along_lon(adj_rest)
    return adj_height, adj_east, adj_north


def forward(height, east, north, depth, spin, inside):
    for step in range(STEPS):
        height = inside * (height - mass_rate * (along_lon(depth * east) + along_lat(depth * north)))
        east = east + mass_rate * spin * north - press_rate * along_lon(height)
        north = north - mass_rate * spin * east - press_rate * along_lat(height)
    return height, east, north


def total(value):
    return jnp.sum(value)


def body(model_rhs, obs_rhs, model_var, obs_var, obs_weight, depth):
    rows = model_rhs.shape[2]
    total_rows = rows * lax.axis_size("lat")
    offset = (GRID_ROWS - total_rows) // 2
    local_rows = lax.axis_index("lat") * rows - REACH + jnp.arange(rows + 2 * REACH, dtype=jnp.int32)
    latitude = -jnp.pi / 2 + (local_rows.astype(jnp.float32) + offset + 0.5) * (jnp.pi / GRID_ROWS)
    inside = ((local_rows >= 0) & (local_rows < total_rows)).astype(jnp.float32)[:, None]
    spin = inside * (spin_rate * jnp.sin(latitude))[:, None]
    p, m, dvar, rvar, hobs = model_rhs[0], obs_rhs[0], model_var[0], obs_var[0], obs_weight[0]
    axes = ("win", "lat")
    up = dvar * p
    um = rvar * m
    first = total(up * p) + total(um * m)
    wide_depth = halo(depth[0])
    pair = shifted(jnp.stack([p, up], axis=1), "win", -1)
    wide = halo(pair)
    back = adjoint(wide[0], wide[1], wide[2], wide_depth, spin, inside)
    back = jnp.stack(back)[:, :, REACH:REACH + rows]
    ux = p - back[:, 0] + hobs * m
    far = shifted(dvar * up + ux, "win", -1)
    wide = halo(ux)
    end = jnp.stack(forward(wide[0], wide[1], wide[2], wide_depth, spin, inside))[:, REACH:REACH + rows]
    zx = up - back[:, 1] + hobs * um
    zm = rvar * um + hobs * ux
    window = lax.axis_index("win")
    lead = jnp.where(window == 0, 1.0, 0.0)
    zp = far - jnp.where(window == lax.axis_size("win") - 1, 0.0, 1.0) * end
    own = dvar * up + ux
    uu = total(up * up) + total(um * um) + total(ux * ux)
    uz = total(dvar * up * up) + total(rvar * um * um) + 2.0 * total(zx * ux)
    zz = total(zp * zp) + lead * total(own * own) + total(zm * zm) + total(zx * zx)
    ranks = lax.axis_size("win") * lax.axis_size("lat")
    parts = jnp.stack([first, uu, uz, zz])
    sent = jnp.broadcast_to(jnp.pad(parts, (0, 124))[None], (ranks, 128))
    sums = jnp.sum(lax.all_to_all(sent, axes, 0, 0, tiled=True), axis=0)
    m1, m2, m3, m4 = sums[0], sums[1], sums[2], sums[3]
    tau, sigma, rho = m1 / m2, m3 / m2, m4 / m2
    gap = rho - sigma * sigma
    y1 = (tau * rho - sigma) / gap
    y2 = (1.0 - sigma * tau) / gap
    return ((y1 * p + y2 * up)[None], (y1 * m + y2 * um)[None], (y2 * ux)[None])


def solution(mesh):
    split = P("win", None, "lat", None)
    in_specs = (split,) * 5 + (P("win", "lat", None),)
    return jax.shard_map(body, mesh=mesh, in_specs=in_specs, out_specs=(split,) * 3, check_vma=False)
```

```python
import jax
import jax.numpy as jnp
from jax import lax
from jax.experimental import pallas as pl
from jax.experimental.pallas import tpu as pltpu
from jax.sharding import PartitionSpec as P

GRID_ROWS = 768
STEPS = 4

mass_rate = 0.5
press_rate = 0.5
spin_rate = 0.4


def lon_gap(field):
    width = field.shape[-1]
    return pltpu.roll(field, width - 1, 1) - pltpu.roll(field, 1, 1)


def lat_gap(field):
    rows = field.shape[0]
    return pltpu.roll(field, rows - 1, 0) - pltpu.roll(field, 1, 0)


def stacked(low, own, high, index):
    return jnp.concatenate([low[index], own[index], high[index]], axis=0)


def prep_kernel(p, m, dvar, hobs, depth, pair, straight):
    for part in range(3):
        pair[part] = p[0, part]
        pair[3 + part] = dvar[0, part] * p[0, part]
        straight[1 + part] = p[0, part] + hobs[0, part] * m[0, part]
    straight[0] = depth[0]


def adjoint_kernel(pair, pair_low, pair_high, straight, depth_low, depth_high, spin, inside, state, back):
    depth = 0.25 * jnp.concatenate([depth_low[0], straight[0], depth_high[0]], axis=0)
    turn, keep = spin[...], inside[...]
    rows = pair.shape[1]
    for which in range(2):
        base = 3 * which
        adj_height = stacked(pair_low, pair, pair_high, base)
        adj_east = stacked(pair_low, pair, pair_high, base + 1)
        adj_north = stacked(pair_low, pair, pair_high, base + 2)
        for step in range(STEPS):
            adj_mid = adj_east - turn * adj_north
            adj_height = keep * (adj_height + 0.25 * (lat_gap(adj_north) + lon_gap(adj_mid)))
            adj_north = adj_north + turn * adj_mid + depth * lat_gap(adj_height)
            adj_east = adj_mid + depth * lon_gap(adj_height)
        for part, value in enumerate((adj_height, adj_east, adj_north)):
            own = value[rows:2 * rows]
            back[base + part] = own
            if which == 0:
                state[part] = straight[1 + part] - own


def forward_kernel(state, state_low, state_high, straight, depth_low, depth_high, spin, inside, end):
    depth = 0.25 * jnp.concatenate([depth_low[0], straight[0], depth_high[0]], axis=0)
    turn, keep = spin[...], inside[...]
    rows = state.shape[1]
    height = stacked(state_low, state, state_high, 0)
    east = stacked(state_low, state, state_high, 1)
    north = stacked(state_low, state, state_high, 2)
    for step in range(STEPS):
        height = keep * (height - (lon_gap(depth * east) + lat_gap(depth * north)))
        east = east + turn * north - 0.25 * lon_gap(height)
        north = north - turn * east - 0.25 * lat_gap(height)
    for part, value in enumerate((height, east, north)):
        end[part] = value[rows:2 * rows]


def lane_sum(value):
    rows, width = value.shape
    total = value[:, :128]
    for start in range(128, width, 128):
        total = total + value[:, start:start + 128]
    return total


def inner_kernel(p, m, dvar, rvar, hobs, back, end, linked, sent):
    moments = [0.0, 0.0, 0.0, 0.0]
    link = linked[...]
    for part in range(3):
        dv, rv, hv = dvar[0, part], rvar[0, part], hobs[0, part]
        pv, mv = p[0, part], m[0, part]
        up, um = dv * pv, rv * mv
        ux = pv - back[part] + hv * mv
        zp = dv * up + ux - link * end[part]
        zm = rv * um + hv * ux
        zx = up - back[3 + part] + hv * um
        moments[0] += lane_sum(up * pv + um * mv)
        moments[1] += lane_sum(up * up + um * um + ux * ux)
        moments[2] += lane_sum(dv * up * up + rv * um * um + 2.0 * (zx * ux))
        moments[3] += lane_sum(zp * zp + zm * zm + zx * zx)
    rows = [jnp.sum(value, axis=0, keepdims=True) for value in moments]
    tile = jnp.concatenate(rows + rows, axis=0)
    for rank in range(sent.shape[0] // 8):
        sent[8 * rank:8 * rank + 8] = tile


def two_sum(a, b):
    total = a + b
    part = total - a
    return total, (a - (total - part)) + (b - part)


def split(a):
    wide = 4097.0 * a
    top = wide - (wide - a)
    return top, a - top


def two_product(a, b):
    product = a * b
    a_top, a_low = split(a)
    b_top, b_low = split(b)
    return product, ((a_top * b_top - product) + a_top * b_low + a_low * b_top) + a_low * b_low


def pair_product(a, b):
    product, rest = two_product(a[0], b[0])
    return product, rest + (a[0] * b[1] + a[1] * b[0])


def pair_gap(a, b):
    total, rest = two_sum(a[0], -b[0])
    return total + (rest + (a[1] - b[1]))


def coefficients(gathered):
    top = gathered[0:8]
    for rank in range(1, gathered.shape[0] // 8):
        top = top + gathered[8 * rank:8 * rank + 8]
    low = jnp.zeros_like(top)
    shift = 64
    while shift:
        total, rest = two_sum(top, pltpu.roll(top, shift, 1))
        low = low + pltpu.roll(low, shift, 1) + rest
        top = total
        shift //= 2
    scale = 1.0 / top[1:2, :128]
    moments = []
    for row in range(4):
        product, rest = two_product(top[row:row + 1], scale)
        moments.append((product, rest + low[row:row + 1] * scale))
    m1, m2, m3, m4 = moments
    gap = pair_gap(pair_product(m2, m4), pair_product(m3, m3))
    y1 = pair_gap(pair_product(m1, m4), pair_product(m2, m3)) / gap
    y2 = pair_gap(pair_product(m2, m2), pair_product(m1, m3)) / gap
    return y1, y2


def combine_kernel(gathered, p, m, dvar, rvar, hobs, back, dual_model, dual_obs, increment):
    y1, y2 = coefficients(gathered)
    rows, width = p.shape[2:]
    y1 = jnp.broadcast_to(jnp.concatenate([y1] * (width // 128), axis=1), (rows, width))
    y2 = jnp.broadcast_to(jnp.concatenate([y2] * (width // 128), axis=1), (rows, width))
    for part in range(3):
        pv, mv = p[0, part], m[0, part]
        dual_model[0, part] = (y1 + y2 * dvar[0, part]) * pv
        dual_obs[0, part] = (y1 + y2 * rvar[0, part]) * mv
        increment[0, part] = y2 * (pv - back[part] + hobs[0, part] * mv)


def run(kernel, out_shapes, *operands):
    shapes = [jax.ShapeDtypeStruct(shape, jnp.float32) for shape in out_shapes]
    size = sum(4 * operand.size for operand in operands) + sum(4 * shape.size for shape in shapes)
    return pl.pallas_call(
        kernel,
        out_shape=shapes,
        in_specs=[pl.BlockSpec(memory_space=pltpu.VMEM)] * len(operands),
        out_specs=[pl.BlockSpec(memory_space=pltpu.VMEM)] * len(shapes),
        compiler_params=pltpu.CompilerParams(vmem_limit_bytes=32 * 1024 * 1024),
        cost_estimate=pl.CostEstimate(flops=4 * size, bytes_accessed=size, transcendentals=0),
    )(*operands)


def moved(value, win_step, lat_step):
    wins, lats = lax.axis_size("win"), lax.axis_size("lat")
    pairs = []
    for win in range(wins):
        for lat in range(lats):
            if 0 <= win + win_step < wins and 0 <= lat + lat_step < lats:
                pairs.append((win * lats + lat, (win + win_step) * lats + lat + lat_step))
    return lax.ppermute(value, ("win", "lat"), pairs)


def body(model_rhs, obs_rhs, model_var, obs_var, obs_weight, depth):
    rows, width = model_rhs.shape[2:]
    ranks = lax.axis_size("win") * lax.axis_size("lat")
    total_rows = rows * lax.axis_size("lat")
    offset = (GRID_ROWS - total_rows) // 2
    local_rows = lax.axis_index("lat") * rows - rows + jnp.arange(3 * rows, dtype=jnp.int32)
    latitude = -jnp.pi / 2 + (local_rows.astype(jnp.float32) + offset + 0.5) * (jnp.pi / GRID_ROWS)
    inside = ((local_rows >= 0) & (local_rows < total_rows)).astype(jnp.float32)
    spin = inside * (mass_rate * spin_rate * jnp.sin(latitude))
    inside = jnp.broadcast_to(inside[:, None], (3 * rows, width))
    spin = jnp.broadcast_to(spin[:, None], (3 * rows, width))
    linked = jnp.full((rows, width), jnp.where(lax.axis_index("win") > 0, 1.0, 0.0))

    depth_low, depth_high = moved(depth, 1, 1), moved(depth, 1, -1)
    pair, straight = run(
        prep_kernel, [(6, rows, width), (4, rows, width)], model_rhs, obs_rhs, model_var, obs_weight, depth
    )
    pair_low, pair_high = moved(pair, 0, 1), moved(pair, 0, -1)
    came = moved(straight, 1, 0)
    state, back = run(
        adjoint_kernel, [(3, rows, width), (6, rows, width)],
        pair, pair_low, pair_high, came, depth_low, depth_high, spin, inside,
    )
    state_low, state_high = moved(state, 0, 1), moved(state, 0, -1)
    back = moved(back, -1, 0)
    (end,) = run(
        forward_kernel, [(3, rows, width)], state, state_low, state_high, came, depth_low, depth_high, spin, inside
    )
    (sent,) = run(
        inner_kernel, [(8 * ranks, 128)],
        model_rhs, obs_rhs, model_var, obs_var, obs_weight, back, end, linked,
    )
    gathered = lax.all_to_all(sent, ("win", "lat"), 0, 0, tiled=True)
    return run(
        combine_kernel, [model_rhs.shape] * 3,
        gathered, model_rhs, obs_rhs, model_var, obs_var, obs_weight, back,
    )


def solution(mesh):
    split_spec = P("win", None, "lat", None)
    in_specs = (split_spec,) * 5 + (P("win", "lat", None),)
    return jax.shard_map(body, mesh=mesh, in_specs=in_specs, out_specs=(split_spec,) * 3, check_vma=False)
```

```python
import jax
import jax.numpy as jnp
from jax import lax
from jax.experimental import pallas as pl
from jax.experimental.pallas import tpu as pltpu
from jax.sharding import PartitionSpec as P

GRID_ROWS = 768
STEPS = 4

mass_rate = 0.5
press_rate = 0.5
spin_rate = 0.4


def lon_gap(field):
    width = field.shape[-1]
    return pltpu.roll(field, width - 1, 1) - pltpu.roll(field, 1, 1)


def lat_gap(field):
    rows = field.shape[0]
    return pltpu.roll(field, rows - 1, 0) - pltpu.roll(field, 1, 0)


def even_lat():
    return lax.axis_index("lat") % 2 == 0


def has_previous():
    return lax.axis_index("win") > 0


def stacked(own, near, far, index):
    even = even_lat()
    low = jnp.where(even, far[index], near[index])
    high = jnp.where(even, near[index], far[index])
    return jnp.concatenate([low, own[index], high], axis=0)


def prep_kernel(p, m, dvar, rvar, hobs, depth, pair, straight, pv, mv, dv, rv, hv, sems):
    copies = [
        pltpu.make_async_copy(p, pv, sems.at[0]),
        pltpu.make_async_copy(dvar, dv, sems.at[1]),
        pltpu.make_async_copy(m, mv, sems.at[2]),
        pltpu.make_async_copy(hobs, hv, sems.at[3]),
        pltpu.make_async_copy(rvar, rv, sems.at[4]),
        pltpu.make_async_copy(depth, straight.at[0:1], sems.at[5]),
    ]
    for copy in copies:
        copy.start()
    for copy in copies:
        copy.wait()
    for part in range(3):
        up = dv[0, part] * pv[0, part]
        seen = hv[0, part] * mv[0, part]
        pair[part] = pv[0, part]
        pair[3 + part] = up
        straight[1 + part] = pv[0, part] + seen
        straight[4 + part] = up + rv[0, part] * seen


def adjoint(pair, pair_near, pair_far, straight, depth_near, depth_far, spin, inside, base):
    depth = 0.25 * stacked(straight, depth_near, depth_far, 0)
    turn, keep = spin[...], inside[...]
    adj_height, adj_east, adj_north = [stacked(pair, pair_near, pair_far, base + part) for part in range(3)]
    for step in range(STEPS):
        adj_mid = adj_east - turn * adj_north
        adj_height = keep * (adj_height + 0.25 * (lat_gap(adj_north) + lon_gap(adj_mid)))
        adj_north = adj_north + turn * adj_mid + depth * lat_gap(adj_height)
        adj_east = adj_mid + depth * lon_gap(adj_height)
    rows = pair.shape[1]
    return [value[rows:2 * rows] for value in (adj_height, adj_east, adj_north)]


def first_adjoint_kernel(pair, pair_near, pair_far, straight, depth_near, depth_far, spin, inside, state, back):
    swept = adjoint(pair, pair_near, pair_far, straight, depth_near, depth_far, spin, inside, 0)
    link = has_previous()
    for part, value in enumerate(swept):
        back[part] = value
        state[part] = jnp.where(link, straight[1 + part] - value, 0.0)


def second_adjoint_kernel(pair, pair_near, pair_far, straight, depth_near, depth_far, spin, inside, state, tally):
    swept = adjoint(pair, pair_near, pair_far, straight, depth_near, depth_far, spin, inside, 3)
    link = has_previous()
    cross = square = 0.0
    for part, value in enumerate(swept):
        zx = jnp.where(link, straight[4 + part] - value, 0.0)
        cross += lane_sum(zx * state[part])
        square += lane_sum(zx * zx)
    tally[0] = cross
    tally[1] = square


def forward_kernel(state, state_near, state_far, straight, depth_near, depth_far, spin, inside, end):
    depth = 0.25 * stacked(straight, depth_near, depth_far, 0)
    turn, keep = spin[...], inside[...]
    height, east, north = [stacked(state, state_near, state_far, part) for part in range(3)]
    for step in range(STEPS):
        height = keep * (height - (lon_gap(depth * east) + lat_gap(depth * north)))
        east = east + turn * north - 0.25 * lon_gap(height)
        north = north - turn * east - 0.25 * lat_gap(height)
    rows = state.shape[1]
    for part, value in enumerate((height, east, north)):
        end[part] = value[rows:2 * rows]


def lane_sum(value):
    rows, width = value.shape
    total = value[:, :128]
    for start in range(128, width, 128):
        total = total + value[:, start:start + 128]
    return total


def inner_kernel(p, m, dvar, rvar, hobs, back, end, tally, sent):
    last = lax.axis_index("win") == lax.axis_size("win") - 1
    moments = [0.0, 0.0, 2.0 * tally[0], tally[1]]
    for part in range(3):
        dv, rv, hv = dvar[0, part], rvar[0, part], hobs[0, part]
        pv, mv = p[0, part], m[0, part]
        up, um = dv * pv, rv * mv
        ux = pv - back[part] + hv * mv
        zp = dv * up + ux - end[part]
        zm = rv * um + hv * ux
        zx = jnp.where(last, up + hv * um, 0.0)
        moments[0] += lane_sum(up * pv + um * mv)
        moments[1] += lane_sum(up * up + um * um + ux * ux)
        moments[2] += lane_sum(dv * up * up + rv * um * um + 2.0 * (zx * ux))
        moments[3] += lane_sum(zp * zp + zm * zm + zx * zx)
    rows = [jnp.sum(value, axis=0, keepdims=True) for value in moments]
    tile = jnp.concatenate(rows + rows, axis=0)
    for rank in range(sent.shape[0] // 8):
        sent[8 * rank:8 * rank + 8] = tile


def two_sum(a, b):
    total = a + b
    part = total - a
    return total, (a - (total - part)) + (b - part)


def split(a):
    wide = 4097.0 * a
    top = wide - (wide - a)
    return top, a - top


def two_product(a, b):
    product = a * b
    a_top, a_low = split(a)
    b_top, b_low = split(b)
    return product, ((a_top * b_top - product) + a_top * b_low + a_low * b_top) + a_low * b_low


def pair_product(a, b):
    product, rest = two_product(a[0], b[0])
    return product, rest + (a[0] * b[1] + a[1] * b[0])


def pair_gap(a, b):
    total, rest = two_sum(a[0], -b[0])
    return total + (rest + (a[1] - b[1]))


def coefficients(gathered):
    top = gathered[0:8]
    for rank in range(1, gathered.shape[0] // 8):
        top = top + gathered[8 * rank:8 * rank + 8]
    low = jnp.zeros_like(top)
    shift = 64
    while shift:
        total, rest = two_sum(top, pltpu.roll(top, shift, 1))
        low = low + pltpu.roll(low, shift, 1) + rest
        top = total
        shift //= 2
    scale = 1.0 / top[1:2, :128]
    moments = []
    for row in range(4):
        product, rest = two_product(top[row:row + 1], scale)
        moments.append((product, rest + low[row:row + 1] * scale))
    m1, m2, m3, m4 = moments
    gap = pair_gap(pair_product(m2, m4), pair_product(m3, m3))
    y1 = pair_gap(pair_product(m1, m4), pair_product(m2, m3)) / gap
    y2 = pair_gap(pair_product(m2, m2), pair_product(m1, m3)) / gap
    return y1, y2


def combine_kernel(gathered, p, m, dvar, rvar, hobs, back, dual_model, dual_obs, increment):
    y1, y2 = coefficients(gathered)
    rows, width = p.shape[2:]
    y1 = jnp.broadcast_to(jnp.concatenate([y1] * (width // 128), axis=1), (rows, width))
    y2 = jnp.broadcast_to(jnp.concatenate([y2] * (width // 128), axis=1), (rows, width))
    for part in range(3):
        pv, mv = p[0, part], m[0, part]
        dual_model[0, part] = (y1 + y2 * dvar[0, part]) * pv
        dual_obs[0, part] = (y1 + y2 * rvar[0, part]) * mv
        increment[0, part] = y2 * (pv - back[part] + hobs[0, part] * mv)


def run(kernel, out_shapes, *operands, scratch=(), space=pltpu.VMEM, limit=32):
    shapes = [jax.ShapeDtypeStruct(shape, jnp.float32) for shape in out_shapes]
    size = sum(4 * operand.size for operand in operands) + sum(4 * shape.size for shape in shapes)
    return pl.pallas_call(
        kernel,
        out_shape=shapes,
        in_specs=[pl.BlockSpec(memory_space=space)] * len(operands),
        out_specs=[pl.BlockSpec(memory_space=pltpu.VMEM)] * len(shapes),
        scratch_shapes=scratch,
        compiler_params=pltpu.CompilerParams(vmem_limit_bytes=limit * 1024 * 1024),
        cost_estimate=pl.CostEstimate(flops=4 * size, bytes_accessed=size, transcendentals=0),
    )(*operands)


def shifted(value, step):
    count = lax.axis_size("win")
    initial, last = (max(0, -step), min(count, count - step))
    return lax.ppermute(value, "win", [(source, source + step) for source in range(initial, last)])


def swapped(value, first, win_step=0):
    wins, lats = lax.axis_size("win"), lax.axis_size("lat")
    pairs = []
    for win in range(wins - win_step):
        for lat in range(first, lats - 1, 2):
            for source, target in ((lat, lat + 1), (lat + 1, lat)):
                pairs.append((win * lats + source, (win + win_step) * lats + target))
    return lax.ppermute(value, ("win", "lat"), pairs)


def body(model_rhs, obs_rhs, model_var, obs_var, obs_weight, depth):
    rows, width = model_rhs.shape[2:]
    ranks = lax.axis_size("win") * lax.axis_size("lat")
    total_rows = rows * lax.axis_size("lat")
    offset = (GRID_ROWS - total_rows) // 2
    local_rows = lax.axis_index("lat") * rows - rows + jnp.arange(3 * rows, dtype=jnp.int32)
    latitude = -jnp.pi / 2 + (local_rows.astype(jnp.float32) + offset + 0.5) * (jnp.pi / GRID_ROWS)
    inside = ((local_rows >= 0) & (local_rows < total_rows)).astype(jnp.float32)
    spin = inside * (mass_rate * spin_rate * jnp.sin(latitude))
    inside = jnp.broadcast_to(inside[:, None], (3 * rows, width))
    spin = jnp.broadcast_to(spin[:, None], (3 * rows, width))
    fields = (3, rows, width)

    depth_near, depth_far = swapped(depth, 0, 1), swapped(depth, 1, 1)
    pair, straight = run(
        prep_kernel, [(6, rows, width), (7, rows, width)],
        model_rhs, obs_rhs, model_var, obs_var, obs_weight, depth,
        scratch=[pltpu.VMEM(model_rhs.shape, jnp.float32)] * 5 + [pltpu.SemaphoreType.DMA((6,))],
        space=pltpu.HBM, limit=60,
    )
    came = shifted(straight, 1)
    pair_near, pair_far = swapped(pair, 0), swapped(pair, 1)
    known = (pair, pair_near, pair_far, came, depth_near, depth_far, spin, inside)
    state, back = run(first_adjoint_kernel, [fields, fields], *known)
    back = shifted(back, -1)
    state_near, state_far = swapped(state, 0), swapped(state, 1)
    (tally,) = run(second_adjoint_kernel, [(2, rows, 128)], *known, state)
    (end,) = run(forward_kernel, [fields], state, state_near, state_far, came, depth_near, depth_far, spin, inside)
    (sent,) = run(
        inner_kernel, [(8 * ranks, 128)],
        model_rhs, obs_rhs, model_var, obs_var, obs_weight, back, end, tally,
    )
    gathered = lax.all_to_all(sent, ("win", "lat"), 0, 0, tiled=True)
    return run(
        combine_kernel, [model_rhs.shape] * 3,
        gathered, model_rhs, obs_rhs, model_var, obs_var, obs_weight, back,
    )


def solution(mesh):
    split_spec = P("win", None, "lat", None)
    in_specs = (split_spec,) * 5 + (P("win", "lat", None),)
    return jax.shard_map(body, mesh=mesh, in_specs=in_specs, out_specs=(split_spec,) * 3, check_vma=False)
```

```python
import jax
import jax.numpy as jnp
from jax import lax
from jax.experimental import pallas as pl
from jax.experimental.pallas import tpu as pltpu
from jax.sharding import PartitionSpec as P

GRID_ROWS = 768
STEPS = 4

mass_rate = 0.5
press_rate = 0.5
spin_rate = 0.4


def lon_gap(field):
    width = field.shape[-1]
    return pltpu.roll(field, width - 1, 1) - pltpu.roll(field, 1, 1)


def lat_gap(field):
    rows = field.shape[0]
    return pltpu.roll(field, rows - 1, 0) - pltpu.roll(field, 1, 0)


def even_lat():
    return lax.axis_index("lat") % 2 == 0


def has_previous():
    return lax.axis_index("win") > 0


def stacked(own, near, far, index):
    even = even_lat()
    low = jnp.where(even, far[index], near[index])
    high = jnp.where(even, near[index], far[index])
    return jnp.concatenate([low, own[index], high], axis=0)


def prep_kernel(p, m, dvar, rvar, hobs, depth, pair, straight, pv, mv, dv, rv, hv, sems):
    copies = [
        pltpu.make_async_copy(p, pv, sems.at[0]),
        pltpu.make_async_copy(dvar, dv, sems.at[1]),
        pltpu.make_async_copy(m, mv, sems.at[2]),
        pltpu.make_async_copy(hobs, hv, sems.at[3]),
        pltpu.make_async_copy(rvar, rv, sems.at[4]),
        pltpu.make_async_copy(depth, straight.at[0:1], sems.at[5]),
    ]
    for copy in copies:
        copy.start()
    for copy in copies:
        copy.wait()
    for part in range(3):
        up = dv[0, part] * pv[0, part]
        seen = hv[0, part] * mv[0, part]
        pair[part] = pv[0, part]
        pair[3 + part] = up
        straight[1 + part] = pv[0, part] + seen
        straight[4 + part] = up + rv[0, part] * seen


def adjoint(pair, pair_near, pair_far, straight, depth_near, depth_far, spin, inside, base):
    depth = 0.25 * stacked(straight, depth_near, depth_far, 0)
    turn, keep = spin[...], inside[...]
    adj_height, adj_east, adj_north = [stacked(pair, pair_near, pair_far, base + part) for part in range(3)]
    for step in range(STEPS):
        adj_mid = adj_east - turn * adj_north
        adj_height = keep * (adj_height + 0.25 * (lat_gap(adj_north) + lon_gap(adj_mid)))
        adj_north = adj_north + turn * adj_mid + depth * lat_gap(adj_height)
        adj_east = adj_mid + depth * lon_gap(adj_height)
    rows = pair.shape[1]
    return [value[rows:2 * rows] for value in (adj_height, adj_east, adj_north)]


def first_adjoint_kernel(pair, pair_near, pair_far, straight, depth_near, depth_far, spin, inside, state, back):
    swept = adjoint(pair, pair_near, pair_far, straight, depth_near, depth_far, spin, inside, 0)
    link = has_previous()
    for part, value in enumerate(swept):
        back[part] = value
        state[part] = jnp.where(link, straight[1 + part] - value, 0.0)


def second_adjoint_kernel(pair, pair_near, pair_far, straight, depth_near, depth_far, spin, inside, state, tally):
    swept = adjoint(pair, pair_near, pair_far, straight, depth_near, depth_far, spin, inside, 3)
    link = has_previous()
    cross = square = 0.0
    for part, value in enumerate(swept):
        zx = jnp.where(link, straight[4 + part] - value, 0.0)
        cross += lane_sum(zx * state[part])
        square += lane_sum(zx * zx)
    tally[0] = cross
    tally[1] = square


def forward_kernel(state, state_near, state_far, straight, depth_near, depth_far, spin, inside, end):
    depth = 0.25 * stacked(straight, depth_near, depth_far, 0)
    turn, keep = spin[...], inside[...]
    height, east, north = [stacked(state, state_near, state_far, part) for part in range(3)]
    for step in range(STEPS):
        height = keep * (height - (lon_gap(depth * east) + lat_gap(depth * north)))
        east = east + turn * north - 0.25 * lon_gap(height)
        north = north - turn * east - 0.25 * lat_gap(height)
    rows = state.shape[1]
    for part, value in enumerate((height, east, north)):
        end[part] = value[rows:2 * rows]


def lane_sum(value):
    rows, width = value.shape
    total = value[:, :128]
    for start in range(128, width, 128):
        total = total + value[:, start:start + 128]
    return total


def inner_kernel(p, m, dvar, rvar, hobs, back, end, tally, sent):
    last = lax.axis_index("win") == lax.axis_size("win") - 1
    moments = [0.0, 0.0, 2.0 * tally[0], tally[1]]
    for part in range(3):
        dv, rv, hv = dvar[0, part], rvar[0, part], hobs[0, part]
        pv, mv = p[0, part], m[0, part]
        up, um = dv * pv, rv * mv
        ux = pv - back[part] + hv * mv
        zp = dv * up + ux - end[part]
        zm = rv * um + hv * ux
        zx = jnp.where(last, up + hv * um, 0.0)
        moments[0] += lane_sum(up * pv + um * mv)
        moments[1] += lane_sum(up * up + um * um + ux * ux)
        moments[2] += lane_sum(dv * up * up + rv * um * um + 2.0 * (zx * ux))
        moments[3] += lane_sum(zp * zp + zm * zm + zx * zx)
    rows = [jnp.sum(value, axis=0, keepdims=True) for value in moments]
    tile = jnp.concatenate(rows + rows, axis=0)
    sent[...] = tile


def two_sum(a, b):
    total = a + b
    part = total - a
    return total, (a - (total - part)) + (b - part)


def split(a):
    wide = 4097.0 * a
    top = wide - (wide - a)
    return top, a - top


def two_product(a, b):
    product = a * b
    a_top, a_low = split(a)
    b_top, b_low = split(b)
    return product, ((a_top * b_top - product) + a_top * b_low + a_low * b_top) + a_low * b_low


def pair_product(a, b):
    product, rest = two_product(a[0], b[0])
    return product, rest + (a[0] * b[1] + a[1] * b[0])


def pair_gap(a, b):
    total, rest = two_sum(a[0], -b[0])
    return total + (rest + (a[1] - b[1]))


def coefficients(gathered):
    top = gathered[0:8]
    for rank in range(1, gathered.shape[0] // 8):
        top = top + gathered[8 * rank:8 * rank + 8]
    low = jnp.zeros_like(top)
    shift = 64
    while shift:
        total, rest = two_sum(top, pltpu.roll(top, shift, 1))
        low = low + pltpu.roll(low, shift, 1) + rest
        top = total
        shift //= 2
    scale = 1.0 / top[1:2, :128]
    moments = []
    for row in range(4):
        product, rest = two_product(top[row:row + 1], scale)
        moments.append((product, rest + low[row:row + 1] * scale))
    m1, m2, m3, m4 = moments
    gap = pair_gap(pair_product(m2, m4), pair_product(m3, m3))
    y1 = pair_gap(pair_product(m1, m4), pair_product(m2, m3)) / gap
    y2 = pair_gap(pair_product(m2, m2), pair_product(m1, m3)) / gap
    return y1, y2


def combine_kernel(gathered, p, m, dvar, rvar, hobs, back, dual_model, dual_obs, increment):
    y1, y2 = coefficients(gathered)
    rows, width = p.shape[2:]
    y1 = jnp.broadcast_to(jnp.concatenate([y1] * (width // 128), axis=1), (rows, width))
    y2 = jnp.broadcast_to(jnp.concatenate([y2] * (width // 128), axis=1), (rows, width))
    for part in range(3):
        pv, mv = p[0, part], m[0, part]
        dual_model[0, part] = (y1 + y2 * dvar[0, part]) * pv
        dual_obs[0, part] = (y1 + y2 * rvar[0, part]) * mv
        increment[0, part] = y2 * (pv - back[part] + hobs[0, part] * mv)


def run(kernel, out_shapes, *operands, scratch=(), space=pltpu.VMEM, limit=32):
    shapes = [jax.ShapeDtypeStruct(shape, jnp.float32) for shape in out_shapes]
    size = sum(4 * operand.size for operand in operands) + sum(4 * shape.size for shape in shapes)
    return pl.pallas_call(
        kernel,
        out_shape=shapes,
        in_specs=[pl.BlockSpec(memory_space=space)] * len(operands),
        out_specs=[pl.BlockSpec(memory_space=pltpu.VMEM)] * len(shapes),
        scratch_shapes=scratch,
        compiler_params=pltpu.CompilerParams(vmem_limit_bytes=limit * 1024 * 1024),
        cost_estimate=pl.CostEstimate(flops=4 * size, bytes_accessed=size, transcendentals=0),
    )(*operands)


def shifted(value, step):
    count = lax.axis_size("win")
    initial, last = (max(0, -step), min(count, count - step))
    return lax.ppermute(value, "win", [(source, source + step) for source in range(initial, last)])


def swapped(value, first, win_step=0):
    wins, lats = lax.axis_size("win"), lax.axis_size("lat")
    pairs = []
    for win in range(wins - win_step):
        for lat in range(first, lats - 1, 2):
            for source, target in ((lat, lat + 1), (lat + 1, lat)):
                pairs.append((win * lats + source, (win + win_step) * lats + target))
    return lax.ppermute(value, ("win", "lat"), pairs)


def body(model_rhs, obs_rhs, model_var, obs_var, obs_weight, depth):
    rows, width = model_rhs.shape[2:]
    total_rows = rows * lax.axis_size("lat")
    offset = (GRID_ROWS - total_rows) // 2
    local_rows = lax.axis_index("lat") * rows - rows + jnp.arange(3 * rows, dtype=jnp.int32)
    latitude = -jnp.pi / 2 + (local_rows.astype(jnp.float32) + offset + 0.5) * (jnp.pi / GRID_ROWS)
    inside = ((local_rows >= 0) & (local_rows < total_rows)).astype(jnp.float32)
    spin = inside * (mass_rate * spin_rate * jnp.sin(latitude))
    inside = jnp.broadcast_to(inside[:, None], (3 * rows, width))
    spin = jnp.broadcast_to(spin[:, None], (3 * rows, width))
    fields = (3, rows, width)

    depth_near, depth_far = swapped(depth, 0, 1), swapped(depth, 1, 1)
    pair, straight = run(
        prep_kernel, [(6, rows, width), (7, rows, width)],
        model_rhs, obs_rhs, model_var, obs_var, obs_weight, depth,
        scratch=[pltpu.VMEM(model_rhs.shape, jnp.float32)] * 5 + [pltpu.SemaphoreType.DMA((6,))],
        space=pltpu.HBM, limit=60,
    )
    came = shifted(straight, 1)
    pair_near, pair_far = swapped(pair, 0), swapped(pair, 1)
    known = (pair, pair_near, pair_far, came, depth_near, depth_far, spin, inside)
    state, back = run(first_adjoint_kernel, [fields, fields], *known)
    back = shifted(back, -1)
    state_near, state_far = swapped(state, 0), swapped(state, 1)
    (tally,) = run(second_adjoint_kernel, [(2, rows, 128)], *known, state)
    (end,) = run(forward_kernel, [fields], state, state_near, state_far, came, depth_near, depth_far, spin, inside)
    (sent,) = run(
        inner_kernel, [(8, 128)],
        model_rhs, obs_rhs, model_var, obs_var, obs_weight, back, end, tally,
    )
    gathered = lax.all_gather(sent, ("win", "lat"), axis=0, tiled=True)
    return run(
        combine_kernel, [model_rhs.shape] * 3,
        gathered, model_rhs, obs_rhs, model_var, obs_var, obs_weight, back,
    )


def solution(mesh):
    split_spec = P("win", None, "lat", None)
    in_specs = (split_spec,) * 5 + (P("win", "lat", None),)
    return jax.shard_map(body, mesh=mesh, in_specs=in_specs, out_specs=(split_spec,) * 3, check_vma=False)
```

```python
import jax
import jax.numpy as jnp
from jax import lax
from jax.experimental import pallas as pl
from jax.experimental.pallas import tpu as pltpu
from jax.sharding import Mesh, PartitionSpec as P

GRID_ROWS = 768
STEPS = 4

mass_rate = 0.5
press_rate = 0.5
spin_rate = 0.4


def lon_gap(field):
    width = field.shape[-1]
    return pltpu.roll(field, width - 1, 1) - pltpu.roll(field, 1, 1)


def lat_gap(field):
    rows = field.shape[0]
    return pltpu.roll(field, rows - 1, 0) - pltpu.roll(field, 1, 0)


def even_lat():
    return lax.axis_index("half") == 0


def stacked(own, near, far, index):
    even = even_lat()
    low = jnp.where(even, far[index], near[index])
    high = jnp.where(even, near[index], far[index])
    return jnp.concatenate([low, own[index], high], axis=0)


def scale_kernel(p, dvar, scaled, pv, dv, sems):
    copies = [pltpu.make_async_copy(p, pv, sems.at[0]), pltpu.make_async_copy(dvar, dv, sems.at[1])]
    for copy in copies:
        copy.start()
    for copy in copies:
        copy.wait()
    for part in range(3):
        scaled[0, part] = dv[0, part] * pv[0, part]


def adjoint(own, near, far, depth, turn, keep):
    adj_height, adj_east, adj_north = [
        stacked(own.at[0], near.at[0], far.at[0], part) for part in range(3)
    ]
    for step in range(STEPS):
        adj_mid = adj_east - turn * adj_north
        adj_height = keep * (adj_height + 0.25 * (lat_gap(adj_north) + lon_gap(adj_mid)))
        adj_north = adj_north + turn * adj_mid + depth * lat_gap(adj_height)
        adj_east = adj_mid + depth * lon_gap(adj_height)
    rows = own.shape[2]
    return [value[rows:2 * rows] for value in (adj_height, adj_east, adj_north)]


def first_adjoint_kernel(own, near, far, depth, depth_near, depth_far, spin, inside, p, m, dvar, hobs, state, lead):
    quarter = 0.25 * stacked(depth, depth_near, depth_far, 0)
    swept = adjoint(own, near, far, quarter, spin[...], inside[...])
    for part, value in enumerate(swept):
        pv, dv = p[0, part], dvar[0, part]
        ux = pv - value + hobs[0, part] * m[0, part]
        state[0, part] = ux
        lead[0, part] = dv * (dv * pv) + ux


def second_adjoint_kernel(
    own, near, far, depth, depth_near, depth_far, spin, inside, p, m, dvar, rvar, hobs, state, lead, tally
):
    quarter = 0.25 * stacked(depth, depth_near, depth_far, 0)
    swept = adjoint(own, near, far, quarter, spin[...], inside[...])
    first = lax.axis_index("win") == 0
    moments = [0.0, 0.0, 0.0, 0.0]
    for part, value in enumerate(swept):
        dv, rv, hv = dvar[0, part], rvar[0, part], hobs[0, part]
        pv, mv, ux = p[0, part], m[0, part], state[0, part]
        up, um = dv * pv, rv * mv
        zp = jnp.where(first, lead[0, part], 0.0)
        zm = rv * um + hv * ux
        zx = up - value + hv * um
        moments[0] += lane_sum(up * pv + um * mv)
        moments[1] += lane_sum(up * up + um * um + ux * ux)
        moments[2] += lane_sum(dv * up * up + rv * um * um + 2.0 * (zx * ux))
        moments[3] += lane_sum(zp * zp + zm * zm + zx * zx)
    for row, value in enumerate(moments):
        tally[row] = value


def forward_kernel(state, near, far, depth, depth_near, depth_far, spin, inside, tally, end):
    quarter = 0.25 * stacked(depth, depth_near, depth_far, 0)
    turn, keep = spin[...], inside[...]
    height, east, north = [stacked(state.at[0], near.at[0], far.at[0], part) for part in range(3)]
    for step in range(STEPS):
        height = keep * (height - (lon_gap(quarter * east) + lat_gap(quarter * north)))
        east = east + turn * north - 0.25 * lon_gap(height)
        north = north - turn * east - 0.25 * lat_gap(height)
    rows = state.shape[2]
    for part, value in enumerate((height, east, north)):
        end[0, part] = value[rows:2 * rows]


def lane_sum(value):
    rows, width = value.shape
    total = value[:, :128]
    for start in range(128, width, 128):
        total = total + value[:, start:start + 128]
    return total


def inner_kernel(lead, end, tally, tile):
    last = lax.axis_index("win") == lax.axis_size("win") - 1
    square = 0.0
    for part in range(3):
        zp = lead[0, part] - end[0, part]
        square += lane_sum(zp * zp)
    moments = [tally[0], tally[1], tally[2], tally[3] + jnp.where(last, 0.0, square)]
    rows = [jnp.sum(value, axis=0, keepdims=True) for value in moments]
    tile[...] = jnp.concatenate(rows + rows, axis=0)


def spread_kernel(own, other, sent):
    tile = own[...] + other[...]
    for rank in range(sent.shape[0] // 8):
        sent[8 * rank:8 * rank + 8] = tile


def two_sum(a, b):
    total = a + b
    part = total - a
    return total, (a - (total - part)) + (b - part)


def split(a):
    wide = 4097.0 * a
    top = wide - (wide - a)
    return top, a - top


def two_product(a, b):
    product = a * b
    a_top, a_low = split(a)
    b_top, b_low = split(b)
    return product, ((a_top * b_top - product) + a_top * b_low + a_low * b_top) + a_low * b_low


def pair_product(a, b):
    product, rest = two_product(a[0], b[0])
    return product, rest + (a[0] * b[1] + a[1] * b[0])


def pair_gap(a, b):
    total, rest = two_sum(a[0], -b[0])
    return total + (rest + (a[1] - b[1]))


def coefficients(gathered):
    top = gathered[0:8]
    for rank in range(1, gathered.shape[0] // 8):
        top = top + gathered[8 * rank:8 * rank + 8]
    low = jnp.zeros_like(top)
    shift = 64
    while shift:
        total, rest = two_sum(top, pltpu.roll(top, shift, 1))
        low = low + pltpu.roll(low, shift, 1) + rest
        top = total
        shift //= 2
    scale = 1.0 / top[1:2, :128]
    moments = []
    for row in range(4):
        product, rest = two_product(top[row:row + 1], scale)
        moments.append((product, rest + low[row:row + 1] * scale))
    m1, m2, m3, m4 = moments
    gap = pair_gap(pair_product(m2, m4), pair_product(m3, m3))
    y1 = pair_gap(pair_product(m1, m4), pair_product(m2, m3)) / gap
    y2 = pair_gap(pair_product(m2, m2), pair_product(m1, m3)) / gap
    return y1, y2


def combine_kernel(gathered, p, m, dvar, rvar, state, dual_model, dual_obs, increment):
    y1, y2 = coefficients(gathered)
    rows, width = p.shape[2:]
    y1 = jnp.broadcast_to(jnp.concatenate([y1] * (width // 128), axis=1), (rows, width))
    y2 = jnp.broadcast_to(jnp.concatenate([y2] * (width // 128), axis=1), (rows, width))
    for part in range(3):
        dual_model[0, part] = (y1 + y2 * dvar[0, part]) * p[0, part]
        dual_obs[0, part] = (y1 + y2 * rvar[0, part]) * m[0, part]
        increment[0, part] = y2 * state[0, part]


def run(kernel, out_shapes, *operands, scratch=(), space=pltpu.VMEM, work=4):
    shapes = [jax.ShapeDtypeStruct(shape, jnp.float32) for shape in out_shapes]
    size = sum(4 * operand.size for operand in operands) + sum(4 * shape.size for shape in shapes)
    if space is not pltpu.VMEM:
        operands = [pltpu.with_memory_space_constraint(operand, space) for operand in operands]
    return pl.pallas_call(
        kernel,
        out_shape=shapes,
        in_specs=[pl.BlockSpec(memory_space=space)] * len(operands),
        out_specs=[pl.BlockSpec(memory_space=pltpu.VMEM)] * len(shapes),
        scratch_shapes=scratch,
        compiler_params=pltpu.CompilerParams(vmem_limit_bytes=32 * 1024 * 1024),
        cost_estimate=pl.CostEstimate(flops=work * size, bytes_accessed=size, transcendentals=0),
    )(*operands)


def shifted(value, step):
    count = lax.axis_size("win")
    initial, last = (max(0, -step), min(count, count - step))
    return lax.ppermute(value, "win", [(source, source + step) for source in range(initial, last)])


def lat_count():
    return lax.axis_size("band") * lax.axis_size("half")


def lat_index():
    return lax.axis_index("band") * lax.axis_size("half") + lax.axis_index("half")


def swapped(value, first, win_step=0):
    wins, lats = lax.axis_size("win"), lat_count()
    pairs = []
    for win in range(max(0, -win_step), min(wins, wins - win_step)):
        for lat in range(first, lats - 1, 2):
            for source, target in ((lat, lat + 1), (lat + 1, lat)):
                pairs.append((win * lats + source, (win + win_step) * lats + target))
    return lax.ppermute(value, ("win", "band", "half"), pairs)


def body(model_rhs, obs_rhs, model_var, obs_var, obs_weight, depth):
    rows, width = model_rhs.shape[2:]
    ranks = lax.axis_size("win") * lax.axis_size("band")
    total_rows = rows * lat_count()
    offset = (GRID_ROWS - total_rows) // 2
    local_rows = lat_index() * rows - rows + jnp.arange(3 * rows, dtype=jnp.int32)
    latitude = -jnp.pi / 2 + (local_rows.astype(jnp.float32) + offset + 0.5) * (jnp.pi / GRID_ROWS)
    inside = ((local_rows >= 0) & (local_rows < total_rows)).astype(jnp.float32)
    spin = inside * (mass_rate * spin_rate * jnp.sin(latitude))
    inside = jnp.broadcast_to(inside[:, None], (3 * rows, width))
    spin = jnp.broadcast_to(spin[:, None], (3 * rows, width))
    field = model_rhs.shape
    came = shifted(model_rhs, -1)
    came_far = swapped(model_rhs, 1, -1)
    place = (depth, swapped(depth, 0), swapped(depth, 1), spin, inside)
    (scaled,) = run(
        scale_kernel, [field], model_rhs, model_var, space=pltpu.HBM,
        scratch=[pltpu.VMEM(field, jnp.float32)] * 2 + [pltpu.SemaphoreType.DMA((2,))],
    )
    scaled_came = shifted(scaled, -1)
    scaled_far = swapped(scaled, 1, -1)
    state, lead = run(
        first_adjoint_kernel, [field, field],
        came, swapped(came, 0), came_far, *place, model_rhs, obs_rhs, model_var, obs_weight,
    )
    near, far = swapped(state, 0), swapped(state, 1)
    lead_came = shifted(lead, -1)
    held, _ = lax.optimization_barrier((scaled_came, state))
    (tally,) = run(
        second_adjoint_kernel, [(4, rows, 128)],
        scaled_came, swapped(held, 0), scaled_far, *place,
        model_rhs, obs_rhs, model_var, obs_var, obs_weight, state, lead,
    )
    (end,) = run(forward_kernel, [field], state, near, far, *place, tally)
    (tile,) = run(inner_kernel, [(8, 128)], lead_came, end, tally)
    (sent,) = run(spread_kernel, [(8 * ranks, 128)], tile, swapped(tile, 0))
    gathered = lax.all_to_all(sent, ("win", "band"), 0, 0, tiled=True)
    return run(combine_kernel, [field] * 3, gathered, model_rhs, obs_rhs, model_var, obs_var, state)


def solution(mesh):
    wins, lats = mesh.devices.shape
    mesh = Mesh(mesh.devices.reshape(wins, lats // 2, 2), ("win", "band", "half"))
    lat = ("band", "half")
    field = P("win", None, lat, None)
    in_specs = (field,) * 5 + (P("win", lat, None),)
    return jax.shard_map(body, mesh=mesh, in_specs=in_specs, out_specs=(field,) * 3, check_vma=False)
```

```python
import jax
import jax.numpy as jnp
from jax import lax
from jax.experimental import pallas as pl
from jax.experimental.pallas import tpu as pltpu
from jax.sharding import Mesh, PartitionSpec as P

GRID_ROWS = 768
STEPS = 4

mass_rate = 0.5
press_rate = 0.5
spin_rate = 0.4


def lon_gap(field):
    width = field.shape[-1]
    return pltpu.roll(field, width - 1, 1) - pltpu.roll(field, 1, 1)


def lat_gap(field):
    rows = field.shape[0]
    return pltpu.roll(field, rows - 1, 0) - pltpu.roll(field, 1, 0)


def is_middle():
    return lax.axis_index("band") != lax.axis_index("half")


def stacked(own, near, far, index):
    even = lax.axis_index("half") == 0
    outer = jnp.where(is_middle(), far[index], 0.0)
    low = jnp.where(even, outer, near[index])
    high = jnp.where(even, near[index], outer)
    return jnp.concatenate([low, own[index], high], axis=0)


def stretched(depth, depth_near, depth_far):
    return 0.25 * stacked(depth, depth_near, depth_far, 0)


def adjoint(own, near, far, far_start, depth, turn, keep):
    outer = far.at[0, far_start:far_start + 3]
    adj_height, adj_east, adj_north = [stacked(own.at[0], near.at[0], outer, part) for part in range(3)]
    for step in range(STEPS):
        adj_mid = adj_east - turn * adj_north
        adj_height = keep * (adj_height + 0.25 * (lat_gap(adj_north) + lon_gap(adj_mid)))
        adj_north = adj_north + turn * adj_mid + depth * lat_gap(adj_height)
        adj_east = adj_mid + depth * lon_gap(adj_height)
    rows = own.shape[2]
    return [value[rows:2 * rows] for value in (adj_height, adj_east, adj_north)]


def first_adjoint_kernel(own, near, far, depth, depth_near, depth_far, spin, inside, p, m, dvar, hobs, state, lead):
    swept = adjoint(own, near, far, 0, stretched(depth, depth_near, depth_far), spin[...], inside[...])
    for part, value in enumerate(swept):
        pv, dv = p[0, part], dvar[0, part]
        ux = pv - value + hobs[0, part] * m[0, part]
        state[0, part] = ux
        lead[0, part] = dv * (dv * pv) + ux


def second_adjoint_kernel(
    own, near, far, depth, depth_near, depth_far, spin, inside, p, m, dvar, rvar, hobs, state, lead, tally
):
    swept = adjoint(own, near, far, 3, stretched(depth, depth_near, depth_far), spin[...], inside[...])
    first = lax.axis_index("win") == 0
    moments = [0.0, 0.0, 0.0, 0.0]
    for part, value in enumerate(swept):
        dv, rv, hv = dvar[0, part], rvar[0, part], hobs[0, part]
        pv, mv, ux = p[0, part], m[0, part], state[0, part]
        up, um = dv * pv, rv * mv
        zp = jnp.where(first, lead[0, part], 0.0)
        zm = rv * um + hv * ux
        zx = up - value + hv * um
        moments[0] += lane_sum(up * pv + um * mv)
        moments[1] += lane_sum(up * up + um * um + ux * ux)
        moments[2] += lane_sum(dv * up * up + rv * um * um + 2.0 * (zx * ux))
        moments[3] += lane_sum(zp * zp + zm * zm + zx * zx)
    for row, value in enumerate(moments):
        tally[row] = value


def forward_kernel(state, near, far, depth, depth_near, depth_far, spin, inside, lead, tally, sent):
    quarter = stretched(depth, depth_near, depth_far)
    turn, keep = spin[...], inside[...]
    height, east, north = [stacked(state.at[0], near.at[0], far.at[0], part) for part in range(3)]
    for step in range(STEPS):
        height = keep * (height - (lon_gap(quarter * east) + lat_gap(quarter * north)))
        east = east + turn * north - 0.25 * lon_gap(height)
        north = north - turn * east - 0.25 * lat_gap(height)
    rows = state.shape[2]
    square = 0.0
    for part, value in enumerate((height, east, north)):
        zp = lead[0, part] - value[rows:2 * rows]
        square += lane_sum(zp * zp)
    last = lax.axis_index("win") == lax.axis_size("win") - 1
    moments = [tally[0], tally[1], tally[2], tally[3] + jnp.where(last, 0.0, square)]
    lane = lax.broadcasted_iota(jnp.int32, (1, 128), 1)
    row = 0.0
    for slot, value in enumerate(moments):
        folded = jnp.sum(value, axis=0, keepdims=True)
        folded = folded + pltpu.roll(folded, 64, 1)
        folded = folded + pltpu.roll(folded, 32, 1)
        row = jnp.where(lane // 32 == slot, folded, row)
    sent[...] = jnp.broadcast_to(row, sent.shape)


def lane_sum(value):
    rows, width = value.shape
    total = value[:, :128]
    for start in range(128, width, 128):
        total = total + value[:, start:start + 128]
    return total


def two_sum(a, b):
    total = a + b
    part = total - a
    return total, (a - (total - part)) + (b - part)


def split(a):
    wide = 4097.0 * a
    top = wide - (wide - a)
    return top, a - top


def two_product(a, b):
    product = a * b
    a_top, a_low = split(a)
    b_top, b_low = split(b)
    return product, ((a_top * b_top - product) + a_top * b_low + a_low * b_top) + a_low * b_low


def pair_product(a, b):
    product, rest = two_product(a[0], b[0])
    return product, rest + (a[0] * b[1] + a[1] * b[0])


def pair_gap(a, b):
    total, rest = two_sum(a[0], -b[0])
    return total + (rest + (a[1] - b[1]))


def coefficients(gathered):
    top = jnp.sum(gathered[...], axis=0, keepdims=True)
    low = jnp.zeros_like(top)
    shift = 1
    while shift < 32:
        top, rest = two_sum(top, pltpu.roll(top, shift, 1))
        low = low + pltpu.roll(low, shift, 1) + rest
        shift *= 2
    tops = [jnp.broadcast_to(top[:, lane:lane + 1], (1, 128)) for lane in range(31, 128, 32)]
    lows = [jnp.broadcast_to(low[:, lane:lane + 1], (1, 128)) for lane in range(31, 128, 32)]
    scale = 1.0 / tops[1]
    moments = []
    for value, rest in zip(tops, lows):
        product, error = two_product(value, scale)
        moments.append((product, error + rest * scale))
    m1, m2, m3, m4 = moments
    gap = pair_gap(pair_product(m2, m4), pair_product(m3, m3))
    y1 = pair_gap(pair_product(m1, m4), pair_product(m2, m3)) / gap
    y2 = pair_gap(pair_product(m2, m2), pair_product(m1, m3)) / gap
    return y1, y2


def combine_kernel(gathered, p, m, dvar, rvar, state, dual_model, dual_obs, increment):
    y1, y2 = coefficients(gathered)
    rows, width = p.shape[2:]
    y1 = jnp.broadcast_to(jnp.concatenate([y1] * (width // 128), axis=1), (rows, width))
    y2 = jnp.broadcast_to(jnp.concatenate([y2] * (width // 128), axis=1), (rows, width))
    for part in range(3):
        dual_model[0, part] = (y1 + y2 * dvar[0, part]) * p[0, part]
        dual_obs[0, part] = (y1 + y2 * rvar[0, part]) * m[0, part]
        increment[0, part] = y2 * state[0, part]


def run(kernel, out_shapes, *operands, scratch=(), space=pltpu.VMEM, work=4):
    shapes = [jax.ShapeDtypeStruct(shape, jnp.float32) for shape in out_shapes]
    size = sum(4 * operand.size for operand in operands) + sum(4 * shape.size for shape in shapes)
    if space is not pltpu.VMEM:
        operands = [pltpu.with_memory_space_constraint(operand, space) for operand in operands]
    return pl.pallas_call(
        kernel,
        out_shape=shapes,
        in_specs=[pl.BlockSpec(memory_space=space)] * len(operands),
        out_specs=[pl.BlockSpec(memory_space=pltpu.VMEM)] * len(shapes),
        scratch_shapes=scratch,
        compiler_params=pltpu.CompilerParams(vmem_limit_bytes=32 * 1024 * 1024),
        cost_estimate=pl.CostEstimate(flops=work * size, bytes_accessed=size, transcendentals=0),
    )(*operands)


def shifted(value, step):
    count = lax.axis_size("win")
    initial, last = (max(0, -step), min(count, count - step))
    return lax.ppermute(value, "win", [(source, source + step) for source in range(initial, last)])


def lat_count():
    return lax.axis_size("band") * lax.axis_size("half")


def lat_index():
    return lax.axis_index("band") * lax.axis_size("half") + lax.axis_index("half")


def swapped(value, first):
    pairs = []
    for lat in range(first, lat_count() - 1, 2):
        pairs += [(lat, lat + 1), (lat + 1, lat)]
    return lax.ppermute(value, ("band", "half"), pairs)


def crossed(value, middle_step, edge_step):
    wins = lax.axis_size("win")
    pairs = []
    for win in range(wins):
        for source, target, step in ((1, 2, middle_step), (2, 1, middle_step), (0, 3, edge_step), (3, 0, edge_step)):
            if step is not None and 0 <= win + step < wins:
                pairs.append((4 * win + source, 4 * (win + step) + target))
    return lax.ppermute(value, ("win", "band", "half"), pairs)


def body(model_rhs, obs_rhs, model_var, obs_var, obs_weight, depth):
    rows, width = model_rhs.shape[2:]
    ranks = lax.axis_size("win") * lat_count()
    total_rows = rows * lat_count()
    offset = (GRID_ROWS - total_rows) // 2
    local_rows = lat_index() * rows - rows + jnp.arange(3 * rows, dtype=jnp.int32)
    latitude = -jnp.pi / 2 + (local_rows.astype(jnp.float32) + offset + 0.5) * (jnp.pi / GRID_ROWS)
    inside = ((local_rows >= 0) & (local_rows < total_rows)).astype(jnp.float32)
    spin = inside * (mass_rate * spin_rate * jnp.sin(latitude))
    inside = jnp.broadcast_to(inside[:, None], (3 * rows, width))
    spin = jnp.broadcast_to(spin[:, None], (3 * rows, width))
    field = model_rhs.shape
    depth_near = swapped(depth, 0)
    came = shifted(model_rhs, -1)
    scaled = model_rhs * model_var
    pair = jnp.concatenate([model_rhs, scaled], axis=1)
    edges = jnp.where(is_middle(), pair, depth_near[:, None])
    far = crossed(edges, -1, 0)
    place = (depth, depth_near, swapped(far[:, 0], 0), spin, inside)
    held_scaled, _ = lax.optimization_barrier((scaled, edges))
    scaled_came = shifted(held_scaled, -1)
    state, lead = run(
        first_adjoint_kernel, [field] * 2,
        came, swapped(came, 0), far, *place, model_rhs, obs_rhs, model_var, obs_weight,
    )
    lead_came = shifted(lead, -1)
    held, _ = lax.optimization_barrier((scaled_came, state))
    (tally,) = run(
        second_adjoint_kernel, [(4, rows, 128)],
        scaled_came, swapped(held, 0), far, *place,
        model_rhs, obs_rhs, model_var, obs_var, obs_weight, state, lead,
    )
    (sent,) = run(
        forward_kernel, [(ranks, 128)],
        state, swapped(state, 0), crossed(state, 0, None), *place, lead_came, tally,
    )
    gathered = lax.all_to_all(sent, ("win", "band", "half"), 0, 0, tiled=True)
    return run(combine_kernel, [field] * 3, gathered, model_rhs, obs_rhs, model_var, obs_var, state)


def solution(mesh):
    wins, lats = mesh.devices.shape
    mesh = Mesh(mesh.devices.reshape(wins, lats // 2, 2), ("win", "band", "half"))
    lat = ("band", "half")
    field = P("win", None, lat, None)
    in_specs = (field,) * 5 + (P("win", lat, None),)
    return jax.shard_map(body, mesh=mesh, in_specs=in_specs, out_specs=(field,) * 3, check_vma=False)
```

```python
import jax
import jax.numpy as jnp
from jax import lax
from jax.experimental import pallas as pl
from jax.experimental.pallas import tpu as pltpu
from jax.sharding import Mesh, PartitionSpec as P

GRID_ROWS = 768
STEPS = 4

mass_rate = 0.5
press_rate = 0.5
spin_rate = 0.4


def lon_gap(field):
    width = field.shape[-1]
    return pltpu.roll(field, width - 1, 1) - pltpu.roll(field, 1, 1)


def lat_gap(field):
    rows = field.shape[0]
    return pltpu.roll(field, rows - 1, 0) - pltpu.roll(field, 1, 0)


def is_middle():
    return lax.axis_index("band") != lax.axis_index("half")


def stacked(own, near, far, index):
    even = lax.axis_index("half") == 0
    outer = jnp.where(is_middle(), far[index], 0.0)
    low = jnp.where(even, outer, near[index])
    high = jnp.where(even, near[index], outer)
    return jnp.concatenate([low, own[index], high], axis=0)


def scale_kernel(p, dvar, scaled, pv, dv, sems):
    copies = [pltpu.make_async_copy(p, pv, sems.at[0]), pltpu.make_async_copy(dvar, dv, sems.at[1])]
    for copy in copies:
        copy.start()
    for copy in copies:
        copy.wait()
    for part in range(3):
        scaled[0, part] = dv[0, part] * pv[0, part]


def stretched(depth, depth_near, depth_far):
    return 0.25 * stacked(depth, depth_near, depth_far, 0)


def adjoint(own, near, far, depth, turn, keep):
    adj_height, adj_east, adj_north = [stacked(own.at[0], near.at[0], far.at[0], part) for part in range(3)]
    for step in range(STEPS):
        adj_mid = adj_east - turn * adj_north
        adj_height = keep * (adj_height + 0.25 * (lat_gap(adj_north) + lon_gap(adj_mid)))
        adj_north = adj_north + turn * adj_mid + depth * lat_gap(adj_height)
        adj_east = adj_mid + depth * lon_gap(adj_height)
    rows = own.shape[2]
    return [value[rows:2 * rows] for value in (adj_height, adj_east, adj_north)]


def first_adjoint_kernel(own, near, far, depth, depth_near, depth_far, spin, inside, p, m, dvar, hobs, state, lead):
    swept = adjoint(own, near, far, stretched(depth, depth_near, depth_far), spin[...], inside[...])
    for part, value in enumerate(swept):
        pv, dv = p[0, part], dvar[0, part]
        ux = pv - value + hobs[0, part] * m[0, part]
        state[0, part] = ux
        lead[0, part] = dv * (dv * pv) + ux


def second_adjoint_kernel(
    own, near, far, depth, depth_near, depth_far, spin, inside, p, m, dvar, rvar, hobs, state, lead, tally
):
    swept = adjoint(own, near, far, stretched(depth, depth_near, depth_far), spin[...], inside[...])
    first = lax.axis_index("win") == 0
    moments = [0.0, 0.0, 0.0, 0.0]
    for part, value in enumerate(swept):
        dv, rv, hv = dvar[0, part], rvar[0, part], hobs[0, part]
        pv, mv, ux = p[0, part], m[0, part], state[0, part]
        up, um = dv * pv, rv * mv
        zp = jnp.where(first, lead[0, part], 0.0)
        zm = rv * um + hv * ux
        zx = up - value + hv * um
        moments[0] += lane_sum(up * pv + um * mv)
        moments[1] += lane_sum(up * up + um * um + ux * ux)
        moments[2] += lane_sum(dv * up * up + rv * um * um + 2.0 * (zx * ux))
        moments[3] += lane_sum(zp * zp + zm * zm + zx * zx)
    for row, value in enumerate(moments):
        tally[row] = value


def forward_kernel(state, near, far, depth, depth_near, depth_far, spin, inside, lead, tally, sent):
    quarter = stretched(depth, depth_near, depth_far)
    turn, keep = spin[...], inside[...]
    height, east, north = [stacked(state.at[0], near.at[0], far.at[0], part) for part in range(3)]
    for step in range(STEPS):
        height = keep * (height - (lon_gap(quarter * east) + lat_gap(quarter * north)))
        east = east + turn * north - 0.25 * lon_gap(height)
        north = north - turn * east - 0.25 * lat_gap(height)
    rows = state.shape[2]
    square = 0.0
    for part, value in enumerate((height, east, north)):
        zp = lead[0, part] - value[rows:2 * rows]
        square += lane_sum(zp * zp)
    last = lax.axis_index("win") == lax.axis_size("win") - 1
    moments = [tally[0], tally[1], tally[2], tally[3] + jnp.where(last, 0.0, square)]
    lane = lax.broadcasted_iota(jnp.int32, (1, 128), 1)
    row = 0.0
    for slot, value in enumerate(moments):
        folded = jnp.sum(value, axis=0, keepdims=True)
        folded = folded + pltpu.roll(folded, 64, 1)
        folded = folded + pltpu.roll(folded, 32, 1)
        row = jnp.where(lane // 32 == slot, folded, row)
    sent[...] = jnp.broadcast_to(row, sent.shape)


def lane_sum(value):
    rows, width = value.shape
    total = value[:, :128]
    for start in range(128, width, 128):
        total = total + value[:, start:start + 128]
    return total


def two_sum(a, b):
    total = a + b
    part = total - a
    return total, (a - (total - part)) + (b - part)


def split(a):
    wide = 4097.0 * a
    top = wide - (wide - a)
    return top, a - top


def two_product(a, b):
    product = a * b
    a_top, a_low = split(a)
    b_top, b_low = split(b)
    return product, ((a_top * b_top - product) + a_top * b_low + a_low * b_top) + a_low * b_low


def pair_product(a, b):
    product, rest = two_product(a[0], b[0])
    return product, rest + (a[0] * b[1] + a[1] * b[0])


def pair_gap(a, b):
    total, rest = two_sum(a[0], -b[0])
    return total + (rest + (a[1] - b[1]))


def coefficients(gathered):
    top = jnp.sum(gathered[...], axis=0, keepdims=True)
    low = jnp.zeros_like(top)
    shift = 1
    while shift < 32:
        top, rest = two_sum(top, pltpu.roll(top, shift, 1))
        low = low + pltpu.roll(low, shift, 1) + rest
        shift *= 2
    tops = [jnp.broadcast_to(top[:, lane:lane + 1], (1, 128)) for lane in range(31, 128, 32)]
    lows = [jnp.broadcast_to(low[:, lane:lane + 1], (1, 128)) for lane in range(31, 128, 32)]
    scale = 1.0 / tops[1]
    moments = []
    for value, rest in zip(tops, lows):
        product, error = two_product(value, scale)
        moments.append((product, error + rest * scale))
    m1, m2, m3, m4 = moments
    gap = pair_gap(pair_product(m2, m4), pair_product(m3, m3))
    y1 = pair_gap(pair_product(m1, m4), pair_product(m2, m3)) / gap
    y2 = pair_gap(pair_product(m2, m2), pair_product(m1, m3)) / gap
    return y1, y2


def combine_kernel(gathered, p, m, dvar, rvar, state, dual_model, dual_obs, increment):
    y1, y2 = coefficients(gathered)
    rows, width = p.shape[2:]
    y1 = jnp.broadcast_to(jnp.concatenate([y1] * (width // 128), axis=1), (rows, width))
    y2 = jnp.broadcast_to(jnp.concatenate([y2] * (width // 128), axis=1), (rows, width))
    for part in range(3):
        dual_model[0, part] = (y1 + y2 * dvar[0, part]) * p[0, part]
        dual_obs[0, part] = (y1 + y2 * rvar[0, part]) * m[0, part]
        increment[0, part] = y2 * state[0, part]


def run(kernel, out_shapes, *operands, scratch=(), space=pltpu.VMEM, work=4):
    shapes = [jax.ShapeDtypeStruct(shape, jnp.float32) for shape in out_shapes]
    size = sum(4 * operand.size for operand in operands) + sum(4 * shape.size for shape in shapes)
    if space is not pltpu.VMEM:
        operands = [pltpu.with_memory_space_constraint(operand, space) for operand in operands]
    return pl.pallas_call(
        kernel,
        out_shape=shapes,
        in_specs=[pl.BlockSpec(memory_space=space)] * len(operands),
        out_specs=[pl.BlockSpec(memory_space=pltpu.VMEM)] * len(shapes),
        scratch_shapes=scratch,
        compiler_params=pltpu.CompilerParams(vmem_limit_bytes=32 * 1024 * 1024),
        cost_estimate=pl.CostEstimate(flops=work * size, bytes_accessed=size, transcendentals=0),
    )(*operands)


def shifted(value, step):
    count = lax.axis_size("win")
    initial, last = (max(0, -step), min(count, count - step))
    return lax.ppermute(value, "win", [(source, source + step) for source in range(initial, last)])


def lat_count():
    return lax.axis_size("band") * lax.axis_size("half")


def lat_index():
    return lax.axis_index("band") * lax.axis_size("half") + lax.axis_index("half")


def swapped(value, first):
    pairs = []
    for lat in range(first, lat_count() - 1, 2):
        pairs += [(lat, lat + 1), (lat + 1, lat)]
    return lax.ppermute(value, ("band", "half"), pairs)


def crossed(value, ends, win_step=0):
    wins = lax.axis_size("win")
    pairs = []
    for win in range(wins):
        for source, target in (ends, ends[::-1]):
            if 0 <= win + win_step < wins:
                pairs.append((4 * win + source, 4 * (win + win_step) + target))
    return lax.ppermute(value, ("win", "band", "half"), pairs)


def body(model_rhs, obs_rhs, model_var, obs_var, obs_weight, depth):
    rows, width = model_rhs.shape[2:]
    ranks = lax.axis_size("win") * lat_count()
    total_rows = rows * lat_count()
    offset = (GRID_ROWS - total_rows) // 2
    local_rows = lat_index() * rows - rows + jnp.arange(3 * rows, dtype=jnp.int32)
    latitude = -jnp.pi / 2 + (local_rows.astype(jnp.float32) + offset + 0.5) * (jnp.pi / GRID_ROWS)
    inside = ((local_rows >= 0) & (local_rows < total_rows)).astype(jnp.float32)
    spin = inside * (mass_rate * spin_rate * jnp.sin(latitude))
    inside = jnp.broadcast_to(inside[:, None], (3 * rows, width))
    spin = jnp.broadcast_to(spin[:, None], (3 * rows, width))
    field = model_rhs.shape
    middle, outer = (1, 2), (0, 3)
    came = shifted(model_rhs, -1)
    came_far = crossed(model_rhs, middle, -1)
    depth_near = swapped(depth, 0)
    place = (depth, depth_near, swapped(crossed(depth_near, outer), 0), spin, inside)
    (scaled,) = run(
        scale_kernel, [field], model_rhs, model_var, space=pltpu.HBM,
        scratch=[pltpu.VMEM(field, jnp.float32)] * 2 + [pltpu.SemaphoreType.DMA((2,))],
    )
    scaled_came = shifted(scaled, -1)
    scaled_far = crossed(swapped(scaled, 0), outer, -1)
    state, lead = run(
        first_adjoint_kernel, [field] * 2,
        came, swapped(came, 0), came_far, *place, model_rhs, obs_rhs, model_var, obs_weight,
    )
    lead_came = shifted(lead, -1)
    held, held_far, _ = lax.optimization_barrier((scaled_came, scaled_far, state))
    (tally,) = run(
        second_adjoint_kernel, [(4, rows, 128)],
        scaled_came, swapped(held, 0), swapped(held_far, 0), *place,
        model_rhs, obs_rhs, model_var, obs_var, obs_weight, state, lead,
    )
    (sent,) = run(
        forward_kernel, [(ranks, 128)],
        state, swapped(state, 0), crossed(state, middle), *place, lead_came, tally,
    )
    gathered = lax.all_to_all(sent, ("win", "band", "half"), 0, 0, tiled=True)
    return run(combine_kernel, [field] * 3, gathered, model_rhs, obs_rhs, model_var, obs_var, state)


def solution(mesh):
    wins, lats = mesh.devices.shape
    mesh = Mesh(mesh.devices.reshape(wins, lats // 2, 2), ("win", "band", "half"))
    lat = ("band", "half")
    field = P("win", None, lat, None)
    in_specs = (field,) * 5 + (P("win", lat, None),)
    return jax.shard_map(body, mesh=mesh, in_specs=in_specs, out_specs=(field,) * 3, check_vma=False)
```

```python
import jax
import jax.numpy as jnp
from jax import lax
from jax.experimental import pallas as pl
from jax.experimental.pallas import tpu as pltpu
from jax.sharding import Mesh, PartitionSpec as P

GRID_ROWS = 768
STEPS = 4

mass_rate = 0.5
press_rate = 0.5
spin_rate = 0.4


def lon_gap(field):
    width = field.shape[-1]
    return pltpu.roll(field, width - 1, 1) - pltpu.roll(field, 1, 1)


def lat_gap(field):
    rows = field.shape[0]
    return pltpu.roll(field, rows - 1, 0) - pltpu.roll(field, 1, 0)


def even_lat():
    return lax.axis_index("half") == 0


def has_previous():
    return lax.axis_index("win") > 0


def stacked(own, near, far, index):
    even = even_lat()
    low = jnp.where(even, far[index], near[index])
    high = jnp.where(even, near[index], far[index])
    return jnp.concatenate([low, own[index], high], axis=0)


def prep_kernel(p, m, dvar, rvar, hobs, depth, pair, straight, local, pv, mv, dv, rv, hv, sems):
    copies = [
        pltpu.make_async_copy(source, target, sems.at[slot])
        for slot, (source, target) in enumerate(
            ((p, pv), (m, mv), (dvar, dv), (rvar, rv), (hobs, hv), (depth, straight.at[0:1]))
        )
    ]
    for copy in copies:
        copy.start()
    for copy in copies:
        copy.wait()
    for part in range(3):
        up = dv[0, part] * pv[0, part]
        seen = hv[0, part] * mv[0, part]
        pair[part] = pv[0, part]
        pair[3 + part] = up
        straight[1 + part] = pv[0, part] + seen
        local[part] = up + rv[0, part] * seen


def stretched(straight, relayed):
    even = even_lat()
    low = jnp.where(even, relayed[1], relayed[0])
    high = jnp.where(even, relayed[0], relayed[1])
    return 0.25 * jnp.concatenate([low, straight[0], high], axis=0)


def adjoint(pair, pair_near, pair_far, straight, relayed, spin, inside, base):
    depth = stretched(straight, relayed)
    turn, keep = spin[...], inside[...]
    adj_height, adj_east, adj_north = [stacked(pair, pair_near, pair_far, base + part) for part in range(3)]
    for step in range(STEPS):
        adj_mid = adj_east - turn * adj_north
        adj_height = keep * (adj_height + 0.25 * (lat_gap(adj_north) + lon_gap(adj_mid)))
        adj_north = adj_north + turn * adj_mid + depth * lat_gap(adj_height)
        adj_east = adj_mid + depth * lon_gap(adj_height)
    rows = pair.shape[1]
    return [value[rows:2 * rows] for value in (adj_height, adj_east, adj_north)]


def first_adjoint_kernel(pair, pair_near, pair_far, straight, relayed, spin, inside, state, back):
    swept = adjoint(pair, pair_near, pair_far, straight, relayed, spin, inside, 0)
    link = has_previous()
    for part, value in enumerate(swept):
        back[part] = value
        state[part] = jnp.where(link, straight[1 + part] - value, 0.0)


def second_adjoint_kernel(pair, pair_near, pair_far, straight, relayed, spin, inside, local, state, tally):
    swept = adjoint(pair, pair_near, pair_far, straight, relayed, spin, inside, 3)
    link = has_previous()
    cross = square = 0.0
    for part, value in enumerate(swept):
        zx = jnp.where(link, local[part] - value, 0.0)
        cross += lane_sum(zx * state[part])
        square += lane_sum(zx * zx)
    tally[0] = cross
    tally[1] = square


def forward_kernel(state, state_near, state_far, straight, relayed, spin, inside, end):
    depth = stretched(straight, relayed)
    turn, keep = spin[...], inside[...]
    height, east, north = [stacked(state, state_near, state_far, part) for part in range(3)]
    for step in range(STEPS):
        height = keep * (height - (lon_gap(depth * east) + lat_gap(depth * north)))
        east = east + turn * north - 0.25 * lon_gap(height)
        north = north - turn * east - 0.25 * lat_gap(height)
    rows = state.shape[1]
    for part, value in enumerate((height, east, north)):
        end[part] = value[rows:2 * rows]


def lane_sum(value):
    rows, width = value.shape
    total = value[:, :128]
    for start in range(128, width, 128):
        total = total + value[:, start:start + 128]
    return total


def inner_kernel(p, m, dvar, rvar, hobs, back, end, tally, sent):
    last = lax.axis_index("win") == lax.axis_size("win") - 1
    moments = [0.0, 0.0, 2.0 * tally[0], tally[1]]
    for part in range(3):
        dv, rv, hv = dvar[0, part], rvar[0, part], hobs[0, part]
        pv, mv = p[0, part], m[0, part]
        up, um = dv * pv, rv * mv
        ux = pv - back[part] + hv * mv
        zp = dv * up + ux - end[part]
        zm = rv * um + hv * ux
        zx = jnp.where(last, up + hv * um, 0.0)
        moments[0] += lane_sum(up * pv + um * mv)
        moments[1] += lane_sum(up * up + um * um + ux * ux)
        moments[2] += lane_sum(dv * up * up + rv * um * um + 2.0 * (zx * ux))
        moments[3] += lane_sum(zp * zp + zm * zm + zx * zx)
    lane = lax.broadcasted_iota(jnp.int32, (1, 128), 1)
    row = 0.0
    for slot, value in enumerate(moments):
        folded = jnp.sum(value, axis=0, keepdims=True)
        folded = folded + pltpu.roll(folded, 64, 1)
        folded = folded + pltpu.roll(folded, 32, 1)
        row = jnp.where(lane // 32 == slot, folded, row)
    sent[...] = jnp.broadcast_to(row, sent.shape)


def lane_sum(value):
    rows, width = value.shape
    total = value[:, :128]
    for start in range(128, width, 128):
        total = total + value[:, start:start + 128]
    return total


def two_sum(a, b):
    total = a + b
    part = total - a
    return total, (a - (total - part)) + (b - part)


def split(a):
    wide = 4097.0 * a
    top = wide - (wide - a)
    return top, a - top


def two_product(a, b):
    product = a * b
    a_top, a_low = split(a)
    b_top, b_low = split(b)
    return product, ((a_top * b_top - product) + a_top * b_low + a_low * b_top) + a_low * b_low


def pair_product(a, b):
    product, rest = two_product(a[0], b[0])
    return product, rest + (a[0] * b[1] + a[1] * b[0])


def pair_gap(a, b):
    total, rest = two_sum(a[0], -b[0])
    return total + (rest + (a[1] - b[1]))


def coefficients(gathered):
    top = jnp.sum(gathered[...], axis=0, keepdims=True)
    low = jnp.zeros_like(top)
    shift = 1
    while shift < 32:
        top, rest = two_sum(top, pltpu.roll(top, shift, 1))
        low = low + pltpu.roll(low, shift, 1) + rest
        shift *= 2
    tops = [jnp.broadcast_to(top[:, lane:lane + 1], (1, 128)) for lane in range(31, 128, 32)]
    lows = [jnp.broadcast_to(low[:, lane:lane + 1], (1, 128)) for lane in range(31, 128, 32)]
    scale = 1.0 / tops[1]
    moments = []
    for value, rest in zip(tops, lows):
        product, error = two_product(value, scale)
        moments.append((product, error + rest * scale))
    m1, m2, m3, m4 = moments
    gap = pair_gap(pair_product(m2, m4), pair_product(m3, m3))
    y1 = pair_gap(pair_product(m1, m4), pair_product(m2, m3)) / gap
    y2 = pair_gap(pair_product(m2, m2), pair_product(m1, m3)) / gap
    return y1, y2


def combine_kernel(gathered, p, m, dvar, rvar, hobs, back, dual_model, dual_obs, increment):
    y1, y2 = coefficients(gathered)
    rows, width = p.shape[2:]
    y1 = jnp.broadcast_to(jnp.concatenate([y1] * (width // 128), axis=1), (rows, width))
    y2 = jnp.broadcast_to(jnp.concatenate([y2] * (width // 128), axis=1), (rows, width))
    for part in range(3):
        pv, mv = p[0, part], m[0, part]
        dual_model[0, part] = (y1 + y2 * dvar[0, part]) * pv
        dual_obs[0, part] = (y1 + y2 * rvar[0, part]) * mv
        increment[0, part] = y2 * (pv - back[part] + hobs[0, part] * mv)


def run(kernel, out_shapes, *operands, scratch=(), space=pltpu.VMEM, work=4):
    shapes = [jax.ShapeDtypeStruct(shape, jnp.float32) for shape in out_shapes]
    size = sum(4 * operand.size for operand in operands) + sum(4 * shape.size for shape in shapes)
    if space is not pltpu.VMEM:
        operands = [pltpu.with_memory_space_constraint(operand, space) for operand in operands]
    return pl.pallas_call(
        kernel,
        out_shape=shapes,
        in_specs=[pl.BlockSpec(memory_space=space)] * len(operands),
        out_specs=[pl.BlockSpec(memory_space=pltpu.VMEM)] * len(shapes),
        scratch_shapes=scratch,
        compiler_params=pltpu.CompilerParams(vmem_limit_bytes=32 * 1024 * 1024),
        cost_estimate=pl.CostEstimate(flops=work * size, bytes_accessed=size, transcendentals=0),
    )(*operands)


def shifted(value, step):
    count = lax.axis_size("win")
    initial, last = (max(0, -step), min(count, count - step))
    return lax.ppermute(value, "win", [(source, source + step) for source in range(initial, last)])


def lat_count():
    return lax.axis_size("band") * lax.axis_size("half")


def lat_index():
    return lax.axis_index("band") * lax.axis_size("half") + lax.axis_index("half")


def swapped(value, first):
    pairs = []
    for lat in range(first, lat_count() - 1, 2):
        pairs += [(lat, lat + 1), (lat + 1, lat)]
    return lax.ppermute(value, ("band", "half"), pairs)


def crossed(value, ends, win_step=0):
    wins = lax.axis_size("win")
    pairs = []
    for win in range(wins):
        for source, target in (ends, ends[::-1]):
            if 0 <= win + win_step < wins:
                pairs.append((4 * win + source, 4 * (win + win_step) + target))
    return lax.ppermute(value, ("win", "band", "half"), pairs)


def body(model_rhs, obs_rhs, model_var, obs_var, obs_weight, depth):
    rows, width = model_rhs.shape[2:]
    ranks = lax.axis_size("win") * lat_count()
    total_rows = rows * lat_count()
    offset = (GRID_ROWS - total_rows) // 2
    local_rows = lat_index() * rows - rows + jnp.arange(3 * rows, dtype=jnp.int32)
    latitude = -jnp.pi / 2 + (local_rows.astype(jnp.float32) + offset + 0.5) * (jnp.pi / GRID_ROWS)
    inside = ((local_rows >= 0) & (local_rows < total_rows)).astype(jnp.float32)
    spin = inside * (mass_rate * spin_rate * jnp.sin(latitude))
    inside = jnp.broadcast_to(inside[:, None], (3 * rows, width))
    spin = jnp.broadcast_to(spin[:, None], (3 * rows, width))
    fields = (3, rows, width)

    middle, outer = (1, 2), (0, 3)
    pair, straight, local = run(
        prep_kernel, [(6, rows, width), (4, rows, width), fields],
        model_rhs, obs_rhs, model_var, obs_var, obs_weight, depth,
        scratch=[pltpu.VMEM(model_rhs.shape, jnp.float32)] * 5 + [pltpu.SemaphoreType.DMA((6,))],
        space=pltpu.HBM,
    )
    came = shifted(straight, 1)
    depth_near = swapped(depth, 0)
    depth_edge = crossed(depth_near, outer, 1)
    relayed = swapped(jnp.concatenate([came[:1], depth_edge]), 0)
    local, _ = lax.optimization_barrier((local, depth_near))
    local = shifted(local, 1)
    pair_near, pair_far = swapped(pair, 0), crossed(pair, middle)
    known = (pair, pair_near, pair_far, came, relayed, spin, inside)
    state, back = run(first_adjoint_kernel, [fields, fields], *known)
    back = shifted(back, -1)
    state_near, state_far = swapped(state, 0), crossed(state, middle)
    (tally,) = run(second_adjoint_kernel, [(2, rows, 128)], *known, local, state)
    (end,) = run(forward_kernel, [fields], state, state_near, state_far, came, relayed, spin, inside)
    (sent,) = run(
        inner_kernel, [(ranks, 128)],
        model_rhs, obs_rhs, model_var, obs_var, obs_weight, back, end, tally,
    )
    gathered = lax.all_to_all(sent, ("win", "band", "half"), 0, 0, tiled=True)
    return run(
        combine_kernel, [model_rhs.shape] * 3,
        gathered, model_rhs, obs_rhs, model_var, obs_var, obs_weight, back,
    )


def solution(mesh):
    wins, lats = mesh.devices.shape
    mesh = Mesh(mesh.devices.reshape(wins, lats // 2, 2), ("win", "band", "half"))
    lat = ("band", "half")
    field = P("win", None, lat, None)
    in_specs = (field,) * 5 + (P("win", lat, None),)
    return jax.shard_map(body, mesh=mesh, in_specs=in_specs, out_specs=(field,) * 3, check_vma=False)
```

```python
import jax
import jax.numpy as jnp
from jax import lax
from jax.experimental import pallas as pl
from jax.experimental.pallas import tpu as pltpu
from jax.sharding import Mesh, PartitionSpec as P

GRID_ROWS = 768
STEPS = 4

mass_rate = 0.5
press_rate = 0.5
spin_rate = 0.4


def lon_gap(field):
    width = field.shape[-1]
    return pltpu.roll(field, width - 1, 1) - pltpu.roll(field, 1, 1)


def lat_gap(field):
    rows = field.shape[0]
    return pltpu.roll(field, rows - 1, 0) - pltpu.roll(field, 1, 0)


def even_lat():
    return lax.axis_index("half") == 0


def has_previous():
    return lax.axis_index("win") > 0


def stacked(own, near, far, index):
    even = even_lat()
    low = jnp.where(even, far[index], near[index])
    high = jnp.where(even, near[index], far[index])
    return jnp.concatenate([low, own[index], high], axis=0)


def prep_kernel(p, m, dvar, rvar, hobs, depth, pair, straight, local, pv, mv, dv, rv, hv, sems):
    copies = [
        pltpu.make_async_copy(source, target, sems.at[slot])
        for slot, (source, target) in enumerate(
            ((p, pv), (m, mv), (dvar, dv), (rvar, rv), (hobs, hv), (depth, straight.at[0:1]))
        )
    ]
    for copy in copies:
        copy.start()
    for copy in copies:
        copy.wait()
    for part in range(3):
        up = dv[0, part] * pv[0, part]
        seen = hv[0, part] * mv[0, part]
        pair[part] = pv[0, part]
        pair[3 + part] = up
        straight[1 + part] = pv[0, part] + seen
        local[part] = up + rv[0, part] * seen


def widened(tile, width):
    return jnp.concatenate([tile[...]] * (width // 128), axis=1)


def stretched(straight, relayed):
    even = even_lat()
    low = jnp.where(even, relayed[1], relayed[0])
    high = jnp.where(even, relayed[0], relayed[1])
    return 0.25 * jnp.concatenate([low, straight[0], high], axis=0)


def adjoint(pair, pair_near, pair_far, straight, relayed, spin, inside, base):
    depth = stretched(straight, relayed)
    turn, keep = widened(spin, depth.shape[1]), widened(inside, depth.shape[1])
    adj_height, adj_east, adj_north = [stacked(pair, pair_near, pair_far, base + part) for part in range(3)]
    for step in range(STEPS):
        adj_mid = adj_east - turn * adj_north
        adj_height = keep * (adj_height + 0.25 * (lat_gap(adj_north) + lon_gap(adj_mid)))
        adj_north = adj_north + turn * adj_mid + depth * lat_gap(adj_height)
        adj_east = adj_mid + depth * lon_gap(adj_height)
    rows = pair.shape[1]
    return [value[rows:2 * rows] for value in (adj_height, adj_east, adj_north)]


def first_adjoint_kernel(pair, pair_near, pair_far, straight, relayed, spin, inside, state, back):
    swept = adjoint(pair, pair_near, pair_far, straight, relayed, spin, inside, 0)
    link = has_previous()
    for part, value in enumerate(swept):
        back[part] = value
        state[part] = jnp.where(link, straight[1 + part] - value, 0.0)


def second_adjoint_kernel(pair, pair_near, pair_far, straight, relayed, spin, inside, local, state, tally):
    swept = adjoint(pair, pair_near, pair_far, straight, relayed, spin, inside, 3)
    link = has_previous()
    cross = square = 0.0
    for part, value in enumerate(swept):
        zx = jnp.where(link, local[part] - value, 0.0)
        cross += lane_sum(zx * state[part])
        square += lane_sum(zx * zx)
    tally[0] = cross
    tally[1] = square


def forward_kernel(state, state_near, state_far, straight, relayed, spin, inside, end):
    depth = stretched(straight, relayed)
    turn, keep = widened(spin, depth.shape[1]), widened(inside, depth.shape[1])
    height, east, north = [stacked(state, state_near, state_far, part) for part in range(3)]
    for step in range(STEPS):
        height = keep * (height - (lon_gap(depth * east) + lat_gap(depth * north)))
        east = east + turn * north - 0.25 * lon_gap(height)
        north = north - turn * east - 0.25 * lat_gap(height)
    rows = state.shape[1]
    for part, value in enumerate((height, east, north)):
        end[part] = value[rows:2 * rows]


def lane_sum(value):
    rows, width = value.shape
    total = value[:, :128]
    for start in range(128, width, 128):
        total = total + value[:, start:start + 128]
    return total


def inner_kernel(p, m, dvar, rvar, hobs, back, end, tally, sent):
    last = lax.axis_index("win") == lax.axis_size("win") - 1
    moments = [0.0, 0.0, 2.0 * tally[0], tally[1]]
    for part in range(3):
        dv, rv, hv = dvar[0, part], rvar[0, part], hobs[0, part]
        pv, mv = p[0, part], m[0, part]
        up, um = dv * pv, rv * mv
        ux = pv - back[part] + hv * mv
        zp = dv * up + ux - end[part]
        zm = rv * um + hv * ux
        zx = jnp.where(last, up + hv * um, 0.0)
        moments[0] += lane_sum(up * pv + um * mv)
        moments[1] += lane_sum(up * up + um * um + ux * ux)
        moments[2] += lane_sum(dv * up * up + rv * um * um + 2.0 * (zx * ux))
        moments[3] += lane_sum(zp * zp + zm * zm + zx * zx)
    lane = lax.broadcasted_iota(jnp.int32, (1, 128), 1)
    row = 0.0
    for slot, value in enumerate(moments):
        folded = jnp.sum(value, axis=0, keepdims=True)
        folded = folded + pltpu.roll(folded, 64, 1)
        folded = folded + pltpu.roll(folded, 32, 1)
        row = jnp.where(lane // 32 == slot, folded, row)
    sent[...] = jnp.broadcast_to(row, sent.shape)


def lane_sum(value):
    rows, width = value.shape
    total = value[:, :128]
    for start in range(128, width, 128):
        total = total + value[:, start:start + 128]
    return total


def two_sum(a, b):
    total = a + b
    part = total - a
    return total, (a - (total - part)) + (b - part)


def split(a):
    wide = 4097.0 * a
    top = wide - (wide - a)
    return top, a - top


def two_product(a, b):
    product = a * b
    a_top, a_low = split(a)
    b_top, b_low = split(b)
    return product, ((a_top * b_top - product) + a_top * b_low + a_low * b_top) + a_low * b_low


def pair_product(a, b):
    product, rest = two_product(a[0], b[0])
    return product, rest + (a[0] * b[1] + a[1] * b[0])


def pair_gap(a, b):
    total, rest = two_sum(a[0], -b[0])
    return total + (rest + (a[1] - b[1]))


def coefficients(gathered):
    top = jnp.sum(gathered[...], axis=0, keepdims=True)
    low = jnp.zeros_like(top)
    shift = 1
    while shift < 32:
        top, rest = two_sum(top, pltpu.roll(top, shift, 1))
        low = low + pltpu.roll(low, shift, 1) + rest
        shift *= 2
    tops = [jnp.broadcast_to(top[:, lane:lane + 1], (1, 128)) for lane in range(31, 128, 32)]
    lows = [jnp.broadcast_to(low[:, lane:lane + 1], (1, 128)) for lane in range(31, 128, 32)]
    scale = 1.0 / tops[1]
    moments = []
    for value, rest in zip(tops, lows):
        product, error = two_product(value, scale)
        moments.append((product, error + rest * scale))
    m1, m2, m3, m4 = moments
    gap = pair_gap(pair_product(m2, m4), pair_product(m3, m3))
    y1 = pair_gap(pair_product(m1, m4), pair_product(m2, m3)) / gap
    y2 = pair_gap(pair_product(m2, m2), pair_product(m1, m3)) / gap
    return y1, y2


def combine_kernel(gathered, p, m, dvar, rvar, hobs, back, dual_model, dual_obs, increment):
    y1, y2 = coefficients(gathered)
    rows, width = p.shape[2:]
    y1 = jnp.broadcast_to(jnp.concatenate([y1] * (width // 128), axis=1), (rows, width))
    y2 = jnp.broadcast_to(jnp.concatenate([y2] * (width // 128), axis=1), (rows, width))
    for part in range(3):
        pv, mv = p[0, part], m[0, part]
        dual_model[0, part] = (y1 + y2 * dvar[0, part]) * pv
        dual_obs[0, part] = (y1 + y2 * rvar[0, part]) * mv
        increment[0, part] = y2 * (pv - back[part] + hobs[0, part] * mv)


def run(kernel, out_shapes, *operands, scratch=(), space=pltpu.VMEM, work=4):
    shapes = [jax.ShapeDtypeStruct(shape, jnp.float32) for shape in out_shapes]
    size = sum(4 * operand.size for operand in operands) + sum(4 * shape.size for shape in shapes)
    if space is not pltpu.VMEM:
        operands = [pltpu.with_memory_space_constraint(operand, space) for operand in operands]
    return pl.pallas_call(
        kernel,
        out_shape=shapes,
        in_specs=[pl.BlockSpec(memory_space=space)] * len(operands),
        out_specs=[pl.BlockSpec(memory_space=pltpu.VMEM)] * len(shapes),
        scratch_shapes=scratch,
        compiler_params=pltpu.CompilerParams(vmem_limit_bytes=32 * 1024 * 1024),
        cost_estimate=pl.CostEstimate(flops=work * size, bytes_accessed=size, transcendentals=0),
    )(*operands)


def shifted(value, step):
    count = lax.axis_size("win")
    initial, last = (max(0, -step), min(count, count - step))
    return lax.ppermute(value, "win", [(source, source + step) for source in range(initial, last)])


def lat_count():
    return lax.axis_size("band") * lax.axis_size("half")


def lat_index():
    return lax.axis_index("band") * lax.axis_size("half") + lax.axis_index("half")


def swapped(value, first):
    pairs = []
    for lat in range(first, lat_count() - 1, 2):
        pairs += [(lat, lat + 1), (lat + 1, lat)]
    return lax.ppermute(value, ("band", "half"), pairs)


def crossed(value, ends, win_step=0):
    wins = lax.axis_size("win")
    pairs = []
    for win in range(wins):
        for source, target in (ends, ends[::-1]):
            if 0 <= win + win_step < wins:
                pairs.append((4 * win + source, 4 * (win + win_step) + target))
    return lax.ppermute(value, ("win", "band", "half"), pairs)


def body(model_rhs, obs_rhs, model_var, obs_var, obs_weight, depth):
    rows, width = model_rhs.shape[2:]
    ranks = lax.axis_size("win") * lat_count()
    total_rows = rows * lat_count()
    offset = (GRID_ROWS - total_rows) // 2
    local_rows = lat_index() * rows - rows + jnp.arange(3 * rows, dtype=jnp.int32)
    latitude = -jnp.pi / 2 + (local_rows.astype(jnp.float32) + offset + 0.5) * (jnp.pi / GRID_ROWS)
    inside = ((local_rows >= 0) & (local_rows < total_rows)).astype(jnp.float32)
    spin = inside * (mass_rate * spin_rate * jnp.sin(latitude))
    inside = jnp.broadcast_to(inside[:, None], (3 * rows, 128))
    spin = jnp.broadcast_to(spin[:, None], (3 * rows, 128))
    fields = (3, rows, width)

    middle, outer = (1, 2), (0, 3)
    pair, straight, local = run(
        prep_kernel, [(6, rows, width), (4, rows, width), fields],
        model_rhs, obs_rhs, model_var, obs_var, obs_weight, depth,
        scratch=[pltpu.VMEM(model_rhs.shape, jnp.float32)] * 5 + [pltpu.SemaphoreType.DMA((6,))],
        space=pltpu.HBM,
    )
    came = shifted(straight, 1)
    depth_near = swapped(depth, 0)
    depth_edge = crossed(depth_near, outer, 1)
    relayed = swapped(jnp.concatenate([came[:1], depth_edge]), 0)
    local, _ = lax.optimization_barrier((local, depth_near))
    local = shifted(local, 1)
    held_pair, _ = lax.optimization_barrier((pair, depth_edge))
    pair_near, pair_far = swapped(held_pair, 0), crossed(pair, middle)
    known = (pair, pair_near, pair_far, came, relayed, spin, inside)
    state, back = run(first_adjoint_kernel, [fields, fields], *known)
    back = shifted(back, -1)
    state_near, state_far = swapped(state, 0), crossed(state, middle)
    (tally,) = run(second_adjoint_kernel, [(2, rows, 128)], *known, local, state)
    (end,) = run(forward_kernel, [fields], state, state_near, state_far, came, relayed, spin, inside)
    (sent,) = run(
        inner_kernel, [(ranks, 128)],
        model_rhs, obs_rhs, model_var, obs_var, obs_weight, back, end, tally,
    )
    gathered = lax.all_to_all(sent, ("win", "band", "half"), 0, 0, tiled=True)
    return run(
        combine_kernel, [model_rhs.shape] * 3,
        gathered, model_rhs, obs_rhs, model_var, obs_var, obs_weight, back,
    )


def solution(mesh):
    wins, lats = mesh.devices.shape
    mesh = Mesh(mesh.devices.reshape(wins, lats // 2, 2), ("win", "band", "half"))
    lat = ("band", "half")
    field = P("win", None, lat, None)
    in_specs = (field,) * 5 + (P("win", lat, None),)
    return jax.shard_map(body, mesh=mesh, in_specs=in_specs, out_specs=(field,) * 3, check_vma=False)
```

```python
import jax
import jax.numpy as jnp
from jax import lax
from jax.experimental import pallas as pl
from jax.experimental.pallas import tpu as pltpu
from jax.sharding import Mesh, PartitionSpec as P

GRID_ROWS = 768
STEPS = 4

mass_rate = 0.5
press_rate = 0.5
spin_rate = 0.4


def lon_gap(field):
    width = field.shape[-1]
    return pltpu.roll(field, width - 1, 1) - pltpu.roll(field, 1, 1)


def lat_gap(field):
    rows = field.shape[0]
    return pltpu.roll(field, rows - 1, 0) - pltpu.roll(field, 1, 0)


def even_lat():
    return lax.axis_index("half") == 0


def has_previous():
    return lax.axis_index("win") > 0


def stacked(own, near, far, index):
    even = even_lat()
    low = jnp.where(even, far[index], near[index])
    high = jnp.where(even, near[index], far[index])
    return jnp.concatenate([low, own[index], high], axis=0)


def prep_kernel(p, m, dvar, rvar, hobs, depth, pair, straight, pv, mv, dv, rv, hv, sems):
    copies = [
        pltpu.make_async_copy(source, target, sems.at[slot])
        for slot, (source, target) in enumerate(
            ((p, pv), (m, mv), (dvar, dv), (rvar, rv), (hobs, hv), (depth, straight.at[0:1]))
        )
    ]
    for copy in copies:
        copy.start()
    for copy in copies:
        copy.wait()
    for part in range(3):
        up = dv[0, part] * pv[0, part]
        seen = hv[0, part] * mv[0, part]
        pair[part] = pv[0, part]
        pair[3 + part] = up
        straight[1 + part] = pv[0, part] + seen
        straight[4 + part] = up + rv[0, part] * seen


def widened(tile, width):
    return jnp.concatenate([tile[...]] * (width // 128), axis=1)


def stretched(straight, relayed):
    even = even_lat()
    low = jnp.where(even, relayed[1], relayed[0])
    high = jnp.where(even, relayed[0], relayed[1])
    return 0.25 * jnp.concatenate([low, straight[0], high], axis=0)


def adjoint(pair, pair_near, pair_far, straight, relayed, spin, inside, base):
    depth = stretched(straight, relayed)
    turn, keep = widened(spin, depth.shape[1]), widened(inside, depth.shape[1])
    adj_height, adj_east, adj_north = [stacked(pair, pair_near, pair_far, base + part) for part in range(3)]
    for step in range(STEPS):
        adj_mid = adj_east - turn * adj_north
        adj_height = keep * (adj_height + 0.25 * (lat_gap(adj_north) + lon_gap(adj_mid)))
        adj_north = adj_north + turn * adj_mid + depth * lat_gap(adj_height)
        adj_east = adj_mid + depth * lon_gap(adj_height)
    rows = pair.shape[1]
    return [value[rows:2 * rows] for value in (adj_height, adj_east, adj_north)]


def first_adjoint_kernel(pair, pair_near, pair_far, straight, relayed, spin, inside, state, back):
    swept = adjoint(pair, pair_near, pair_far, straight, relayed, spin, inside, 0)
    link = has_previous()
    for part, value in enumerate(swept):
        back[part] = value
        state[part] = jnp.where(link, straight[1 + part] - value, 0.0)


def second_adjoint_kernel(pair, pair_near, pair_far, straight, relayed, spin, inside, state, tally):
    swept = adjoint(pair, pair_near, pair_far, straight, relayed, spin, inside, 3)
    link = has_previous()
    cross = square = 0.0
    for part, value in enumerate(swept):
        zx = jnp.where(link, straight[4 + part] - value, 0.0)
        cross += lane_sum(zx * state[part])
        square += lane_sum(zx * zx)
    tally[0] = cross
    tally[1] = square


def forward_kernel(state, state_far, state_near, straight, relayed, spin, inside, end):
    depth = stretched(straight, relayed)
    turn, keep = widened(spin, depth.shape[1]), widened(inside, depth.shape[1])
    height, east, north = [stacked(state, state_near, state_far, part) for part in range(3)]
    for step in range(STEPS):
        height = keep * (height - (lon_gap(depth * east) + lat_gap(depth * north)))
        east = east + turn * north - 0.25 * lon_gap(height)
        north = north - turn * east - 0.25 * lat_gap(height)
    rows = state.shape[1]
    for part, value in enumerate((height, east, north)):
        end[part] = value[rows:2 * rows]


def lane_sum(value):
    rows, width = value.shape
    total = value[:, :128]
    for start in range(128, width, 128):
        total = total + value[:, start:start + 128]
    return total


def inner_kernel(p, m, dvar, rvar, hobs, back, end, tally, sent):
    last = lax.axis_index("win") == lax.axis_size("win") - 1
    moments = [0.0, 0.0, 2.0 * tally[0], tally[1]]
    for part in range(3):
        dv, rv, hv = dvar[0, part], rvar[0, part], hobs[0, part]
        pv, mv = p[0, part], m[0, part]
        up, um = dv * pv, rv * mv
        ux = pv - back[part] + hv * mv
        zp = dv * up + ux - end[part]
        zm = rv * um + hv * ux
        zx = jnp.where(last, up + hv * um, 0.0)
        moments[0] += lane_sum(up * pv + um * mv)
        moments[1] += lane_sum(up * up + um * um + ux * ux)
        moments[2] += lane_sum(dv * up * up + rv * um * um + 2.0 * (zx * ux))
        moments[3] += lane_sum(zp * zp + zm * zm + zx * zx)
    lane = lax.broadcasted_iota(jnp.int32, (1, 128), 1)
    row = 0.0
    for slot, value in enumerate(moments):
        folded = jnp.sum(value, axis=0, keepdims=True)
        folded = folded + pltpu.roll(folded, 64, 1)
        folded = folded + pltpu.roll(folded, 32, 1)
        row = jnp.where(lane // 32 == slot, folded, row)
    sent[...] = jnp.broadcast_to(row, sent.shape)


def lane_sum(value):
    rows, width = value.shape
    total = value[:, :128]
    for start in range(128, width, 128):
        total = total + value[:, start:start + 128]
    return total


def two_sum(a, b):
    total = a + b
    part = total - a
    return total, (a - (total - part)) + (b - part)


def split(a):
    wide = 4097.0 * a
    top = wide - (wide - a)
    return top, a - top


def two_product(a, b):
    product = a * b
    a_top, a_low = split(a)
    b_top, b_low = split(b)
    return product, ((a_top * b_top - product) + a_top * b_low + a_low * b_top) + a_low * b_low


def pair_product(a, b):
    product, rest = two_product(a[0], b[0])
    return product, rest + (a[0] * b[1] + a[1] * b[0])


def pair_gap(a, b):
    total, rest = two_sum(a[0], -b[0])
    return total + (rest + (a[1] - b[1]))


def coefficients(gathered):
    top = jnp.sum(gathered[...], axis=0, keepdims=True)
    low = jnp.zeros_like(top)
    shift = 1
    while shift < 32:
        top, rest = two_sum(top, pltpu.roll(top, shift, 1))
        low = low + pltpu.roll(low, shift, 1) + rest
        shift *= 2
    tops = [jnp.broadcast_to(top[:, lane:lane + 1], (1, 128)) for lane in range(31, 128, 32)]
    lows = [jnp.broadcast_to(low[:, lane:lane + 1], (1, 128)) for lane in range(31, 128, 32)]
    scale = 1.0 / tops[1]
    moments = []
    for value, rest in zip(tops, lows):
        product, error = two_product(value, scale)
        moments.append((product, error + rest * scale))
    m1, m2, m3, m4 = moments
    gap = pair_gap(pair_product(m2, m4), pair_product(m3, m3))
    y1 = pair_gap(pair_product(m1, m4), pair_product(m2, m3)) / gap
    y2 = pair_gap(pair_product(m2, m2), pair_product(m1, m3)) / gap
    return y1, y2


def combine_kernel(gathered, p, m, dvar, rvar, hobs, back, dual_model, dual_obs, increment):
    y1, y2 = coefficients(gathered)
    rows, width = p.shape[2:]
    y1 = jnp.broadcast_to(jnp.concatenate([y1] * (width // 128), axis=1), (rows, width))
    y2 = jnp.broadcast_to(jnp.concatenate([y2] * (width // 128), axis=1), (rows, width))
    for part in range(3):
        pv, mv = p[0, part], m[0, part]
        dual_model[0, part] = (y1 + y2 * dvar[0, part]) * pv
        dual_obs[0, part] = (y1 + y2 * rvar[0, part]) * mv
        increment[0, part] = y2 * (pv - back[part] + hobs[0, part] * mv)


def run(kernel, out_shapes, *operands, scratch=(), space=pltpu.VMEM, work=4):
    shapes = [jax.ShapeDtypeStruct(shape, jnp.float32) for shape in out_shapes]
    size = sum(4 * operand.size for operand in operands) + sum(4 * shape.size for shape in shapes)
    if space is not pltpu.VMEM:
        operands = [pltpu.with_memory_space_constraint(operand, space) for operand in operands]
    return pl.pallas_call(
        kernel,
        out_shape=shapes,
        in_specs=[pl.BlockSpec(memory_space=space)] * len(operands),
        out_specs=[pl.BlockSpec(memory_space=pltpu.VMEM)] * len(shapes),
        scratch_shapes=scratch,
        compiler_params=pltpu.CompilerParams(vmem_limit_bytes=32 * 1024 * 1024),
        cost_estimate=pl.CostEstimate(flops=work * size, bytes_accessed=size, transcendentals=0),
    )(*operands)


def shifted(value, step):
    count = lax.axis_size("win")
    initial, last = (max(0, -step), min(count, count - step))
    return lax.ppermute(value, "win", [(source, source + step) for source in range(initial, last)])


def lat_count():
    return lax.axis_size("band") * lax.axis_size("half")


def lat_index():
    return lax.axis_index("band") * lax.axis_size("half") + lax.axis_index("half")


def swapped(value, first):
    pairs = []
    for lat in range(first, lat_count() - 1, 2):
        pairs += [(lat, lat + 1), (lat + 1, lat)]
    return lax.ppermute(value, ("band", "half"), pairs)


def crossed(value, ends, win_step=0):
    wins = lax.axis_size("win")
    pairs = []
    for win in range(wins):
        for source, target in (ends, ends[::-1]):
            if 0 <= win + win_step < wins:
                pairs.append((4 * win + source, 4 * (win + win_step) + target))
    return lax.ppermute(value, ("win", "band", "half"), pairs)


def body(model_rhs, obs_rhs, model_var, obs_var, obs_weight, depth):
    rows, width = model_rhs.shape[2:]
    ranks = lax.axis_size("win") * lat_count()
    total_rows = rows * lat_count()
    offset = (GRID_ROWS - total_rows) // 2
    local_rows = lat_index() * rows - rows + jnp.arange(3 * rows, dtype=jnp.int32)
    latitude = -jnp.pi / 2 + (local_rows.astype(jnp.float32) + offset + 0.5) * (jnp.pi / GRID_ROWS)
    inside = ((local_rows >= 0) & (local_rows < total_rows)).astype(jnp.float32)
    spin = inside * (mass_rate * spin_rate * jnp.sin(latitude))
    inside = jnp.broadcast_to(inside[:, None], (3 * rows, 128))
    spin = jnp.broadcast_to(spin[:, None], (3 * rows, 128))
    fields = (3, rows, width)

    middle, outer = (1, 2), (0, 3)
    pair, straight = run(
        prep_kernel, [(6, rows, width), (7, rows, width)],
        model_rhs, obs_rhs, model_var, obs_var, obs_weight, depth,
        scratch=[pltpu.VMEM(model_rhs.shape, jnp.float32)] * 5 + [pltpu.SemaphoreType.DMA((6,))],
        space=pltpu.HBM,
    )
    came = shifted(straight, 1)
    depth_near = swapped(depth, 0)
    depth_edge = crossed(depth_near, outer, 1)
    relayed = swapped(jnp.concatenate([came[:1], depth_edge]), 0)
    held_pair, _ = lax.optimization_barrier((pair, depth_edge))
    pair_near, pair_far = swapped(held_pair, 0), crossed(pair, middle)
    known = (pair, pair_near, pair_far, came, relayed, spin, inside)
    state, back = run(first_adjoint_kernel, [fields, fields], *known)
    back = shifted(back, -1)
    state_far = crossed(state, middle)
    (tally,) = run(second_adjoint_kernel, [(2, rows, 128)], *known, state)
    state_near = swapped(state, 0)
    (end,) = run(forward_kernel, [fields], state, state_far, state_near, came, relayed, spin, inside)
    (sent,) = run(
        inner_kernel, [(ranks, 128)],
        model_rhs, obs_rhs, model_var, obs_var, obs_weight, back, end, tally,
    )
    gathered = lax.all_to_all(sent, ("win", "band", "half"), 0, 0, tiled=True)
    return run(
        combine_kernel, [model_rhs.shape] * 3,
        gathered, model_rhs, obs_rhs, model_var, obs_var, obs_weight, back,
    )


def solution(mesh):
    wins, lats = mesh.devices.shape
    mesh = Mesh(mesh.devices.reshape(wins, lats // 2, 2), ("win", "band", "half"))
    lat = ("band", "half")
    field = P("win", None, lat, None)
    in_specs = (field,) * 5 + (P("win", lat, None),)
    return jax.shard_map(body, mesh=mesh, in_specs=in_specs, out_specs=(field,) * 3, check_vma=False)
```

```python
import jax
import jax.numpy as jnp
from jax import lax
from jax.experimental import pallas as pl
from jax.experimental.pallas import tpu as pltpu
from jax.sharding import Mesh, PartitionSpec as P

GRID_ROWS = 768
STEPS = 4

mass_rate = 0.5
press_rate = 0.5
spin_rate = 0.4


def lon_gap(field):
    width = field.shape[-1]
    return pltpu.roll(field, width - 1, 1) - pltpu.roll(field, 1, 1)


def lat_gap(field):
    rows = field.shape[0]
    return pltpu.roll(field, rows - 1, 0) - pltpu.roll(field, 1, 0)


def even_lat():
    return lax.axis_index("half") == 0


def has_previous():
    return lax.axis_index("win") > 0


def stacked(own, near, far, index):
    even = even_lat()
    low = jnp.where(even, far[index], near[index])
    high = jnp.where(even, near[index], far[index])
    return jnp.concatenate([low, own[index], high], axis=0)


def prep_kernel(p, m, dvar, rvar, hobs, depth, pair, straight, pv, mv, dv, rv, hv, sems):
    copies = [
        pltpu.make_async_copy(source, target, sems.at[slot])
        for slot, (source, target) in enumerate(
            ((p, pv), (m, mv), (dvar, dv), (rvar, rv), (hobs, hv), (depth, straight.at[0:1]))
        )
    ]
    for copy in copies:
        copy.start()
    for copy in copies:
        copy.wait()
    for part in range(3):
        up = dv[0, part] * pv[0, part]
        seen = hv[0, part] * mv[0, part]
        pair[part] = pv[0, part]
        pair[3 + part] = up
        straight[1 + part] = pv[0, part] + seen
        straight[4 + part] = up + rv[0, part] * seen


def widened(tile, width):
    return jnp.concatenate([tile[...]] * (width // 128), axis=1)


def stretched(straight, relayed):
    even = even_lat()
    low = jnp.where(even, relayed[1], relayed[0])
    high = jnp.where(even, relayed[0], relayed[1])
    return 0.25 * jnp.concatenate([low, straight[0], high], axis=0)


def adjoint(pair, pair_near, pair_far, straight, relayed, spin, inside, base):
    depth = stretched(straight, relayed)
    turn, keep = widened(spin, depth.shape[1]), widened(inside, depth.shape[1])
    adj_height, adj_east, adj_north = [stacked(pair, pair_near, pair_far, base + part) for part in range(3)]
    for step in range(STEPS):
        adj_mid = adj_east - turn * adj_north
        adj_height = keep * (adj_height + 0.25 * (lat_gap(adj_north) + lon_gap(adj_mid)))
        adj_north = adj_north + turn * adj_mid + depth * lat_gap(adj_height)
        adj_east = adj_mid + depth * lon_gap(adj_height)
    rows = pair.shape[1]
    return [value[rows:2 * rows] for value in (adj_height, adj_east, adj_north)]


def first_adjoint_kernel(pair, pair_near, pair_far, straight, relayed, spin, inside, state, back):
    swept = adjoint(pair, pair_near, pair_far, straight, relayed, spin, inside, 0)
    link = has_previous()
    for part, value in enumerate(swept):
        back[part] = value
        state[part] = jnp.where(link, straight[1 + part] - value, 0.0)


def second_adjoint_kernel(pair, pair_near, pair_far, straight, relayed, spin, inside, state, tally):
    swept = adjoint(pair, pair_near, pair_far, straight, relayed, spin, inside, 3)
    link = has_previous()
    cross = square = 0.0
    for part, value in enumerate(swept):
        zx = jnp.where(link, straight[4 + part] - value, 0.0)
        cross += lane_sum(zx * state[part])
        square += lane_sum(zx * zx)
    tally[0] = cross
    tally[1] = square


def forward_kernel(state, state_far, state_near, straight, relayed, spin, inside, end):
    depth = stretched(straight, relayed)
    turn, keep = widened(spin, depth.shape[1]), widened(inside, depth.shape[1])
    height, east, north = [stacked(state, state_near, state_far, part) for part in range(3)]
    for step in range(STEPS):
        height = keep * (height - (lon_gap(depth * east) + lat_gap(depth * north)))
        east = east + turn * north - 0.25 * lon_gap(height)
        north = north - turn * east - 0.25 * lat_gap(height)
    rows = state.shape[1]
    for part, value in enumerate((height, east, north)):
        end[part] = value[rows:2 * rows]


def lane_sum(value):
    rows, width = value.shape
    total = value[:, :128]
    for start in range(128, width, 128):
        total = total + value[:, start:start + 128]
    return total


def inner_kernel(p, m, dvar, rvar, hobs, back, end, tally, sent):
    last = lax.axis_index("win") == lax.axis_size("win") - 1
    moments = [0.0, 0.0, 2.0 * tally[0], tally[1]]
    for part in range(3):
        dv, rv, hv = dvar[0, part], rvar[0, part], hobs[0, part]
        pv, mv = p[0, part], m[0, part]
        up, um = dv * pv, rv * mv
        ux = pv - back[part] + hv * mv
        zp = dv * up + ux - end[part]
        zm = rv * um + hv * ux
        zx = jnp.where(last, up + hv * um, 0.0)
        moments[0] += lane_sum(up * pv + um * mv)
        moments[1] += lane_sum(up * up + um * um + ux * ux)
        moments[2] += lane_sum(dv * up * up + rv * um * um + 2.0 * (zx * ux))
        moments[3] += lane_sum(zp * zp + zm * zm + zx * zx)
    lane = lax.broadcasted_iota(jnp.int32, (1, 128), 1)
    row = 0.0
    for slot, value in enumerate(moments):
        folded = jnp.sum(value, axis=0, keepdims=True)
        folded = folded + pltpu.roll(folded, 64, 1)
        folded = folded + pltpu.roll(folded, 32, 1)
        row = jnp.where(lane // 32 == slot, folded, row)
    sent[...] = jnp.broadcast_to(row, sent.shape)


def lane_sum(value):
    rows, width = value.shape
    total = value[:, :128]
    for start in range(128, width, 128):
        total = total + value[:, start:start + 128]
    return total


def two_sum(a, b):
    total = a + b
    part = total - a
    return total, (a - (total - part)) + (b - part)


def split(a):
    wide = 4097.0 * a
    top = wide - (wide - a)
    return top, a - top


def two_product(a, b):
    product = a * b
    a_top, a_low = split(a)
    b_top, b_low = split(b)
    return product, ((a_top * b_top - product) + a_top * b_low + a_low * b_top) + a_low * b_low


def pair_product(a, b):
    product, rest = two_product(a[0], b[0])
    return product, rest + (a[0] * b[1] + a[1] * b[0])


def pair_gap(a, b):
    total, rest = two_sum(a[0], -b[0])
    return total + (rest + (a[1] - b[1]))


def coefficients(gathered):
    top = jnp.sum(gathered[...], axis=0, keepdims=True)
    low = jnp.zeros_like(top)
    shift = 1
    while shift < 32:
        top, rest = two_sum(top, pltpu.roll(top, shift, 1))
        low = low + pltpu.roll(low, shift, 1) + rest
        shift *= 2
    tops = [jnp.broadcast_to(top[:, lane:lane + 1], (1, 128)) for lane in range(31, 128, 32)]
    lows = [jnp.broadcast_to(low[:, lane:lane + 1], (1, 128)) for lane in range(31, 128, 32)]
    scale = 1.0 / tops[1]
    moments = []
    for value, rest in zip(tops, lows):
        product, error = two_product(value, scale)
        moments.append((product, error + rest * scale))
    m1, m2, m3, m4 = moments
    gap = pair_gap(pair_product(m2, m4), pair_product(m3, m3))
    y1 = pair_gap(pair_product(m1, m4), pair_product(m2, m3)) / gap
    y2 = pair_gap(pair_product(m2, m2), pair_product(m1, m3)) / gap
    return y1, y2


def combine_kernel(gathered, p, m, dvar, rvar, hobs, back, dual_model, dual_obs, increment):
    y1, y2 = coefficients(gathered)
    rows, width = p.shape[2:]
    y1 = jnp.broadcast_to(jnp.concatenate([y1] * (width // 128), axis=1), (rows, width))
    y2 = jnp.broadcast_to(jnp.concatenate([y2] * (width // 128), axis=1), (rows, width))
    for part in range(3):
        pv, mv = p[0, part], m[0, part]
        dual_model[0, part] = (y1 + y2 * dvar[0, part]) * pv
        dual_obs[0, part] = (y1 + y2 * rvar[0, part]) * mv
        increment[0, part] = y2 * (pv - back[part] + hobs[0, part] * mv)


def run(kernel, out_shapes, *operands, scratch=(), space=pltpu.VMEM, work=4):
    shapes = [jax.ShapeDtypeStruct(shape, jnp.float32) for shape in out_shapes]
    size = sum(4 * operand.size for operand in operands) + sum(4 * shape.size for shape in shapes)
    if space is not pltpu.VMEM:
        operands = [pltpu.with_memory_space_constraint(operand, space) for operand in operands]
    return pl.pallas_call(
        kernel,
        out_shape=shapes,
        in_specs=[pl.BlockSpec(memory_space=space)] * len(operands),
        out_specs=[pl.BlockSpec(memory_space=pltpu.VMEM)] * len(shapes),
        scratch_shapes=scratch,
        compiler_params=pltpu.CompilerParams(vmem_limit_bytes=32 * 1024 * 1024),
        cost_estimate=pl.CostEstimate(flops=work * size, bytes_accessed=size, transcendentals=0),
    )(*operands)


def shifted(value, step):
    count = lax.axis_size("win")
    initial, last = (max(0, -step), min(count, count - step))
    return lax.ppermute(value, "win", [(source, source + step) for source in range(initial, last)])


def lat_count():
    return lax.axis_size("band") * lax.axis_size("half")


def lat_index():
    return lax.axis_index("band") * lax.axis_size("half") + lax.axis_index("half")


def swapped(value, first):
    pairs = []
    for lat in range(first, lat_count() - 1, 2):
        pairs += [(lat, lat + 1), (lat + 1, lat)]
    return lax.ppermute(value, ("band", "half"), pairs)


def crossed(value, ends, win_step=0):
    wins = lax.axis_size("win")
    pairs = []
    for win in range(wins):
        for source, target in (ends, ends[::-1]):
            if 0 <= win + win_step < wins:
                pairs.append((4 * win + source, 4 * (win + win_step) + target))
    return lax.ppermute(value, ("win", "band", "half"), pairs)


def body(model_rhs, obs_rhs, model_var, obs_var, obs_weight, depth):
    rows, width = model_rhs.shape[2:]
    ranks = lax.axis_size("win") * lat_count()
    total_rows = rows * lat_count()
    offset = (GRID_ROWS - total_rows) // 2
    local_rows = lat_index() * rows - rows + jnp.arange(3 * rows, dtype=jnp.int32)
    latitude = -jnp.pi / 2 + (local_rows.astype(jnp.float32) + offset + 0.5) * (jnp.pi / GRID_ROWS)
    inside = ((local_rows >= 0) & (local_rows < total_rows)).astype(jnp.float32)
    spin = inside * (mass_rate * spin_rate * jnp.sin(latitude))
    inside = jnp.broadcast_to(inside[:, None], (3 * rows, 128))
    spin = jnp.broadcast_to(spin[:, None], (3 * rows, 128))
    fields = (3, rows, width)

    middle, outer = (1, 2), (0, 3)
    pair, straight = run(
        prep_kernel, [(6, rows, width), (7, rows, width)],
        model_rhs, obs_rhs, model_var, obs_var, obs_weight, depth,
        scratch=[pltpu.VMEM(model_rhs.shape, jnp.float32)] * 5 + [pltpu.SemaphoreType.DMA((6,))],
        space=pltpu.HBM,
    )
    depth_near = swapped(depth, 0)
    depth_edge = crossed(depth_near, outer, 1)
    pair, straight, _ = lax.optimization_barrier((pair, straight, depth_near))
    came = shifted(straight, 1)
    relayed = swapped(jnp.concatenate([came[:1], depth_edge]), 0)
    pair_near, pair_far = swapped(pair, 0), crossed(pair, middle)
    known = (pair, pair_near, pair_far, came, relayed, spin, inside)
    state, back = run(first_adjoint_kernel, [fields, fields], *known)
    back = shifted(back, -1)
    state_far = crossed(state, middle)
    (tally,) = run(second_adjoint_kernel, [(2, rows, 128)], *known, state)
    state_near = swapped(state, 0)
    (end,) = run(forward_kernel, [fields], state, state_far, state_near, came, relayed, spin, inside)
    (sent,) = run(
        inner_kernel, [(ranks, 128)],
        model_rhs, obs_rhs, model_var, obs_var, obs_weight, back, end, tally,
    )
    gathered = lax.all_to_all(sent, ("win", "band", "half"), 0, 0, tiled=True)
    return run(
        combine_kernel, [model_rhs.shape] * 3,
        gathered, model_rhs, obs_rhs, model_var, obs_var, obs_weight, back,
    )


def solution(mesh):
    wins, lats = mesh.devices.shape
    mesh = Mesh(mesh.devices.reshape(wins, lats // 2, 2), ("win", "band", "half"))
    lat = ("band", "half")
    field = P("win", None, lat, None)
    in_specs = (field,) * 5 + (P("win", lat, None),)
    return jax.shard_map(body, mesh=mesh, in_specs=in_specs, out_specs=(field,) * 3, check_vma=False)
```

```python
import jax
import jax.numpy as jnp
from jax import lax
from jax.experimental import pallas as pl
from jax.experimental.pallas import tpu as pltpu
from jax.sharding import Mesh, PartitionSpec as P

GRID_ROWS = 768
STEPS = 4

mass_rate = 0.5
press_rate = 0.5
spin_rate = 0.4


def lon_gap(field):
    width = field.shape[-1]
    return pltpu.roll(field, width - 1, 1) - pltpu.roll(field, 1, 1)


def lat_gap(field):
    rows = field.shape[0]
    return pltpu.roll(field, rows - 1, 0) - pltpu.roll(field, 1, 0)


def even_lat():
    return lax.axis_index("half") == 0


def has_previous():
    return lax.axis_index("win") > 0


def stacked(own, near, far, index):
    even = even_lat()
    low = jnp.where(even, far[index], near[index])
    high = jnp.where(even, near[index], far[index])
    return jnp.concatenate([low, own[index], high], axis=0)


def prep_kernel(p, m, dvar, rvar, hobs, depth, pair, straight, local, pv, mv, dv, rv, hv, sems):
    copies = [
        pltpu.make_async_copy(source, target, sems.at[slot])
        for slot, (source, target) in enumerate(
            ((p, pv), (m, mv), (dvar, dv), (rvar, rv), (hobs, hv), (depth, straight.at[0:1]))
        )
    ]
    for copy in copies:
        copy.start()
    for copy in copies:
        copy.wait()
    for part in range(3):
        up = dv[0, part] * pv[0, part]
        seen = hv[0, part] * mv[0, part]
        pair[part] = pv[0, part]
        pair[3 + part] = up
        straight[1 + part] = pv[0, part] + seen
        local[part] = up + rv[0, part] * seen


def widened(tile, width):
    return jnp.concatenate([tile[...]] * (width // 128), axis=1)


def stretched(straight, relayed):
    even = even_lat()
    low = jnp.where(even, relayed[1], relayed[0])
    high = jnp.where(even, relayed[0], relayed[1])
    return 0.25 * jnp.concatenate([low, straight[0], high], axis=0)


def adjoint(pair, pair_near, pair_far, straight, relayed, spin, inside, base):
    depth = stretched(straight, relayed)
    turn, keep = widened(spin, depth.shape[1]), widened(inside, depth.shape[1])
    adj_height, adj_east, adj_north = [stacked(pair, pair_near, pair_far, base + part) for part in range(3)]
    for step in range(STEPS):
        adj_mid = adj_east - turn * adj_north
        adj_height = keep * (adj_height + 0.25 * (lat_gap(adj_north) + lon_gap(adj_mid)))
        adj_north = adj_north + turn * adj_mid + depth * lat_gap(adj_height)
        adj_east = adj_mid + depth * lon_gap(adj_height)
    rows = pair.shape[1]
    return [value[rows:2 * rows] for value in (adj_height, adj_east, adj_north)]


def first_adjoint_kernel(pair, pair_near, pair_far, straight, relayed, spin, inside, state, back):
    swept = adjoint(pair, pair_near, pair_far, straight, relayed, spin, inside, 0)
    link = has_previous()
    for part, value in enumerate(swept):
        back[part] = value
        state[part] = jnp.where(link, straight[1 + part] - value, 0.0)


def second_adjoint_kernel(pair, pair_near, pair_far, straight, relayed, spin, inside, local, state, tally):
    swept = adjoint(pair, pair_near, pair_far, straight, relayed, spin, inside, 3)
    link = has_previous()
    cross = square = 0.0
    for part, value in enumerate(swept):
        zx = jnp.where(link, local[part] - value, 0.0)
        cross += lane_sum(zx * state[part])
        square += lane_sum(zx * zx)
    tally[0] = cross
    tally[1] = square


def forward_kernel(state, state_far, state_near, straight, relayed, spin, inside, end):
    depth = stretched(straight, relayed)
    turn, keep = widened(spin, depth.shape[1]), widened(inside, depth.shape[1])
    height, east, north = [stacked(state, state_near, state_far, part) for part in range(3)]
    for step in range(STEPS):
        height = keep * (height - (lon_gap(depth * east) + lat_gap(depth * north)))
        east = east + turn * north - 0.25 * lon_gap(height)
        north = north - turn * east - 0.25 * lat_gap(height)
    rows = state.shape[1]
    for part, value in enumerate((height, east, north)):
        end[part] = value[rows:2 * rows]


def lane_sum(value):
    rows, width = value.shape
    total = value[:, :128]
    for start in range(128, width, 128):
        total = total + value[:, start:start + 128]
    return total


def inner_kernel(p, m, dvar, rvar, hobs, back, end, tally, sent):
    last = lax.axis_index("win") == lax.axis_size("win") - 1
    moments = [0.0, 0.0, 2.0 * tally[0], tally[1]]
    for part in range(3):
        dv, rv, hv = dvar[0, part], rvar[0, part], hobs[0, part]
        pv, mv = p[0, part], m[0, part]
        up, um = dv * pv, rv * mv
        ux = pv - back[part] + hv * mv
        zp = dv * up + ux - end[part]
        zm = rv * um + hv * ux
        zx = jnp.where(last, up + hv * um, 0.0)
        moments[0] += lane_sum(up * pv + um * mv)
        moments[1] += lane_sum(up * up + um * um + ux * ux)
        moments[2] += lane_sum(dv * up * up + rv * um * um + 2.0 * (zx * ux))
        moments[3] += lane_sum(zp * zp + zm * zm + zx * zx)
    lane = lax.broadcasted_iota(jnp.int32, (1, 128), 1)
    row = 0.0
    for slot, value in enumerate(moments):
        folded = jnp.sum(value, axis=0, keepdims=True)
        folded = folded + pltpu.roll(folded, 64, 1)
        folded = folded + pltpu.roll(folded, 32, 1)
        row = jnp.where(lane // 32 == slot, folded, row)
    sent[...] = jnp.broadcast_to(row, sent.shape)


def lane_sum(value):
    rows, width = value.shape
    total = value[:, :128]
    for start in range(128, width, 128):
        total = total + value[:, start:start + 128]
    return total


def two_sum(a, b):
    total = a + b
    part = total - a
    return total, (a - (total - part)) + (b - part)


def split(a):
    wide = 4097.0 * a
    top = wide - (wide - a)
    return top, a - top


def two_product(a, b):
    product = a * b
    a_top, a_low = split(a)
    b_top, b_low = split(b)
    return product, ((a_top * b_top - product) + a_top * b_low + a_low * b_top) + a_low * b_low


def pair_product(a, b):
    product, rest = two_product(a[0], b[0])
    return product, rest + (a[0] * b[1] + a[1] * b[0])


def pair_gap(a, b):
    total, rest = two_sum(a[0], -b[0])
    return total + (rest + (a[1] - b[1]))


def coefficients(gathered):
    top = jnp.sum(gathered[...], axis=0, keepdims=True)
    low = jnp.zeros_like(top)
    shift = 1
    while shift < 32:
        top, rest = two_sum(top, pltpu.roll(top, shift, 1))
        low = low + pltpu.roll(low, shift, 1) + rest
        shift *= 2
    tops = [jnp.broadcast_to(top[:, lane:lane + 1], (1, 128)) for lane in range(31, 128, 32)]
    lows = [jnp.broadcast_to(low[:, lane:lane + 1], (1, 128)) for lane in range(31, 128, 32)]
    scale = 1.0 / tops[1]
    moments = []
    for value, rest in zip(tops, lows):
        product, error = two_product(value, scale)
        moments.append((product, error + rest * scale))
    m1, m2, m3, m4 = moments
    gap = pair_gap(pair_product(m2, m4), pair_product(m3, m3))
    y1 = pair_gap(pair_product(m1, m4), pair_product(m2, m3)) / gap
    y2 = pair_gap(pair_product(m2, m2), pair_product(m1, m3)) / gap
    return y1, y2


def combine_kernel(gathered, p, m, dvar, rvar, hobs, back, dual_model, dual_obs, increment):
    y1, y2 = coefficients(gathered)
    rows, width = p.shape[2:]
    y1 = jnp.broadcast_to(jnp.concatenate([y1] * (width // 128), axis=1), (rows, width))
    y2 = jnp.broadcast_to(jnp.concatenate([y2] * (width // 128), axis=1), (rows, width))
    for part in range(3):
        pv, mv = p[0, part], m[0, part]
        dual_model[0, part] = (y1 + y2 * dvar[0, part]) * pv
        dual_obs[0, part] = (y1 + y2 * rvar[0, part]) * mv
        increment[0, part] = y2 * (pv - back[part] + hobs[0, part] * mv)


def run(kernel, out_shapes, *operands, scratch=(), space=pltpu.VMEM, work=4):
    shapes = [jax.ShapeDtypeStruct(shape, jnp.float32) for shape in out_shapes]
    size = sum(4 * operand.size for operand in operands) + sum(4 * shape.size for shape in shapes)
    if space is not pltpu.VMEM:
        operands = [pltpu.with_memory_space_constraint(operand, space) for operand in operands]
    return pl.pallas_call(
        kernel,
        out_shape=shapes,
        in_specs=[pl.BlockSpec(memory_space=space)] * len(operands),
        out_specs=[pl.BlockSpec(memory_space=pltpu.VMEM)] * len(shapes),
        scratch_shapes=scratch,
        compiler_params=pltpu.CompilerParams(vmem_limit_bytes=32 * 1024 * 1024),
        cost_estimate=pl.CostEstimate(flops=work * size // 4, bytes_accessed=work * size // 4, transcendentals=0),
    )(*operands)


def shifted(value, step):
    count = lax.axis_size("win")
    initial, last = (max(0, -step), min(count, count - step))
    return lax.ppermute(value, "win", [(source, source + step) for source in range(initial, last)])


def lat_count():
    return lax.axis_size("band") * lax.axis_size("half")


def lat_index():
    return lax.axis_index("band") * lax.axis_size("half") + lax.axis_index("half")


def swapped(value, first):
    pairs = []
    for lat in range(first, lat_count() - 1, 2):
        pairs += [(lat, lat + 1), (lat + 1, lat)]
    return lax.ppermute(value, ("band", "half"), pairs)


def crossed(value, ends, win_step=0):
    wins = lax.axis_size("win")
    pairs = []
    for win in range(wins):
        for source, target in (ends, ends[::-1]):
            if 0 <= win + win_step < wins:
                pairs.append((4 * win + source, 4 * (win + win_step) + target))
    return lax.ppermute(value, ("win", "band", "half"), pairs)


def body(model_rhs, obs_rhs, model_var, obs_var, obs_weight, depth):
    rows, width = model_rhs.shape[2:]
    ranks = lax.axis_size("win") * lat_count()
    total_rows = rows * lat_count()
    offset = (GRID_ROWS - total_rows) // 2
    local_rows = lat_index() * rows - rows + jnp.arange(3 * rows, dtype=jnp.int32)
    latitude = -jnp.pi / 2 + (local_rows.astype(jnp.float32) + offset + 0.5) * (jnp.pi / GRID_ROWS)
    inside = ((local_rows >= 0) & (local_rows < total_rows)).astype(jnp.float32)
    spin = inside * (mass_rate * spin_rate * jnp.sin(latitude))
    inside = jnp.broadcast_to(inside[:, None], (3 * rows, 128))
    spin = jnp.broadcast_to(spin[:, None], (3 * rows, 128))
    fields = (3, rows, width)

    middle, outer = (1, 2), (0, 3)
    pair, straight, local = run(
        prep_kernel, [(6, rows, width), (4, rows, width), fields],
        model_rhs, obs_rhs, model_var, obs_var, obs_weight, depth,
        scratch=[pltpu.VMEM(model_rhs.shape, jnp.float32)] * 5 + [pltpu.SemaphoreType.DMA((6,))],
        space=pltpu.HBM,
    )
    depth_near = swapped(depth, 0)
    depth_edge = crossed(depth_near, outer, 1)
    pair, straight, local, _ = lax.optimization_barrier((pair, straight, local, depth_near))
    came = shifted(straight, 1)
    relayed = swapped(jnp.concatenate([came[:1], depth_edge]), 0)
    pair_near, pair_far = swapped(pair, 0), crossed(pair, middle)
    known = (pair, pair_near, pair_far, came, relayed, spin, inside)
    local = shifted(local, 1)
    state, back = run(first_adjoint_kernel, [fields, fields], *known, work=4)
    state, back, local = lax.optimization_barrier((state, back, local))
    back = shifted(back, -1)
    state_far = crossed(state, middle)
    (tally,) = run(second_adjoint_kernel, [(2, rows, 128)], *known, local, state)
    state_near = swapped(state, 0)
    (end,) = run(forward_kernel, [fields], state, state_far, state_near, came, relayed, spin, inside)
    (sent,) = run(
        inner_kernel, [(ranks, 128)],
        model_rhs, obs_rhs, model_var, obs_var, obs_weight, back, end, tally,
    )
    gathered = lax.all_to_all(sent, ("win", "band", "half"), 0, 0, tiled=True)
    return run(
        combine_kernel, [model_rhs.shape] * 3,
        gathered, model_rhs, obs_rhs, model_var, obs_var, obs_weight, back,
    )


def solution(mesh):
    wins, lats = mesh.devices.shape
    mesh = Mesh(mesh.devices.reshape(wins, lats // 2, 2), ("win", "band", "half"))
    lat = ("band", "half")
    field = P("win", None, lat, None)
    in_specs = (field,) * 5 + (P("win", lat, None),)
    return jax.shard_map(body, mesh=mesh, in_specs=in_specs, out_specs=(field,) * 3, check_vma=False)
```

```python
import jax
import jax.numpy as jnp
from jax import lax
from jax.experimental import pallas as pl
from jax.experimental.pallas import tpu as pltpu
from jax.sharding import Mesh, PartitionSpec as P

GRID_ROWS = 768
STEPS = 4

mass_rate = 0.5
press_rate = 0.5
spin_rate = 0.4


def lon_gap(field):
    width = field.shape[-1]
    return pltpu.roll(field, width - 1, 1) - pltpu.roll(field, 1, 1)


def lat_gap(field):
    rows = field.shape[0]
    return pltpu.roll(field, rows - 1, 0) - pltpu.roll(field, 1, 0)


def even_lat():
    return lax.axis_index("half") == 0


def has_previous():
    return lax.axis_index("win") > 0


def stacked(own, near, far, index):
    even = even_lat()
    low = jnp.where(even, far[index], near[index])
    high = jnp.where(even, near[index], far[index])
    return jnp.concatenate([low, own[index], high], axis=0)


def prep_kernel(p, m, dvar, rvar, hobs, depth, pair, straight, local, pv, mv, dv, rv, hv, sems):
    copies = [
        pltpu.make_async_copy(source, target, sems.at[slot])
        for slot, (source, target) in enumerate(
            ((p, pv), (m, mv), (dvar, dv), (rvar, rv), (hobs, hv), (depth, straight.at[0:1]))
        )
    ]
    for copy in copies:
        copy.start()
    for copy in copies:
        copy.wait()
    for part in range(3):
        up = dv[0, part] * pv[0, part]
        seen = hv[0, part] * mv[0, part]
        pair[part] = pv[0, part]
        pair[3 + part] = up
        straight[1 + part] = pv[0, part] + seen
        local[part] = up + rv[0, part] * seen


def widened(tile, width):
    return jnp.concatenate([tile[...]] * (width // 128), axis=1)


def stretched(straight, relayed):
    even = even_lat()
    low = jnp.where(even, relayed[1], relayed[0])
    high = jnp.where(even, relayed[0], relayed[1])
    return 0.25 * jnp.concatenate([low, straight[0], high], axis=0)


def adjoint(pair, pair_near, pair_far, straight, relayed, spin, inside, base):
    depth = stretched(straight, relayed)
    turn, keep = widened(spin, depth.shape[1]), widened(inside, depth.shape[1])
    adj_height, adj_east, adj_north = [stacked(pair, pair_near, pair_far, base + part) for part in range(3)]
    for step in range(STEPS):
        adj_mid = adj_east - turn * adj_north
        adj_height = keep * (adj_height + 0.25 * (lat_gap(adj_north) + lon_gap(adj_mid)))
        adj_north = adj_north + turn * adj_mid + depth * lat_gap(adj_height)
        adj_east = adj_mid + depth * lon_gap(adj_height)
    rows = pair.shape[1]
    return [value[rows:2 * rows] for value in (adj_height, adj_east, adj_north)]


def first_adjoint_kernel(pair, pair_near, pair_far, straight, relayed, spin, inside, state, back):
    swept = adjoint(pair, pair_near, pair_far, straight, relayed, spin, inside, 0)
    link = has_previous()
    for part, value in enumerate(swept):
        back[part] = value
        state[part] = jnp.where(link, straight[1 + part] - value, 0.0)


def second_adjoint_kernel(pair, pair_near, pair_far, straight, relayed, spin, inside, local, state, tally):
    swept = adjoint(pair, pair_near, pair_far, straight, relayed, spin, inside, 3)
    link = has_previous()
    cross = square = 0.0
    for part, value in enumerate(swept):
        zx = jnp.where(link, local[part] - value, 0.0)
        cross += lane_sum(zx * state[part])
        square += lane_sum(zx * zx)
    tally[0] = cross
    tally[1] = square


def forward_kernel(state, state_far, state_near, straight, relayed, spin, inside, end):
    depth = stretched(straight, relayed)
    turn, keep = widened(spin, depth.shape[1]), widened(inside, depth.shape[1])
    height, east, north = [stacked(state, state_near, state_far, part) for part in range(3)]
    for step in range(STEPS):
        height = keep * (height - (lon_gap(depth * east) + lat_gap(depth * north)))
        east = east + turn * north - 0.25 * lon_gap(height)
        north = north - turn * east - 0.25 * lat_gap(height)
    rows = state.shape[1]
    for part, value in enumerate((height, east, north)):
        end[part] = value[rows:2 * rows]


def lane_sum(value):
    rows, width = value.shape
    total = value[:, :128]
    for start in range(128, width, 128):
        total = total + value[:, start:start + 128]
    return total


def inner_kernel(p, m, dvar, rvar, hobs, back, end, tally, sent):
    last = lax.axis_index("win") == lax.axis_size("win") - 1
    moments = [0.0, 0.0, 2.0 * tally[0], tally[1]]
    for part in range(3):
        dv, rv, hv = dvar[0, part], rvar[0, part], hobs[0, part]
        pv, mv = p[0, part], m[0, part]
        up, um = dv * pv, rv * mv
        ux = pv - back[part] + hv * mv
        zp = dv * up + ux - end[part]
        zm = rv * um + hv * ux
        zx = jnp.where(last, up + hv * um, 0.0)
        moments[0] += lane_sum(up * pv + um * mv)
        moments[1] += lane_sum(up * up + um * um + ux * ux)
        moments[2] += lane_sum(dv * up * up + rv * um * um + 2.0 * (zx * ux))
        moments[3] += lane_sum(zp * zp + zm * zm + zx * zx)
    lane = lax.broadcasted_iota(jnp.int32, (1, 128), 1)
    row = 0.0
    for slot, value in enumerate(moments):
        folded = jnp.sum(value, axis=0, keepdims=True)
        folded = folded + pltpu.roll(folded, 64, 1)
        folded = folded + pltpu.roll(folded, 32, 1)
        row = jnp.where(lane // 32 == slot, folded, row)
    sent[...] = jnp.broadcast_to(row, sent.shape)


def lane_sum(value):
    rows, width = value.shape
    total = value[:, :128]
    for start in range(128, width, 128):
        total = total + value[:, start:start + 128]
    return total


def two_sum(a, b):
    total = a + b
    part = total - a
    return total, (a - (total - part)) + (b - part)


def split(a):
    wide = 4097.0 * a
    top = wide - (wide - a)
    return top, a - top


def two_product(a, b):
    product = a * b
    a_top, a_low = split(a)
    b_top, b_low = split(b)
    return product, ((a_top * b_top - product) + a_top * b_low + a_low * b_top) + a_low * b_low


def pair_product(a, b):
    product, rest = two_product(a[0], b[0])
    return product, rest + (a[0] * b[1] + a[1] * b[0])


def pair_gap(a, b):
    total, rest = two_sum(a[0], -b[0])
    return total + (rest + (a[1] - b[1]))


def coefficients(gathered):
    top = jnp.sum(gathered[...], axis=0, keepdims=True)
    low = jnp.zeros_like(top)
    shift = 1
    while shift < 32:
        top, rest = two_sum(top, pltpu.roll(top, shift, 1))
        low = low + pltpu.roll(low, shift, 1) + rest
        shift *= 2
    tops = [jnp.broadcast_to(top[:, lane:lane + 1], (1, 128)) for lane in range(31, 128, 32)]
    lows = [jnp.broadcast_to(low[:, lane:lane + 1], (1, 128)) for lane in range(31, 128, 32)]
    scale = 1.0 / tops[1]
    moments = []
    for value, rest in zip(tops, lows):
        product, error = two_product(value, scale)
        moments.append((product, error + rest * scale))
    m1, m2, m3, m4 = moments
    gap = pair_gap(pair_product(m2, m4), pair_product(m3, m3))
    y1 = pair_gap(pair_product(m1, m4), pair_product(m2, m3)) / gap
    y2 = pair_gap(pair_product(m2, m2), pair_product(m1, m3)) / gap
    return y1, y2


def combine_kernel(gathered, p, m, dvar, rvar, hobs, back, dual_model, dual_obs, increment):
    y1, y2 = coefficients(gathered)
    rows, width = p.shape[2:]
    y1 = jnp.broadcast_to(jnp.concatenate([y1] * (width // 128), axis=1), (rows, width))
    y2 = jnp.broadcast_to(jnp.concatenate([y2] * (width // 128), axis=1), (rows, width))
    for part in range(3):
        pv, mv = p[0, part], m[0, part]
        dual_model[0, part] = (y1 + y2 * dvar[0, part]) * pv
        dual_obs[0, part] = (y1 + y2 * rvar[0, part]) * mv
        increment[0, part] = y2 * (pv - back[part] + hobs[0, part] * mv)


def run(kernel, out_shapes, *operands, scratch=(), space=pltpu.VMEM, work=4):
    shapes = [jax.ShapeDtypeStruct(shape, jnp.float32) for shape in out_shapes]
    size = sum(4 * operand.size for operand in operands) + sum(4 * shape.size for shape in shapes)
    if space is not pltpu.VMEM:
        operands = [pltpu.with_memory_space_constraint(operand, space) for operand in operands]
    return pl.pallas_call(
        kernel,
        out_shape=shapes,
        in_specs=[pl.BlockSpec(memory_space=space)] * len(operands),
        out_specs=[pl.BlockSpec(memory_space=pltpu.VMEM)] * len(shapes),
        scratch_shapes=scratch,
        compiler_params=pltpu.CompilerParams(vmem_limit_bytes=32 * 1024 * 1024),
        cost_estimate=pl.CostEstimate(flops=work * size // 4, bytes_accessed=work * size // 4, transcendentals=0),
    )(*operands)


def shifted(value, step):
    count = lax.axis_size("win")
    initial, last = (max(0, -step), min(count, count - step))
    return lax.ppermute(value, "win", [(source, source + step) for source in range(initial, last)])


def lat_count():
    return lax.axis_size("band") * lax.axis_size("half")


def lat_index():
    return lax.axis_index("band") * lax.axis_size("half") + lax.axis_index("half")


def swapped(value, first):
    pairs = []
    for lat in range(first, lat_count() - 1, 2):
        pairs += [(lat, lat + 1), (lat + 1, lat)]
    return lax.ppermute(value, ("band", "half"), pairs)


def crossed(value, ends, win_step=0):
    wins = lax.axis_size("win")
    pairs = []
    for win in range(wins):
        for source, target in (ends, ends[::-1]):
            if 0 <= win + win_step < wins:
                pairs.append((4 * win + source, 4 * (win + win_step) + target))
    return lax.ppermute(value, ("win", "band", "half"), pairs)


def body(model_rhs, obs_rhs, model_var, obs_var, obs_weight, depth):
    rows, width = model_rhs.shape[2:]
    ranks = lax.axis_size("win") * lat_count()
    total_rows = rows * lat_count()
    offset = (GRID_ROWS - total_rows) // 2
    local_rows = lat_index() * rows - rows + jnp.arange(3 * rows, dtype=jnp.int32)
    latitude = -jnp.pi / 2 + (local_rows.astype(jnp.float32) + offset + 0.5) * (jnp.pi / GRID_ROWS)
    inside = ((local_rows >= 0) & (local_rows < total_rows)).astype(jnp.float32)
    spin = inside * (mass_rate * spin_rate * jnp.sin(latitude))
    inside = jnp.broadcast_to(inside[:, None], (3 * rows, 128))
    spin = jnp.broadcast_to(spin[:, None], (3 * rows, 128))
    fields = (3, rows, width)

    middle, outer = (1, 2), (0, 3)
    pair, straight, local = run(
        prep_kernel, [(6, rows, width), (4, rows, width), fields],
        model_rhs, obs_rhs, model_var, obs_var, obs_weight, depth,
        scratch=[pltpu.VMEM(model_rhs.shape, jnp.float32)] * 5 + [pltpu.SemaphoreType.DMA((6,))],
        space=pltpu.HBM,
    )
    depth_near = swapped(depth, 0)
    depth_edge = crossed(depth_near, outer, 1)
    pair, straight, local, _ = lax.optimization_barrier((pair, straight, local, depth_near))
    came = shifted(straight, 1)
    relayed = swapped(jnp.concatenate([came[:1], depth_edge]), 0)
    pair_near, pair_far = swapped(pair, 0), crossed(pair, middle)
    known = (pair, pair_near, pair_far, came, relayed, spin, inside)
    local = shifted(local, 1)
    state, back = run(first_adjoint_kernel, [fields, fields], *known, work=4)
    back, local = lax.optimization_barrier((back, local))
    back = shifted(back, -1)
    state_far = crossed(state, middle)
    (tally,) = run(second_adjoint_kernel, [(2, rows, 128)], *known, local, state)
    state_near = swapped(state, 0)
    (end,) = run(forward_kernel, [fields], state, state_far, state_near, came, relayed, spin, inside)
    (sent,) = run(
        inner_kernel, [(ranks, 128)],
        model_rhs, obs_rhs, model_var, obs_var, obs_weight, back, end, tally,
    )
    gathered = lax.all_to_all(sent, ("win", "band", "half"), 0, 0, tiled=True)
    return run(
        combine_kernel, [model_rhs.shape] * 3,
        gathered, model_rhs, obs_rhs, model_var, obs_var, obs_weight, back,
    )


def solution(mesh):
    wins, lats = mesh.devices.shape
    mesh = Mesh(mesh.devices.reshape(wins, lats // 2, 2), ("win", "band", "half"))
    lat = ("band", "half")
    field = P("win", None, lat, None)
    in_specs = (field,) * 5 + (P("win", lat, None),)
    return jax.shard_map(body, mesh=mesh, in_specs=in_specs, out_specs=(field,) * 3, check_vma=False)
```

```python
import jax
import jax.numpy as jnp
from jax import lax
from jax.experimental import pallas as pl
from jax.experimental.pallas import tpu as pltpu
from jax.sharding import Mesh, PartitionSpec as P

GRID_ROWS = 768
STEPS = 4

mass_rate = 0.5
press_rate = 0.5
spin_rate = 0.4


def lon_gap(field):
    width = field.shape[-1]
    return pltpu.roll(field, width - 1, 1) - pltpu.roll(field, 1, 1)


def lat_gap(field):
    rows = field.shape[0]
    return pltpu.roll(field, rows - 1, 0) - pltpu.roll(field, 1, 0)


def even_lat():
    return lax.axis_index("half") == 0


def has_previous():
    return lax.axis_index("win") > 0


def stacked(own, near, far, index):
    even = even_lat()
    low = jnp.where(even, far[index], near[index])
    high = jnp.where(even, near[index], far[index])
    return jnp.concatenate([low, own[index], high], axis=0)


def prep_kernel(p, m, dvar, rvar, hobs, depth, pair, straight, local, pv, mv, dv, rv, hv, sems):
    copies = [
        pltpu.make_async_copy(source, target, sems.at[slot])
        for slot, (source, target) in enumerate(
            ((p, pv), (m, mv), (dvar, dv), (rvar, rv), (hobs, hv), (depth, straight.at[0:1]))
        )
    ]
    for copy in copies:
        copy.start()
    for copy in copies:
        copy.wait()
    for part in range(3):
        up = dv[0, part] * pv[0, part]
        seen = hv[0, part] * mv[0, part]
        pair[part] = pv[0, part]
        pair[3 + part] = up
        straight[1 + part] = pv[0, part] + seen
        local[part] = up + rv[0, part] * seen


def widened(tile, width):
    return jnp.concatenate([tile[...]] * (width // 128), axis=1)


def stretched(straight, relayed):
    even = even_lat()
    low = jnp.where(even, relayed[1], relayed[0])
    high = jnp.where(even, relayed[0], relayed[1])
    return 0.25 * jnp.concatenate([low, straight[0], high], axis=0)


def adjoint(pair, pair_near, pair_far, straight, relayed, spin, inside, base):
    depth = stretched(straight, relayed)
    turn, keep = widened(spin, depth.shape[1]), widened(inside, depth.shape[1])
    adj_height, adj_east, adj_north = [stacked(pair, pair_near, pair_far, base + part) for part in range(3)]
    for step in range(STEPS):
        adj_mid = adj_east - turn * adj_north
        adj_height = keep * (adj_height + 0.25 * (lat_gap(adj_north) + lon_gap(adj_mid)))
        adj_north = adj_north + turn * adj_mid + depth * lat_gap(adj_height)
        adj_east = adj_mid + depth * lon_gap(adj_height)
    rows = pair.shape[1]
    return [value[rows:2 * rows] for value in (adj_height, adj_east, adj_north)]


def first_adjoint_kernel(pair, pair_near, pair_far, straight, relayed, spin, inside, state, back):
    swept = adjoint(pair, pair_near, pair_far, straight, relayed, spin, inside, 0)
    link = has_previous()
    for part, value in enumerate(swept):
        back[part] = value
        state[part] = jnp.where(link, straight[1 + part] - value, 0.0)


def second_adjoint_kernel(pair, pair_near, pair_far, straight, relayed, spin, inside, local, state, tally):
    swept = adjoint(pair, pair_near, pair_far, straight, relayed, spin, inside, 3)
    link = has_previous()
    cross = square = 0.0
    for part, value in enumerate(swept):
        zx = jnp.where(link, local[part] - value, 0.0)
        cross += lane_sum(zx * state[part])
        square += lane_sum(zx * zx)
    tally[0] = cross
    tally[1] = square


def lane_sum(value):
    rows, width = value.shape
    total = value[:, :128]
    for start in range(128, width, 128):
        total = total + value[:, start:start + 128]
    return total


def home_kernel(p, m, dvar, rvar, hobs, tally, back, lead, sums):
    last = lax.axis_index("win") == lax.axis_size("win") - 1
    moments = [0.0, 0.0, 2.0 * tally[0], tally[1]]
    for part in range(3):
        dv, rv, hv = dvar[0, part], rvar[0, part], hobs[0, part]
        pv, mv = p[0, part], m[0, part]
        up, um = dv * pv, rv * mv
        ux = pv - back[part] + hv * mv
        lead[part] = dv * up + ux
        zm = rv * um + hv * ux
        zx = jnp.where(last, up + hv * um, 0.0)
        moments[0] += lane_sum(up * pv + um * mv)
        moments[1] += lane_sum(up * up + um * um + ux * ux)
        moments[2] += lane_sum(dv * up * up + rv * um * um + 2.0 * (zx * ux))
        moments[3] += lane_sum(zm * zm + zx * zx)
    for row, value in enumerate(moments):
        sums[row] = value


def closing_kernel(state_far, state_near, straight, relayed, spin, inside, state, lead, sums, sent):
    depth = stretched(straight, relayed)
    turn, keep = widened(spin, depth.shape[1]), widened(inside, depth.shape[1])
    height, east, north = [stacked(state, state_near, state_far, part) for part in range(3)]
    for step in range(STEPS):
        height = keep * (height - (lon_gap(depth * east) + lat_gap(depth * north)))
        east = east + turn * north - 0.25 * lon_gap(height)
        north = north - turn * east - 0.25 * lat_gap(height)
    rows = state.shape[1]
    square = 0.0
    for part, value in enumerate((height, east, north)):
        zp = lead[part] - value[rows:2 * rows]
        square += lane_sum(zp * zp)
    moments = [sums[0], sums[1], sums[2], sums[3] + square]
    lane = lax.broadcasted_iota(jnp.int32, (1, 128), 1)
    row = 0.0
    for slot, value in enumerate(moments):
        folded = jnp.sum(value, axis=0, keepdims=True)
        folded = folded + pltpu.roll(folded, 64, 1)
        folded = folded + pltpu.roll(folded, 32, 1)
        row = jnp.where(lane // 32 == slot, folded, row)
    sent[...] = jnp.broadcast_to(row, sent.shape)


def lane_sum(value):
    rows, width = value.shape
    total = value[:, :128]
    for start in range(128, width, 128):
        total = total + value[:, start:start + 128]
    return total


def two_sum(a, b):
    total = a + b
    part = total - a
    return total, (a - (total - part)) + (b - part)


def split(a):
    wide = 4097.0 * a
    top = wide - (wide - a)
    return top, a - top


def two_product(a, b):
    product = a * b
    a_top, a_low = split(a)
    b_top, b_low = split(b)
    return product, ((a_top * b_top - product) + a_top * b_low + a_low * b_top) + a_low * b_low


def pair_product(a, b):
    product, rest = two_product(a[0], b[0])
    return product, rest + (a[0] * b[1] + a[1] * b[0])


def pair_gap(a, b):
    total, rest = two_sum(a[0], -b[0])
    return total + (rest + (a[1] - b[1]))


def coefficients(gathered):
    top = jnp.sum(gathered[...], axis=0, keepdims=True)
    low = jnp.zeros_like(top)
    shift = 1
    while shift < 32:
        top, rest = two_sum(top, pltpu.roll(top, shift, 1))
        low = low + pltpu.roll(low, shift, 1) + rest
        shift *= 2
    tops = [jnp.broadcast_to(top[:, lane:lane + 1], (1, 128)) for lane in range(31, 128, 32)]
    lows = [jnp.broadcast_to(low[:, lane:lane + 1], (1, 128)) for lane in range(31, 128, 32)]
    scale = 1.0 / tops[1]
    moments = []
    for value, rest in zip(tops, lows):
        product, error = two_product(value, scale)
        moments.append((product, error + rest * scale))
    m1, m2, m3, m4 = moments
    gap = pair_gap(pair_product(m2, m4), pair_product(m3, m3))
    y1 = pair_gap(pair_product(m1, m4), pair_product(m2, m3)) / gap
    y2 = pair_gap(pair_product(m2, m2), pair_product(m1, m3)) / gap
    return y1, y2


def combine_kernel(gathered, p, m, dvar, rvar, hobs, back, dual_model, dual_obs, increment):
    y1, y2 = coefficients(gathered)
    rows, width = p.shape[2:]
    y1 = jnp.broadcast_to(jnp.concatenate([y1] * (width // 128), axis=1), (rows, width))
    y2 = jnp.broadcast_to(jnp.concatenate([y2] * (width // 128), axis=1), (rows, width))
    for part in range(3):
        pv, mv = p[0, part], m[0, part]
        dual_model[0, part] = (y1 + y2 * dvar[0, part]) * pv
        dual_obs[0, part] = (y1 + y2 * rvar[0, part]) * mv
        increment[0, part] = y2 * (pv - back[part] + hobs[0, part] * mv)


def run(kernel, out_shapes, *operands, scratch=(), space=pltpu.VMEM, work=4):
    shapes = [jax.ShapeDtypeStruct(shape, jnp.float32) for shape in out_shapes]
    size = sum(4 * operand.size for operand in operands) + sum(4 * shape.size for shape in shapes)
    if space is not pltpu.VMEM:
        operands = [pltpu.with_memory_space_constraint(operand, space) for operand in operands]
    return pl.pallas_call(
        kernel,
        out_shape=shapes,
        in_specs=[pl.BlockSpec(memory_space=space)] * len(operands),
        out_specs=[pl.BlockSpec(memory_space=pltpu.VMEM)] * len(shapes),
        scratch_shapes=scratch,
        compiler_params=pltpu.CompilerParams(vmem_limit_bytes=32 * 1024 * 1024),
        cost_estimate=pl.CostEstimate(flops=work * size // 4, bytes_accessed=work * size // 4, transcendentals=0),
    )(*operands)


def shifted(value, step):
    count = lax.axis_size("win")
    initial, last = (max(0, -step), min(count, count - step))
    return lax.ppermute(value, "win", [(source, source + step) for source in range(initial, last)])


def lat_count():
    return lax.axis_size("band") * lax.axis_size("half")


def lat_index():
    return lax.axis_index("band") * lax.axis_size("half") + lax.axis_index("half")


def swapped(value, first):
    pairs = []
    for lat in range(first, lat_count() - 1, 2):
        pairs += [(lat, lat + 1), (lat + 1, lat)]
    return lax.ppermute(value, ("band", "half"), pairs)


def crossed(value, ends, win_step=0):
    wins = lax.axis_size("win")
    pairs = []
    for win in range(wins):
        for source, target in (ends, ends[::-1]):
            if 0 <= win + win_step < wins:
                pairs.append((4 * win + source, 4 * (win + win_step) + target))
    return lax.ppermute(value, ("win", "band", "half"), pairs)


def body(model_rhs, obs_rhs, model_var, obs_var, obs_weight, depth):
    rows, width = model_rhs.shape[2:]
    ranks = lax.axis_size("win") * lat_count()
    total_rows = rows * lat_count()
    offset = (GRID_ROWS - total_rows) // 2
    local_rows = lat_index() * rows - rows + jnp.arange(3 * rows, dtype=jnp.int32)
    latitude = -jnp.pi / 2 + (local_rows.astype(jnp.float32) + offset + 0.5) * (jnp.pi / GRID_ROWS)
    inside = ((local_rows >= 0) & (local_rows < total_rows)).astype(jnp.float32)
    spin = inside * (mass_rate * spin_rate * jnp.sin(latitude))
    inside = jnp.broadcast_to(inside[:, None], (3 * rows, 128))
    spin = jnp.broadcast_to(spin[:, None], (3 * rows, 128))
    fields = (3, rows, width)

    middle, outer = (1, 2), (0, 3)
    pair, straight, local = run(
        prep_kernel, [(6, rows, width), (4, rows, width), fields],
        model_rhs, obs_rhs, model_var, obs_var, obs_weight, depth,
        scratch=[pltpu.VMEM(model_rhs.shape, jnp.float32)] * 5 + [pltpu.SemaphoreType.DMA((6,))],
        space=pltpu.HBM,
    )
    depth_near = swapped(depth, 0)
    depth_edge = crossed(depth_near, outer, 1)
    pair, straight, local, _ = lax.optimization_barrier((pair, straight, local, depth_near))
    came = shifted(straight, 1)
    relayed = swapped(jnp.concatenate([came[:1], depth_edge]), 0)
    pair_near, pair_far = swapped(pair, 0), crossed(pair, middle)
    known = (pair, pair_near, pair_far, came, relayed, spin, inside)
    local = shifted(local, 1)
    state, back = run(first_adjoint_kernel, [fields, fields], *known, work=4)
    held_state, local = lax.optimization_barrier((state, local))
    back = shifted(back, -1)
    state_far = crossed(held_state, middle)
    (tally,) = run(second_adjoint_kernel, [(2, rows, 128)], *known, local, state)
    state_near = swapped(state, 0)
    lead, sums = run(
        home_kernel, [fields, (4, rows, 128)],
        model_rhs, obs_rhs, model_var, obs_var, obs_weight, tally, back,
    )
    (sent,) = run(closing_kernel, [(ranks, 128)], state_far, state_near, came, relayed, spin, inside, state, lead, sums)
    gathered = lax.all_to_all(sent, ("win", "band", "half"), 0, 0, tiled=True)
    return run(
        combine_kernel, [model_rhs.shape] * 3,
        gathered, model_rhs, obs_rhs, model_var, obs_var, obs_weight, back,
    )


def solution(mesh):
    wins, lats = mesh.devices.shape
    mesh = Mesh(mesh.devices.reshape(wins, lats // 2, 2), ("win", "band", "half"))
    lat = ("band", "half")
    field = P("win", None, lat, None)
    in_specs = (field,) * 5 + (P("win", lat, None),)
    return jax.shard_map(body, mesh=mesh, in_specs=in_specs, out_specs=(field,) * 3, check_vma=False)
```

```python
import jax
import jax.numpy as jnp
from jax import lax
from jax.experimental import pallas as pl
from jax.experimental.pallas import tpu as pltpu
from jax.sharding import Mesh, PartitionSpec as P

GRID_ROWS = 768
STEPS = 4

mass_rate = 0.5
press_rate = 0.5
spin_rate = 0.4


def lon_gap(field):
    width = field.shape[-1]
    return pltpu.roll(field, width - 1, 1) - pltpu.roll(field, 1, 1)


def lat_gap(field):
    rows = field.shape[0]
    return pltpu.roll(field, rows - 1, 0) - pltpu.roll(field, 1, 0)


def own_lat_gap(field, rows):
    above = jnp.concatenate([field[rows + 1:2 * rows], field[2 * rows:2 * rows + 1]], axis=0)
    below = jnp.concatenate([field[rows - 1:rows], field[rows:2 * rows - 1]], axis=0)
    return above - below


def even_lat():
    return lax.axis_index("half") == 0


def has_previous():
    return lax.axis_index("win") > 0


def stacked(own, near, far, index):
    even = even_lat()
    low = jnp.where(even, far[index], near[index])
    high = jnp.where(even, near[index], far[index])
    return jnp.concatenate([low, own[index], high], axis=0)


def prep_kernel(p, m, dvar, rvar, hobs, depth, pair, straight, local, pv, mv, dv, rv, hv, sems):
    copies = [
        pltpu.make_async_copy(source, target, sems.at[slot])
        for slot, (source, target) in enumerate(
            ((p, pv), (m, mv), (dvar, dv), (rvar, rv), (hobs, hv), (depth, straight.at[0:1]))
        )
    ]
    for copy in copies:
        copy.start()
    for copy in copies:
        copy.wait()
    for part in range(3):
        up = dv[0, part] * pv[0, part]
        seen = hv[0, part] * mv[0, part]
        pair[part] = pv[0, part]
        pair[3 + part] = up
        straight[1 + part] = pv[0, part] + seen
        local[part] = up + rv[0, part] * seen


def widened(tile, width):
    return jnp.concatenate([tile[...]] * (width // 128), axis=1)


def stretched(straight, relayed):
    even = even_lat()
    low = jnp.where(even, relayed[1], relayed[0])
    high = jnp.where(even, relayed[0], relayed[1])
    return 0.25 * jnp.concatenate([low, straight[0], high], axis=0)


def adjoint(pair, pair_far, pair_near, straight, relayed, spin, inside, base):
    depth = stretched(straight, relayed)
    turn, keep = widened(spin, depth.shape[1]), widened(inside, depth.shape[1])
    adj_height, adj_east, adj_north = [stacked(pair, pair_near, pair_far, base + part) for part in range(3)]
    rows = pair.shape[1]
    own = slice(rows, 2 * rows)
    for step in range(STEPS):
        adj_mid = adj_east - turn * adj_north
        adj_height = keep * (adj_height + 0.25 * (lat_gap(adj_north) + lon_gap(adj_mid)))
        if step < STEPS - 1:
            adj_north = adj_north + turn * adj_mid + depth * lat_gap(adj_height)
            adj_east = adj_mid + depth * lon_gap(adj_height)
    own_height, own_mid, own_depth = adj_height[own], adj_mid[own], depth[own]
    own_north = adj_north[own] + turn[own] * own_mid + own_depth * own_lat_gap(adj_height, rows)
    own_east = own_mid + own_depth * lon_gap(own_height)
    return own_height, own_east, own_north


def first_adjoint_kernel(pair, pair_far, pair_near, straight, relayed, spin, inside, state, back):
    swept = adjoint(pair, pair_far, pair_near, straight, relayed, spin, inside, 0)
    link = has_previous()
    for part, value in enumerate(swept):
        back[part] = value
        state[part] = jnp.where(link, straight[1 + part] - value, 0.0)


def second_adjoint_kernel(pair, pair_far, pair_near, straight, relayed, spin, inside, local, late, state, tally):
    swept = adjoint(pair, pair_far, pair_near, straight, relayed, spin, inside, 3)
    link = has_previous()
    cross = square = 0.0
    for part, value in enumerate(swept):
        zx = jnp.where(link, local[part] + late[part] - value, 0.0)
        cross += lane_sum(zx * state[part])
        square += lane_sum(zx * zx)
    tally[0] = cross
    tally[1] = square


def lane_sum(value):
    rows, width = value.shape
    total = value[:, :128]
    for start in range(128, width, 128):
        total = total + value[:, start:start + 128]
    return total


def home_kernel(p, m, dvar, rvar, hobs, tally, back, lead, sums):
    last = lax.axis_index("win") == lax.axis_size("win") - 1
    moments = [0.0, 0.0, 2.0 * tally[0], tally[1]]
    for part in range(3):
        dv, rv, hv = dvar[0, part], rvar[0, part], hobs[0, part]
        pv, mv = p[0, part], m[0, part]
        up, um = dv * pv, rv * mv
        ux = pv - back[part] + hv * mv
        lead[part] = dv * up + ux
        zm = rv * um + hv * ux
        zx = jnp.where(last, up + hv * um, 0.0)
        moments[0] += lane_sum(up * pv + um * mv)
        moments[1] += lane_sum(up * up + um * um + ux * ux)
        moments[2] += lane_sum(dv * up * up + rv * um * um + 2.0 * (zx * ux))
        moments[3] += lane_sum(zm * zm + zx * zx)
    for row, value in enumerate(moments):
        sums[row] = value


def closing_kernel(state_far, state_near, straight, relayed, spin, inside, state, lead, sums, sent):
    depth = stretched(straight, relayed)
    turn, keep = widened(spin, depth.shape[1]), widened(inside, depth.shape[1])
    height, east, north = [stacked(state, state_near, state_far, part) for part in range(3)]
    for step in range(STEPS):
        height = keep * (height - (lon_gap(depth * east) + lat_gap(depth * north)))
        if step < STEPS - 1:
            east = east + turn * north - 0.25 * lon_gap(height)
            north = north - turn * east - 0.25 * lat_gap(height)
    rows = state.shape[1]
    own = slice(rows, 2 * rows)
    own_height, own_turn, own_north = height[own], turn[own], north[own]
    own_east = east[own] + own_turn * own_north - 0.25 * lon_gap(own_height)
    own_north = own_north - own_turn * own_east - 0.25 * own_lat_gap(height, rows)
    square = 0.0
    for part, value in enumerate((own_height, own_east, own_north)):
        zp = lead[part] - value
        square += lane_sum(zp * zp)
    moments = [sums[0], sums[1], sums[2], sums[3] + square]
    lane = lax.broadcasted_iota(jnp.int32, (1, 128), 1)
    row = 0.0
    for slot, value in enumerate(moments):
        folded = jnp.sum(value, axis=0, keepdims=True)
        folded = folded + pltpu.roll(folded, 64, 1)
        folded = folded + pltpu.roll(folded, 32, 1)
        row = jnp.where(lane // 32 == slot, folded, row)
    sent[...] = jnp.broadcast_to(row, sent.shape)


def lane_sum(value):
    rows, width = value.shape
    total = value[:, :128]
    for start in range(128, width, 128):
        total = total + value[:, start:start + 128]
    return total


def two_sum(a, b):
    total = a + b
    part = total - a
    return total, (a - (total - part)) + (b - part)


def split(a):
    wide = 4097.0 * a
    top = wide - (wide - a)
    return top, a - top


def two_product(a, b):
    product = a * b
    a_top, a_low = split(a)
    b_top, b_low = split(b)
    return product, ((a_top * b_top - product) + a_top * b_low + a_low * b_top) + a_low * b_low


def pair_product(a, b):
    product, rest = two_product(a[0], b[0])
    return product, rest + (a[0] * b[1] + a[1] * b[0])


def pair_gap(a, b):
    total, rest = two_sum(a[0], -b[0])
    return total + (rest + (a[1] - b[1]))


def coefficients(gathered):
    top = jnp.sum(gathered[...], axis=0, keepdims=True)
    low = jnp.zeros_like(top)
    shift = 1
    while shift < 32:
        top, rest = two_sum(top, pltpu.roll(top, shift, 1))
        low = low + pltpu.roll(low, shift, 1) + rest
        shift *= 2
    tops = [jnp.broadcast_to(top[:, lane:lane + 1], (1, 128)) for lane in range(31, 128, 32)]
    lows = [jnp.broadcast_to(low[:, lane:lane + 1], (1, 128)) for lane in range(31, 128, 32)]
    scale = 1.0 / tops[1]
    moments = []
    for value, rest in zip(tops, lows):
        product, error = two_product(value, scale)
        moments.append((product, error + rest * scale))
    m1, m2, m3, m4 = moments
    gap = pair_gap(pair_product(m2, m4), pair_product(m3, m3))
    y1 = pair_gap(pair_product(m1, m4), pair_product(m2, m3)) / gap
    y2 = pair_gap(pair_product(m2, m2), pair_product(m1, m3)) / gap
    return y1, y2


def combine_kernel(gathered, p, m, dvar, rvar, hobs, back, dual_model, dual_obs, increment):
    y1, y2 = coefficients(gathered)
    rows, width = p.shape[2:]
    y1 = jnp.broadcast_to(jnp.concatenate([y1] * (width // 128), axis=1), (rows, width))
    y2 = jnp.broadcast_to(jnp.concatenate([y2] * (width // 128), axis=1), (rows, width))
    for part in range(3):
        pv, mv = p[0, part], m[0, part]
        dual_model[0, part] = (y1 + y2 * dvar[0, part]) * pv
        dual_obs[0, part] = (y1 + y2 * rvar[0, part]) * mv
        increment[0, part] = y2 * (pv - back[part] + hobs[0, part] * mv)


def run(kernel, out_shapes, *operands, scratch=(), space=pltpu.VMEM, work=4):
    shapes = [jax.ShapeDtypeStruct(shape, jnp.float32) for shape in out_shapes]
    size = sum(4 * operand.size for operand in operands) + sum(4 * shape.size for shape in shapes)
    if space is not pltpu.VMEM:
        operands = [pltpu.with_memory_space_constraint(operand, space) for operand in operands]
    return pl.pallas_call(
        kernel,
        out_shape=shapes,
        in_specs=[pl.BlockSpec(memory_space=space)] * len(operands),
        out_specs=[pl.BlockSpec(memory_space=pltpu.VMEM)] * len(shapes),
        scratch_shapes=scratch,
        compiler_params=pltpu.CompilerParams(vmem_limit_bytes=32 * 1024 * 1024),
        cost_estimate=pl.CostEstimate(flops=work * size // 4, bytes_accessed=work * size // 4, transcendentals=0),
    )(*operands)


def shifted(value, step, lats=(0, 1, 2, 3)):
    wins = lax.axis_size("win")
    pairs = []
    for win in range(max(0, -step), min(wins, wins - step)):
        for lat in lats:
            pairs.append((4 * win + lat, 4 * (win + step) + lat))
    return lax.ppermute(value, ("win", "band", "half"), pairs)


def lat_count():
    return lax.axis_size("band") * lax.axis_size("half")


def lat_index():
    return lax.axis_index("band") * lax.axis_size("half") + lax.axis_index("half")


def swapped(value, first):
    pairs = []
    for lat in range(first, lat_count() - 1, 2):
        pairs += [(lat, lat + 1), (lat + 1, lat)]
    return lax.ppermute(value, ("band", "half"), pairs)


def crossed(value, ends, win_step=0):
    wins = lax.axis_size("win")
    pairs = []
    for win in range(wins):
        for source, target in (ends, ends[::-1]):
            if 0 <= win + win_step < wins:
                pairs.append((4 * win + source, 4 * (win + win_step) + target))
    return lax.ppermute(value, ("win", "band", "half"), pairs)


def body(model_rhs, obs_rhs, model_var, obs_var, obs_weight, depth):
    rows, width = model_rhs.shape[2:]
    ranks = lax.axis_size("win") * lat_count()
    total_rows = rows * lat_count()
    offset = (GRID_ROWS - total_rows) // 2
    local_rows = lat_index() * rows - rows + lax.broadcasted_iota(jnp.int32, (3 * rows, 128), 0)
    latitude = -jnp.pi / 2 + (local_rows.astype(jnp.float32) + offset + 0.5) * (jnp.pi / GRID_ROWS)
    inside = ((local_rows >= 0) & (local_rows < total_rows)).astype(jnp.float32)
    spin = inside * (mass_rate * spin_rate * jnp.sin(latitude))
    fields = (3, rows, width)

    middle, outer = (1, 2), (0, 3)
    pair, straight, local = run(
        prep_kernel, [(6, rows, width), (4, rows, width), fields],
        model_rhs, obs_rhs, model_var, obs_var, obs_weight, depth,
        scratch=[pltpu.VMEM(model_rhs.shape, jnp.float32)] * 5 + [pltpu.SemaphoreType.DMA((6,))],
        space=pltpu.HBM,
    )
    depth_near = swapped(depth, 0)
    depth_edge = crossed(depth_near, outer, 1)
    pair, straight, local, _ = lax.optimization_barrier((pair, straight, local, depth_near))
    came = shifted(straight, 1)
    relayed = swapped(jnp.concatenate([came[:1], depth_edge]), 0)
    pair_near, pair_far = swapped(pair, 0), crossed(pair, middle)
    known = (pair, pair_far, pair_near, came, relayed, spin, inside)
    late, local = local, shifted(local, 1, middle)
    state, back = run(first_adjoint_kernel, [fields, fields], *known, work=4)
    held_state, local = lax.optimization_barrier((state, local))
    late, _ = lax.optimization_barrier((late, state))
    late = shifted(late, 1, outer)
    back = shifted(back, -1)
    state_far = crossed(held_state, middle)
    (tally,) = run(second_adjoint_kernel, [(2, rows, 128)], *known, local, late, state)
    state_near = swapped(state, 0)
    lead, sums = run(
        home_kernel, [fields, (4, rows, 128)],
        model_rhs, obs_rhs, model_var, obs_var, obs_weight, tally, back,
    )
    (sent,) = run(closing_kernel, [(ranks, 128)], state_far, state_near, came, relayed, spin, inside, state, lead, sums)
    gathered = lax.all_to_all(sent, ("win", "band", "half"), 0, 0, tiled=True)
    return run(
        combine_kernel, [model_rhs.shape] * 3,
        gathered, model_rhs, obs_rhs, model_var, obs_var, obs_weight, back,
    )


def solution(mesh):
    wins, lats = mesh.devices.shape
    mesh = Mesh(mesh.devices.reshape(wins, lats // 2, 2), ("win", "band", "half"))
    lat = ("band", "half")
    field = P("win", None, lat, None)
    in_specs = (field,) * 5 + (P("win", lat, None),)
    return jax.shard_map(body, mesh=mesh, in_specs=in_specs, out_specs=(field,) * 3, check_vma=False)
```

```python
import jax
import jax.numpy as jnp
from jax import lax
from jax.experimental import pallas as pl
from jax.experimental.pallas import tpu as pltpu
from jax.sharding import Mesh, PartitionSpec as P

GRID_ROWS = 768
STEPS = 4

mass_rate = 0.5
press_rate = 0.5
spin_rate = 0.4


def lon_gap(field):
    width = field.shape[-1]
    return pltpu.roll(field, width - 1, 1) - pltpu.roll(field, 1, 1)


def lat_gap(field):
    rows = field.shape[0]
    return pltpu.roll(field, rows - 1, 0) - pltpu.roll(field, 1, 0)


def even_lat():
    return lax.axis_index("half") == 0


def has_previous():
    return lax.axis_index("win") > 0


def stacked(own, near, far, index):
    even = even_lat()
    low = jnp.where(even, far[index], near[index])
    high = jnp.where(even, near[index], far[index])
    return jnp.concatenate([low, own[index], high], axis=0)


def prep_kernel(p, m, dvar, rvar, hobs, depth, pair, straight, local, pv, mv, dv, rv, hv, sems):
    copies = [
        pltpu.make_async_copy(source, target, sems.at[slot])
        for slot, (source, target) in enumerate(
            ((p, pv), (m, mv), (dvar, dv), (rvar, rv), (hobs, hv), (depth, straight.at[0:1]))
        )
    ]
    for copy in copies:
        copy.start()
    for copy in copies:
        copy.wait()
    for part in range(3):
        up = dv[0, part] * pv[0, part]
        seen = hv[0, part] * mv[0, part]
        pair[part] = pv[0, part]
        pair[3 + part] = up
        straight[1 + part] = pv[0, part] + seen
        local[part] = up + rv[0, part] * seen


def widened(tile, width):
    return jnp.concatenate([tile[...]] * (width // 128), axis=1)


def stretched(straight, relayed):
    even = even_lat()
    low = jnp.where(even, relayed[1], relayed[0])
    high = jnp.where(even, relayed[0], relayed[1])
    return 0.25 * jnp.concatenate([low, straight[0], high], axis=0)


def adjoint(pair, pair_near, pair_far, straight, relayed, spin, inside, base):
    depth = stretched(straight, relayed)
    turn, keep = widened(spin, depth.shape[1]), widened(inside, depth.shape[1])
    adj_height, adj_east, adj_north = [stacked(pair, pair_near, pair_far, base + part) for part in range(3)]
    for step in range(STEPS):
        adj_mid = adj_east - turn * adj_north
        adj_height = keep * (adj_height + 0.25 * (lat_gap(adj_north) + lon_gap(adj_mid)))
        adj_north = adj_north + turn * adj_mid + depth * lat_gap(adj_height)
        adj_east = adj_mid + depth * lon_gap(adj_height)
    rows = pair.shape[1]
    return [value[rows:2 * rows] for value in (adj_height, adj_east, adj_north)]


def first_adjoint_kernel(pair, pair_near, pair_far, straight, relayed, spin, inside, state, back):
    swept = adjoint(pair, pair_near, pair_far, straight, relayed, spin, inside, 0)
    link = has_previous()
    for part, value in enumerate(swept):
        back[part] = value
        state[part] = jnp.where(link, straight[1 + part] - value, 0.0)


def second_adjoint_kernel(pair, pair_near, pair_far, straight, relayed, spin, inside, local, state, tally):
    swept = adjoint(pair, pair_near, pair_far, straight, relayed, spin, inside, 3)
    link = has_previous()
    cross = square = 0.0
    for part, value in enumerate(swept):
        zx = jnp.where(link, local[part] - value, 0.0)
        cross += lane_sum(zx * state[part])
        square += lane_sum(zx * zx)
    tally[0] = cross
    tally[1] = square


def lane_sum(value):
    rows, width = value.shape
    total = value[:, :128]
    for start in range(128, width, 128):
        total = total + value[:, start:start + 128]
    return total


def home_kernel(p, m, dvar, rvar, hobs, tally, back, lead, sums):
    last = lax.axis_index("win") == lax.axis_size("win") - 1
    moments = [0.0, 0.0, 2.0 * tally[0], tally[1]]
    for part in range(3):
        dv, rv, hv = dvar[0, part], rvar[0, part], hobs[0, part]
        pv, mv = p[0, part], m[0, part]
        up, um = dv * pv, rv * mv
        ux = pv - back[part] + hv * mv
        lead[part] = dv * up + ux
        zm = rv * um + hv * ux
        zx = jnp.where(last, up + hv * um, 0.0)
        moments[0] += lane_sum(up * pv + um * mv)
        moments[1] += lane_sum(up * up + um * um + ux * ux)
        moments[2] += lane_sum(dv * up * up + rv * um * um + 2.0 * (zx * ux))
        moments[3] += lane_sum(zm * zm + zx * zx)
    for row, value in enumerate(moments):
        sums[row] = value


def forward(height, east, north, depth, turn, keep, gap):
    for step in range(STEPS):
        height = keep * (height - (lon_gap(depth * east) + gap(depth * north)))
        east = east + turn * north - 0.25 * lon_gap(height)
        north = north - turn * east - 0.25 * gap(height)
    return height, east, north


def inner_forward_kernel(state, state_near, straight, relayed, spin, inside, lead, rest):
    depth = stretched(straight, relayed)
    turn, keep = widened(spin, depth.shape[1]), widened(inside, depth.shape[1])
    even = even_lat()
    rows = state.shape[1]
    fields = []
    for part in range(3):
        low = jnp.where(even, 0.0, state_near[part])
        high = jnp.where(even, state_near[part], 0.0)
        fields.append(jnp.concatenate([low, state[part], high], axis=0))
    for part, value in enumerate(forward(*fields, depth, turn, keep, lat_gap)):
        rest[part] = lead[part] - value[rows:2 * rows]


def open_lat_gap(field):
    rows = field.shape[0]
    row = lax.broadcasted_iota(jnp.int32, field.shape, 0)
    above = jnp.where(row < rows - 1, pltpu.roll(field, rows - 1, 0), 0.0)
    below = jnp.where(row > 0, pltpu.roll(field, 1, 0), 0.0)
    return above - below


def closing_kernel(state_far, rest, straight, relayed, spin, inside, sums, sent, remainder):
    even = even_lat()
    rows, width = state_far.shape[1:]
    middle = lax.axis_index("band") != lax.axis_index("half")

    @pl.when(middle)
    def _():
        depth = jnp.where(
            even,
            jnp.concatenate([relayed[1], straight[0]], axis=0),
            jnp.concatenate([straight[0], relayed[1]], axis=0),
        )
        turn, keep = [
            jnp.where(even, factor[:2 * rows], factor[rows:])
            for factor in (widened(spin, width), widened(inside, width))
        ]
        empty = jnp.zeros((rows, width), jnp.float32)
        fields = [
            jnp.where(
                even,
                jnp.concatenate([state_far[part], empty], axis=0),
                jnp.concatenate([empty, state_far[part]], axis=0),
            )
            for part in range(3)
        ]
        for part, value in enumerate(forward(*fields, 0.25 * depth, turn, keep, open_lat_gap)):
            remainder[part] = rest[part] - jnp.where(even, value[rows:], value[:rows])

    @pl.when(jnp.logical_not(middle))
    def _():
        for part in range(3):
            remainder[part] = rest[part]

    square = 0.0
    for part in range(3):
        square += lane_sum(remainder[part] * remainder[part])
    moments = [sums[0], sums[1], sums[2], sums[3] + square]
    lane = lax.broadcasted_iota(jnp.int32, (1, 128), 1)
    row = 0.0
    for slot, value in enumerate(moments):
        folded = jnp.sum(value, axis=0, keepdims=True)
        folded = folded + pltpu.roll(folded, 64, 1)
        folded = folded + pltpu.roll(folded, 32, 1)
        row = jnp.where(lane // 32 == slot, folded, row)
    sent[...] = jnp.broadcast_to(row, sent.shape)


def lane_sum(value):
    rows, width = value.shape
    total = value[:, :128]
    for start in range(128, width, 128):
        total = total + value[:, start:start + 128]
    return total


def two_sum(a, b):
    total = a + b
    part = total - a
    return total, (a - (total - part)) + (b - part)


def split(a):
    wide = 4097.0 * a
    top = wide - (wide - a)
    return top, a - top


def two_product(a, b):
    product = a * b
    a_top, a_low = split(a)
    b_top, b_low = split(b)
    return product, ((a_top * b_top - product) + a_top * b_low + a_low * b_top) + a_low * b_low


def pair_product(a, b):
    product, rest = two_product(a[0], b[0])
    return product, rest + (a[0] * b[1] + a[1] * b[0])


def pair_gap(a, b):
    total, rest = two_sum(a[0], -b[0])
    return total + (rest + (a[1] - b[1]))


def coefficients(gathered):
    top = jnp.sum(gathered[...], axis=0, keepdims=True)
    low = jnp.zeros_like(top)
    shift = 1
    while shift < 32:
        top, rest = two_sum(top, pltpu.roll(top, shift, 1))
        low = low + pltpu.roll(low, shift, 1) + rest
        shift *= 2
    tops = [jnp.broadcast_to(top[:, lane:lane + 1], (1, 128)) for lane in range(31, 128, 32)]
    lows = [jnp.broadcast_to(low[:, lane:lane + 1], (1, 128)) for lane in range(31, 128, 32)]
    scale = 1.0 / tops[1]
    moments = []
    for value, rest in zip(tops, lows):
        product, error = two_product(value, scale)
        moments.append((product, error + rest * scale))
    m1, m2, m3, m4 = moments
    gap = pair_gap(pair_product(m2, m4), pair_product(m3, m3))
    y1 = pair_gap(pair_product(m1, m4), pair_product(m2, m3)) / gap
    y2 = pair_gap(pair_product(m2, m2), pair_product(m1, m3)) / gap
    return y1, y2


def combine_kernel(gathered, p, m, dvar, rvar, hobs, back, dual_model, dual_obs, increment, first, second, third, sems):
    y1, y2 = coefficients(gathered)
    rows, width = p.shape[2:]
    y1 = jnp.broadcast_to(jnp.concatenate([y1] * (width // 128), axis=1), (rows, width))
    y2 = jnp.broadcast_to(jnp.concatenate([y2] * (width // 128), axis=1), (rows, width))
    copies = [
        pltpu.make_async_copy(source, target, sems.at[slot])
        for slot, (source, target) in enumerate(((first, dual_model), (second, dual_obs), (third, increment)))
    ]
    for part in range(3):
        first[0, part] = (y1 + y2 * dvar[0, part]) * p[0, part]
    copies[0].start()
    for part in range(3):
        second[0, part] = (y1 + y2 * rvar[0, part]) * m[0, part]
    copies[1].start()
    for part in range(3):
        third[0, part] = y2 * (p[0, part] - back[part] + hobs[0, part] * m[0, part])
    copies[2].start()
    for copy in copies:
        copy.wait()


def run(kernel, out_shapes, *operands, scratch=(), space=pltpu.VMEM, target=pltpu.VMEM, work=4):
    shapes = [jax.ShapeDtypeStruct(shape, jnp.float32) for shape in out_shapes]
    size = sum(4 * operand.size for operand in operands) + sum(4 * shape.size for shape in shapes)
    if space is not pltpu.VMEM:
        operands = [pltpu.with_memory_space_constraint(operand, space) for operand in operands]
    return pl.pallas_call(
        kernel,
        out_shape=shapes,
        in_specs=[pl.BlockSpec(memory_space=space)] * len(operands),
        out_specs=[pl.BlockSpec(memory_space=target)] * len(shapes),
        scratch_shapes=scratch,
        compiler_params=pltpu.CompilerParams(vmem_limit_bytes=32 * 1024 * 1024),
        cost_estimate=pl.CostEstimate(flops=work * size // 4, bytes_accessed=work * size // 4, transcendentals=0),
    )(*operands)


def shifted(value, step):
    count = lax.axis_size("win")
    initial, last = (max(0, -step), min(count, count - step))
    return lax.ppermute(value, "win", [(source, source + step) for source in range(initial, last)])


def lat_count():
    return lax.axis_size("band") * lax.axis_size("half")


def lat_index():
    return lax.axis_index("band") * lax.axis_size("half") + lax.axis_index("half")


def swapped(value, first):
    pairs = []
    for lat in range(first, lat_count() - 1, 2):
        pairs += [(lat, lat + 1), (lat + 1, lat)]
    return lax.ppermute(value, ("band", "half"), pairs)


def crossed(value, ends, win_step=0):
    wins = lax.axis_size("win")
    pairs = []
    for win in range(wins):
        for source, target in (ends, ends[::-1]):
            if 0 <= win + win_step < wins:
                pairs.append((4 * win + source, 4 * (win + win_step) + target))
    return lax.ppermute(value, ("win", "band", "half"), pairs)


def body(model_rhs, obs_rhs, model_var, obs_var, obs_weight, depth):
    rows, width = model_rhs.shape[2:]
    ranks = lax.axis_size("win") * lat_count()
    total_rows = rows * lat_count()
    offset = (GRID_ROWS - total_rows) // 2
    local_rows = lat_index() * rows - rows + lax.broadcasted_iota(jnp.int32, (3 * rows, 128), 0)
    latitude = -jnp.pi / 2 + (local_rows.astype(jnp.float32) + offset + 0.5) * (jnp.pi / GRID_ROWS)
    inside = ((local_rows >= 0) & (local_rows < total_rows)).astype(jnp.float32)
    spin = inside * (mass_rate * spin_rate * jnp.sin(latitude))
    fields = (3, rows, width)

    middle, outer = (1, 2), (0, 3)
    pair, straight, local = run(
        prep_kernel, [(6, rows, width), (4, rows, width), fields],
        model_rhs, obs_rhs, model_var, obs_var, obs_weight, depth,
        scratch=[pltpu.VMEM(model_rhs.shape, jnp.float32)] * 5 + [pltpu.SemaphoreType.DMA((6,))],
        space=pltpu.HBM,
    )
    depth_near = swapped(depth, 0)
    depth_edge = crossed(depth_near, outer, 1)
    pair, straight, local, _ = lax.optimization_barrier((pair, straight, local, depth_near))
    came = shifted(straight, 1)
    relayed = swapped(jnp.concatenate([came[:1], depth_edge]), 0)
    pair_near, pair_far = swapped(pair, 0), crossed(pair, middle)
    known = (pair, pair_near, pair_far, came, relayed, spin, inside)
    local = shifted(local, 1)
    state, back = run(first_adjoint_kernel, [fields, fields], *known, work=4)
    held_state, local = lax.optimization_barrier((state, local))
    back = shifted(back, -1)
    state_far = crossed(held_state, middle)
    (tally,) = run(second_adjoint_kernel, [(2, rows, 128)], *known, local, state)
    state_near = swapped(state, 0)
    lead, sums = run(
        home_kernel, [fields, (4, rows, 128)],
        model_rhs, obs_rhs, model_var, obs_var, obs_weight, tally, back,
    )
    (rest,) = run(inner_forward_kernel, [fields], state, state_near, came, relayed, spin, inside, lead)
    (sent,) = run(
        closing_kernel, [(ranks, 128)], state_far, rest, came, relayed, spin, inside, sums,
        scratch=[pltpu.VMEM(fields, jnp.float32)],
    )
    gathered = lax.all_to_all(sent, ("win", "band", "half"), 0, 0, tiled=True)
    return run(
        combine_kernel, [model_rhs.shape] * 3,
        gathered, model_rhs, obs_rhs, model_var, obs_var, obs_weight, back, target=pltpu.HBM,
        scratch=[pltpu.VMEM(model_rhs.shape, jnp.float32)] * 3 + [pltpu.SemaphoreType.DMA((3,))],
    )


def solution(mesh):
    wins, lats = mesh.devices.shape
    mesh = Mesh(mesh.devices.reshape(wins, lats // 2, 2), ("win", "band", "half"))
    lat = ("band", "half")
    field = P("win", None, lat, None)
    in_specs = (field,) * 5 + (P("win", lat, None),)
    return jax.shard_map(body, mesh=mesh, in_specs=in_specs, out_specs=(field,) * 3, check_vma=False)
```

```python
import jax
import jax.numpy as jnp
from jax import lax
from jax.experimental import pallas as pl
from jax.experimental.pallas import tpu as pltpu
from jax.sharding import Mesh, PartitionSpec as P

GRID_ROWS = 768
STEPS = 4

mass_rate = 0.5
press_rate = 0.5
spin_rate = 0.4


def lon_gap(field):
    width = field.shape[-1]
    return pltpu.roll(field, width - 1, 1) - pltpu.roll(field, 1, 1)


def lat_gap(field):
    rows = field.shape[0]
    return pltpu.roll(field, rows - 1, 0) - pltpu.roll(field, 1, 0)


def even_lat():
    return lax.axis_index("half") == 0


def has_previous():
    return lax.axis_index("win") > 0


def stacked(own, near, far, index):
    even = even_lat()
    low = jnp.where(even, far[index], near[index])
    high = jnp.where(even, near[index], far[index])
    return jnp.concatenate([low, own[index], high], axis=0)


def prep_kernel(p, m, dvar, rvar, hobs, depth, pair, straight, local, pv, mv, dv, rv, hv, sems):
    copies = [
        pltpu.make_async_copy(source, target, sems.at[slot])
        for slot, (source, target) in enumerate(
            ((p, pv), (m, mv), (dvar, dv), (rvar, rv), (hobs, hv), (depth, straight.at[0:1]))
        )
    ]
    for copy in copies:
        copy.start()
    for copy in copies:
        copy.wait()
    for part in range(3):
        up = dv[0, part] * pv[0, part]
        seen = hv[0, part] * mv[0, part]
        pair[part] = pv[0, part]
        pair[3 + part] = up
        straight[1 + part] = pv[0, part] + seen
        local[part] = up + rv[0, part] * seen


def widened(tile, width):
    return jnp.concatenate([tile[...]] * (width // 128), axis=1)


def stretch_kernel(straight, depth_far, depth):
    even = even_lat()
    rows = straight.shape[1]
    depth[0:rows] = 0.25 * jnp.where(even, depth_far[0], straight[4])
    depth[rows:2 * rows] = 0.25 * straight[0]
    depth[2 * rows:] = 0.25 * jnp.where(even, straight[4], depth_far[0])


def adjoint(pair, pair_near, pair_far, straight, depth, spin, inside, base):
    depth = depth[...]
    turn, keep = widened(spin, depth.shape[1]), widened(inside, depth.shape[1])
    adj_height, adj_east, adj_north = [stacked(pair, pair_near, pair_far, base + part) for part in range(3)]
    for step in range(STEPS):
        adj_mid = adj_east - turn * adj_north
        adj_height = keep * (adj_height + 0.25 * (lat_gap(adj_north) + lon_gap(adj_mid)))
        adj_north = adj_north + turn * adj_mid + depth * lat_gap(adj_height)
        adj_east = adj_mid + depth * lon_gap(adj_height)
    rows = pair.shape[1]
    return [value[rows:2 * rows] for value in (adj_height, adj_east, adj_north)]


def first_adjoint_kernel(pair, pair_near, pair_far, straight, depth, spin, inside, state, back):
    swept = adjoint(pair, pair_near, pair_far, straight, depth, spin, inside, 0)
    link = has_previous()
    for part, value in enumerate(swept):
        back[part] = value
        state[part] = jnp.where(link, straight[1 + part] - value, 0.0)


def second_adjoint_kernel(pair, pair_near, pair_far, straight, depth, spin, inside, local, state, tally):
    swept = adjoint(pair, pair_near, pair_far, straight, depth, spin, inside, 3)
    link = has_previous()
    cross = square = 0.0
    for part, value in enumerate(swept):
        zx = jnp.where(link, local[part] - value, 0.0)
        cross += lane_sum(zx * state[part])
        square += lane_sum(zx * zx)
    tally[0] = cross
    tally[1] = square


def lane_sum(value):
    rows, width = value.shape
    total = value[:, :128]
    for start in range(128, width, 128):
        total = total + value[:, start:start + 128]
    return total


def home_kernel(p, m, dvar, rvar, hobs, tally, back, lead, sums):
    last = lax.axis_index("win") == lax.axis_size("win") - 1
    moments = [0.0, 0.0, 2.0 * tally[0], tally[1]]
    for part in range(3):
        dv, rv, hv = dvar[0, part], rvar[0, part], hobs[0, part]
        pv, mv = p[0, part], m[0, part]
        up, um = dv * pv, rv * mv
        ux = pv - back[part] + hv * mv
        lead[part] = dv * up + ux
        zm = rv * um + hv * ux
        zx = jnp.where(last, up + hv * um, 0.0)
        moments[0] += lane_sum(up * pv + um * mv)
        moments[1] += lane_sum(up * up + um * um + ux * ux)
        moments[2] += lane_sum(dv * up * up + rv * um * um + 2.0 * (zx * ux))
        moments[3] += lane_sum(zm * zm + zx * zx)
    for row, value in enumerate(moments):
        sums[row] = value


def forward(height, east, north, depth, turn, keep, gap):
    for step in range(STEPS):
        height = keep * (height - (lon_gap(depth * east) + gap(depth * north)))
        east = east + turn * north - 0.25 * lon_gap(height)
        north = north - turn * east - 0.25 * gap(height)
    return height, east, north


def inner_forward_kernel(state, state_near, straight, depth, spin, inside, lead, rest):
    depth = depth[...]
    turn, keep = widened(spin, depth.shape[1]), widened(inside, depth.shape[1])
    even = even_lat()
    rows = state.shape[1]
    fields = []
    for part in range(3):
        low = jnp.where(even, 0.0, state_near[part])
        high = jnp.where(even, state_near[part], 0.0)
        fields.append(jnp.concatenate([low, state[part], high], axis=0))
    for part, value in enumerate(forward(*fields, depth, turn, keep, lat_gap)):
        rest[part] = lead[part] - value[rows:2 * rows]


def open_lat_gap(field):
    rows = field.shape[0]
    row = lax.broadcasted_iota(jnp.int32, field.shape, 0)
    above = jnp.where(row < rows - 1, pltpu.roll(field, rows - 1, 0), 0.0)
    below = jnp.where(row > 0, pltpu.roll(field, 1, 0), 0.0)
    return above - below


def closing_kernel(state_far, rest, straight, depth, spin, inside, sums, sent, remainder):
    even = even_lat()
    rows, width = state_far.shape[1:]
    middle = lax.axis_index("band") != lax.axis_index("half")

    @pl.when(middle)
    def _():
        quarter = jnp.where(even, depth[:2 * rows], depth[rows:])
        turn, keep = [
            jnp.where(even, factor[:2 * rows], factor[rows:])
            for factor in (widened(spin, width), widened(inside, width))
        ]
        empty = jnp.zeros((rows, width), jnp.float32)
        fields = [
            jnp.where(
                even,
                jnp.concatenate([state_far[part], empty], axis=0),
                jnp.concatenate([empty, state_far[part]], axis=0),
            )
            for part in range(3)
        ]
        for part, value in enumerate(forward(*fields, quarter, turn, keep, open_lat_gap)):
            remainder[part] = rest[part] - jnp.where(even, value[rows:], value[:rows])

    @pl.when(jnp.logical_not(middle))
    def _():
        for part in range(3):
            remainder[part] = rest[part]

    square = 0.0
    for part in range(3):
        square += lane_sum(remainder[part] * remainder[part])
    moments = [sums[0], sums[1], sums[2], sums[3] + square]
    lane = lax.broadcasted_iota(jnp.int32, (1, 128), 1)
    row = 0.0
    for slot, value in enumerate(moments):
        folded = jnp.sum(value, axis=0, keepdims=True)
        folded = folded + pltpu.roll(folded, 64, 1)
        folded = folded + pltpu.roll(folded, 32, 1)
        row = jnp.where(lane // 32 == slot, folded, row)
    sent[...] = jnp.broadcast_to(row, sent.shape)


def lane_sum(value):
    rows, width = value.shape
    total = value[:, :128]
    for start in range(128, width, 128):
        total = total + value[:, start:start + 128]
    return total


def two_sum(a, b):
    total = a + b
    part = total - a
    return total, (a - (total - part)) + (b - part)


def split(a):
    wide = 4097.0 * a
    top = wide - (wide - a)
    return top, a - top


def two_product(a, b):
    product = a * b
    a_top, a_low = split(a)
    b_top, b_low = split(b)
    return product, ((a_top * b_top - product) + a_top * b_low + a_low * b_top) + a_low * b_low


def pair_product(a, b):
    product, rest = two_product(a[0], b[0])
    return product, rest + (a[0] * b[1] + a[1] * b[0])


def pair_gap(a, b):
    total, rest = two_sum(a[0], -b[0])
    return total + (rest + (a[1] - b[1]))


def coefficients(gathered):
    top = jnp.sum(gathered[...], axis=0, keepdims=True)
    low = jnp.zeros_like(top)
    shift = 1
    while shift < 32:
        top, rest = two_sum(top, pltpu.roll(top, shift, 1))
        low = low + pltpu.roll(low, shift, 1) + rest
        shift *= 2
    tops = [jnp.broadcast_to(top[:, lane:lane + 1], (1, 128)) for lane in range(31, 128, 32)]
    lows = [jnp.broadcast_to(low[:, lane:lane + 1], (1, 128)) for lane in range(31, 128, 32)]
    scale = 1.0 / tops[1]
    moments = []
    for value, rest in zip(tops, lows):
        product, error = two_product(value, scale)
        moments.append((product, error + rest * scale))
    m1, m2, m3, m4 = moments
    gap = pair_gap(pair_product(m2, m4), pair_product(m3, m3))
    y1 = pair_gap(pair_product(m1, m4), pair_product(m2, m3)) / gap
    y2 = pair_gap(pair_product(m2, m2), pair_product(m1, m3)) / gap
    return y1, y2


def combine_kernel(gathered, p, m, dvar, rvar, hobs, back, dual_model, dual_obs, increment, first, second, third, sems):
    y1, y2 = coefficients(gathered)
    rows, width = p.shape[2:]
    y1 = jnp.broadcast_to(jnp.concatenate([y1] * (width // 128), axis=1), (rows, width))
    y2 = jnp.broadcast_to(jnp.concatenate([y2] * (width // 128), axis=1), (rows, width))
    copies = [
        pltpu.make_async_copy(source, target, sems.at[slot])
        for slot, (source, target) in enumerate(((first, dual_model), (second, dual_obs), (third, increment)))
    ]
    for part in range(3):
        first[0, part] = (y1 + y2 * dvar[0, part]) * p[0, part]
    copies[0].start()
    for part in range(3):
        second[0, part] = (y1 + y2 * rvar[0, part]) * m[0, part]
    copies[1].start()
    for part in range(3):
        third[0, part] = y2 * (p[0, part] - back[part] + hobs[0, part] * m[0, part])
    copies[2].start()
    for copy in copies:
        copy.wait()


def run(kernel, out_shapes, *operands, scratch=(), space=pltpu.VMEM, target=pltpu.VMEM, work=4):
    shapes = [jax.ShapeDtypeStruct(shape, jnp.float32) for shape in out_shapes]
    size = sum(4 * operand.size for operand in operands) + sum(4 * shape.size for shape in shapes)
    if space is not pltpu.VMEM:
        operands = [pltpu.with_memory_space_constraint(operand, space) for operand in operands]
    return pl.pallas_call(
        kernel,
        out_shape=shapes,
        in_specs=[pl.BlockSpec(memory_space=space)] * len(operands),
        out_specs=[pl.BlockSpec(memory_space=target)] * len(shapes),
        scratch_shapes=scratch,
        compiler_params=pltpu.CompilerParams(vmem_limit_bytes=32 * 1024 * 1024),
        cost_estimate=pl.CostEstimate(flops=work * size // 4, bytes_accessed=work * size // 4, transcendentals=0),
    )(*operands)


def shifted(value, step):
    count = lax.axis_size("win")
    initial, last = (max(0, -step), min(count, count - step))
    return lax.ppermute(value, "win", [(source, source + step) for source in range(initial, last)])


def lat_count():
    return lax.axis_size("band") * lax.axis_size("half")


def lat_index():
    return lax.axis_index("band") * lax.axis_size("half") + lax.axis_index("half")


def swapped(value, first):
    pairs = []
    for lat in range(first, lat_count() - 1, 2):
        pairs += [(lat, lat + 1), (lat + 1, lat)]
    return lax.ppermute(value, ("band", "half"), pairs)


def sent_on(value, steps, win_step):
    wins = lax.axis_size("win")
    pairs = []
    for win in range(wins - win_step):
        for source, target in steps:
            pairs.append((4 * win + source, 4 * (win + win_step) + target))
    return lax.ppermute(value, ("win", "band", "half"), pairs)


def crossed(value, ends):
    return sent_on(value, (ends, ends[::-1]), 0)


def body(model_rhs, obs_rhs, model_var, obs_var, obs_weight, depth):
    rows, width = model_rhs.shape[2:]
    ranks = lax.axis_size("win") * lat_count()
    total_rows = rows * lat_count()
    offset = (GRID_ROWS - total_rows) // 2
    local_rows = lat_index() * rows - rows + lax.broadcasted_iota(jnp.int32, (3 * rows, 128), 0)
    latitude = -jnp.pi / 2 + (local_rows.astype(jnp.float32) + offset + 0.5) * (jnp.pi / GRID_ROWS)
    inside = ((local_rows >= 0) & (local_rows < total_rows)).astype(jnp.float32)
    spin = inside * (mass_rate * spin_rate * jnp.sin(latitude))
    fields = (3, rows, width)

    middle = (1, 2)
    pair, straight, local = run(
        prep_kernel, [(6, rows, width), (4, rows, width), fields],
        model_rhs, obs_rhs, model_var, obs_var, obs_weight, depth,
        scratch=[pltpu.VMEM(model_rhs.shape, jnp.float32)] * 5 + [pltpu.SemaphoreType.DMA((6,))],
        space=pltpu.HBM,
    )
    depth_near = swapped(depth, 0)
    depth_far = sent_on(depth_near, ((0, 2), (3, 1)), 1)
    pair, straight, local, _ = lax.optimization_barrier((pair, straight, local, depth_near))
    came = shifted(jnp.concatenate([straight, depth_near]), 1)
    pair_near, pair_far = swapped(pair, 0), crossed(pair, middle)
    (stretched,) = run(stretch_kernel, [(3 * rows, width)], came, depth_far, work=100000)
    known = (pair, pair_near, pair_far, came, stretched, spin, inside)
    local = shifted(local, 1)
    state, back = run(first_adjoint_kernel, [fields, fields], *known, work=4)
    held_state, local = lax.optimization_barrier((state, local))
    back = shifted(back, -1)
    state_far = crossed(held_state, middle)
    (tally,) = run(second_adjoint_kernel, [(2, rows, 128)], *known, local, state)
    state_near = swapped(state, 0)
    lead, sums = run(
        home_kernel, [fields, (4, rows, 128)],
        model_rhs, obs_rhs, model_var, obs_var, obs_weight, tally, back,
    )
    (rest,) = run(inner_forward_kernel, [fields], state, state_near, came, stretched, spin, inside, lead)
    (sent,) = run(
        closing_kernel, [(ranks, 128)], state_far, rest, came, stretched, spin, inside, sums,
        scratch=[pltpu.VMEM(fields, jnp.float32)],
    )
    gathered = lax.all_to_all(sent, ("win", "band", "half"), 0, 0, tiled=True)
    return run(
        combine_kernel, [model_rhs.shape] * 3,
        gathered, model_rhs, obs_rhs, model_var, obs_var, obs_weight, back, target=pltpu.HBM,
        scratch=[pltpu.VMEM(model_rhs.shape, jnp.float32)] * 3 + [pltpu.SemaphoreType.DMA((3,))],
    )


def solution(mesh):
    wins, lats = mesh.devices.shape
    mesh = Mesh(mesh.devices.reshape(wins, lats // 2, 2), ("win", "band", "half"))
    lat = ("band", "half")
    field = P("win", None, lat, None)
    in_specs = (field,) * 5 + (P("win", lat, None),)
    return jax.shard_map(body, mesh=mesh, in_specs=in_specs, out_specs=(field,) * 3, check_vma=False)
```

```python
import jax
import jax.numpy as jnp
from jax import lax
from jax.experimental import pallas as pl
from jax.experimental.pallas import tpu as pltpu
from jax.sharding import Mesh, PartitionSpec as P

GRID_ROWS = 768
STEPS = 4

mass_rate = 0.5
press_rate = 0.5
spin_rate = 0.4


def lon_gap(field):
    width = field.shape[-1]
    return pltpu.roll(field, width - 1, 1) - pltpu.roll(field, 1, 1)


def lat_gap(field):
    rows = field.shape[0]
    return pltpu.roll(field, rows - 1, 0) - pltpu.roll(field, 1, 0)


def even_lat():
    return lax.axis_index("half") == 0


def has_previous():
    return lax.axis_index("win") > 0


def stacked(own, near, far, index):
    even = even_lat()
    low = jnp.where(even, far[index], near[index])
    high = jnp.where(even, near[index], far[index])
    return jnp.concatenate([low, own[index], high], axis=0)


def prep_kernel(p, m, dvar, rvar, hobs, depth, pair, straight, local, pv, mv, dv, rv, hv, sems):
    copies = [
        pltpu.make_async_copy(source, target, sems.at[slot])
        for slot, (source, target) in enumerate(
            ((p, pv), (m, mv), (dvar, dv), (rvar, rv), (hobs, hv), (depth, straight.at[0:1]))
        )
    ]
    for copy in copies:
        copy.start()
    for copy in copies:
        copy.wait()
    for part in range(3):
        up = dv[0, part] * pv[0, part]
        seen = hv[0, part] * mv[0, part]
        pair[part] = pv[0, part]
        pair[3 + part] = up
        straight[1 + part] = pv[0, part] + seen
        local[part] = up + rv[0, part] * seen


def widened(tile, width):
    return jnp.concatenate([tile[...]] * (width // 128), axis=1)


def stretched(straight, relayed):
    even = even_lat()
    low = jnp.where(even, relayed[1], relayed[0])
    high = jnp.where(even, relayed[0], relayed[1])
    return 0.25 * jnp.concatenate([low, straight[0], high], axis=0)


def adjoint(pair, pair_near, pair_far, straight, relayed, spin, inside, base):
    depth = stretched(straight, relayed)
    turn, keep = widened(spin, depth.shape[1]), widened(inside, depth.shape[1])
    adj_height, adj_east, adj_north = [stacked(pair, pair_near, pair_far, base + part) for part in range(3)]
    for step in range(STEPS):
        adj_mid = adj_east - turn * adj_north
        adj_height = keep * (adj_height + 0.25 * (lat_gap(adj_north) + lon_gap(adj_mid)))
        adj_north = adj_north + turn * adj_mid + depth * lat_gap(adj_height)
        adj_east = adj_mid + depth * lon_gap(adj_height)
    rows = pair.shape[1]
    return [value[rows:2 * rows] for value in (adj_height, adj_east, adj_north)]


def first_adjoint_kernel(pair, pair_near, pair_far, straight, relayed, spin, inside, state, back):
    swept = adjoint(pair, pair_near, pair_far, straight, relayed, spin, inside, 0)
    link = has_previous()
    for part, value in enumerate(swept):
        back[part] = value
        state[part] = jnp.where(link, straight[1 + part] - value, 0.0)


def second_adjoint_kernel(pair, pair_near, pair_far, straight, relayed, spin, inside, local, state, tally):
    swept = adjoint(pair, pair_near, pair_far, straight, relayed, spin, inside, 3)
    link = has_previous()
    zero = jnp.zeros((pair.shape[1], 128), jnp.float32)
    cross = square = (zero, zero)
    for part, value in enumerate(swept):
        zx = jnp.where(link, local[part] - value, 0.0)
        cross = gathered_in(cross, zx * state[part])
        square = gathered_in(square, zx * zx)
    for slot, value in enumerate(cross + square):
        tally[slot] = value


def lane_sum(value):
    tiles = [value[:, start:start + 128] for start in range(0, value.shape[1], 128)]
    while len(tiles) > 1:
        tiles = [sum(tiles[at:at + 2]) for at in range(0, len(tiles), 2)]
    return tiles[0]


def two_sum(a, b):
    total = a + b
    part = total - a
    return total, (a - (total - part)) + (b - part)


def gathered_in(pair, value):
    total, rest = two_sum(pair[0], lane_sum(value))
    return total, pair[1] + rest


def folded(pair, shift, axis):
    total, rest = two_sum(pair[0], pltpu.roll(pair[0], shift, axis))
    return total, pair[1] + pltpu.roll(pair[1], shift, axis) + rest


def home_kernel(p, m, dvar, rvar, hobs, tally, back, lead, sums):
    last = lax.axis_index("win") == lax.axis_size("win") - 1
    zero = jnp.zeros_like(tally[0])
    m1 = m2 = (zero, zero)
    m3, m4 = (2.0 * tally[0], 2.0 * tally[1]), (tally[2], tally[3])
    for part in range(3):
        dv, rv, hv = dvar[0, part], rvar[0, part], hobs[0, part]
        pv, mv = p[0, part], m[0, part]
        up, um = dv * pv, rv * mv
        ux = pv - back[part] + hv * mv
        lead[part] = dv * up + ux
        zm = rv * um + hv * ux
        zx = jnp.where(last, up + hv * um, 0.0)
        m1 = gathered_in(m1, up * pv + um * mv)
        m2 = gathered_in(m2, up * up + um * um + ux * ux)
        m3 = gathered_in(m3, dv * up * up + rv * um * um + 2.0 * (zx * ux))
        m4 = gathered_in(m4, zm * zm + zx * zx)
    for slot, value in enumerate(m1 + m2 + m3 + m4):
        sums[slot] = value


def forward(height, east, north, depth, turn, keep, gap):
    for step in range(STEPS):
        height = keep * (height - (lon_gap(depth * east) + gap(depth * north)))
        east = east + turn * north - 0.25 * lon_gap(height)
        north = north - turn * east - 0.25 * gap(height)
    return height, east, north


def inner_forward_kernel(state, state_near, straight, relayed, spin, inside, lead, rest):
    depth = stretched(straight, relayed)
    turn, keep = widened(spin, depth.shape[1]), widened(inside, depth.shape[1])
    even = even_lat()
    rows = state.shape[1]
    fields = []
    for part in range(3):
        low = jnp.where(even, 0.0, state_near[part])
        high = jnp.where(even, state_near[part], 0.0)
        fields.append(jnp.concatenate([low, state[part], high], axis=0))
    for part, value in enumerate(forward(*fields, depth, turn, keep, lat_gap)):
        rest[part] = lead[part] - value[rows:2 * rows]


def open_lat_gap(field):
    rows = field.shape[0]
    row = lax.broadcasted_iota(jnp.int32, field.shape, 0)
    above = jnp.where(row < rows - 1, pltpu.roll(field, rows - 1, 0), 0.0)
    below = jnp.where(row > 0, pltpu.roll(field, 1, 0), 0.0)
    return above - below


def closing_kernel(state_far, rest, straight, relayed, spin, inside, sums, sent, remainder):
    even = even_lat()
    rows, width = state_far.shape[1:]
    middle = lax.axis_index("band") != lax.axis_index("half")

    @pl.when(middle)
    def _():
        depth = jnp.where(
            even,
            jnp.concatenate([relayed[1], straight[0]], axis=0),
            jnp.concatenate([straight[0], relayed[1]], axis=0),
        )
        turn, keep = [
            jnp.where(even, factor[:2 * rows], factor[rows:])
            for factor in (widened(spin, width), widened(inside, width))
        ]
        empty = jnp.zeros((rows, width), jnp.float32)
        fields = [
            jnp.where(
                even,
                jnp.concatenate([state_far[part], empty], axis=0),
                jnp.concatenate([empty, state_far[part]], axis=0),
            )
            for part in range(3)
        ]
        for part, value in enumerate(forward(*fields, 0.25 * depth, turn, keep, open_lat_gap)):
            remainder[part] = rest[part] - jnp.where(even, value[rows:], value[:rows])

    @pl.when(jnp.logical_not(middle))
    def _():
        for part in range(3):
            remainder[part] = rest[part]

    moments = [(sums[slot], sums[slot + 1]) for slot in range(0, 8, 2)]
    for part in range(3):
        moments[3] = gathered_in(moments[3], remainder[part] * remainder[part])
    lane = lax.broadcasted_iota(jnp.int32, (rows, 128), 1) // 16
    row = 0.0
    for slot, pair in enumerate(moments):
        for axis, shift in ((0, 4), (0, 2), (0, 1), (1, 64), (1, 32), (1, 16)):
            pair = folded(pair, shift, axis)
        row = jnp.where(lane == slot, pair[0], jnp.where(lane == slot + 4, pair[1], row))
    for start in range(0, sent.shape[0], rows):
        sent[start:start + rows] = row


def split(a):
    wide = 4097.0 * a
    top = wide - (wide - a)
    return top, a - top


def two_product(a, b):
    product = a * b
    a_top, a_low = split(a)
    b_top, b_low = split(b)
    return product, ((a_top * b_top - product) + a_top * b_low + a_low * b_top) + a_low * b_low


def pair_product(a, b):
    product, rest = two_product(a[0], b[0])
    return product, rest + (a[0] * b[1] + a[1] * b[0])


def pair_gap(a, b):
    total, rest = two_sum(a[0], -b[0])
    return total + (rest + (a[1] - b[1]))


def coefficients(gathered):
    pair = gathered[0:8], jnp.zeros((8, 128), jnp.float32)
    for start in range(8, gathered.shape[0], 8):
        total, rest = two_sum(pair[0], gathered[start:start + 8])
        pair = total, pair[1] + rest
    for axis, shift in ((0, 4), (0, 2), (0, 1), (1, 1), (1, 2), (1, 4), (1, 8)):
        pair = folded(pair, shift, axis)
    tops, lows = [], []
    for lane in range(15, 64, 16):
        top, low = [
            jnp.broadcast_to(value[0:1, at:at + 1], (1, 128))
            for value, at in ((pair[0], lane), (pair[1] + pltpu.roll(pair[0], 64, 1), lane))
        ]
        tops.append(top)
        lows.append(low)
    scale = 1.0 / tops[1]
    moments = []
    for value, rest in zip(tops, lows):
        product, error = two_product(value, scale)
        moments.append((product, error + rest * scale))
    m1, m2, m3, m4 = moments
    gap = pair_gap(pair_product(m2, m4), pair_product(m3, m3))
    y1 = pair_gap(pair_product(m1, m4), pair_product(m2, m3)) / gap
    y2 = pair_gap(pair_product(m2, m2), pair_product(m1, m3)) / gap
    return y1, y2


def combine_kernel(gathered, p, m, dvar, rvar, hobs, back, dual_model, dual_obs, increment, first, second, third, sems):
    y1, y2 = coefficients(gathered)
    rows, width = p.shape[2:]
    y1 = jnp.broadcast_to(jnp.concatenate([y1] * (width // 128), axis=1), (rows, width))
    y2 = jnp.broadcast_to(jnp.concatenate([y2] * (width // 128), axis=1), (rows, width))
    copies = [
        pltpu.make_async_copy(source, target, sems.at[slot])
        for slot, (source, target) in enumerate(((first, dual_model), (second, dual_obs), (third, increment)))
    ]
    for part in range(3):
        first[0, part] = (y1 + y2 * dvar[0, part]) * p[0, part]
    copies[0].start()
    for part in range(3):
        second[0, part] = (y1 + y2 * rvar[0, part]) * m[0, part]
    copies[1].start()
    for part in range(3):
        third[0, part] = y2 * (p[0, part] - back[part] + hobs[0, part] * m[0, part])
    copies[2].start()
    for copy in copies:
        copy.wait()


def run(kernel, out_shapes, *operands, scratch=(), space=pltpu.VMEM, target=pltpu.VMEM, work=4):
    shapes = [jax.ShapeDtypeStruct(shape, jnp.float32) for shape in out_shapes]
    size = sum(4 * operand.size for operand in operands) + sum(4 * shape.size for shape in shapes)
    if space is not pltpu.VMEM:
        operands = [pltpu.with_memory_space_constraint(operand, space) for operand in operands]
    return pl.pallas_call(
        kernel,
        out_shape=shapes,
        in_specs=[pl.BlockSpec(memory_space=space)] * len(operands),
        out_specs=[pl.BlockSpec(memory_space=target)] * len(shapes),
        scratch_shapes=scratch,
        compiler_params=pltpu.CompilerParams(vmem_limit_bytes=32 * 1024 * 1024),
        cost_estimate=pl.CostEstimate(flops=work * size // 4, bytes_accessed=work * size // 4, transcendentals=0),
    )(*operands)


def shifted(value, step):
    count = lax.axis_size("win")
    initial, last = (max(0, -step), min(count, count - step))
    return lax.ppermute(value, "win", [(source, source + step) for source in range(initial, last)])


def lat_count():
    return lax.axis_size("band") * lax.axis_size("half")


def lat_index():
    return lax.axis_index("band") * lax.axis_size("half") + lax.axis_index("half")


def swapped(value, first):
    pairs = []
    for lat in range(first, lat_count() - 1, 2):
        pairs += [(lat, lat + 1), (lat + 1, lat)]
    return lax.ppermute(value, ("band", "half"), pairs)


def crossed(value, ends, win_step=0):
    wins = lax.axis_size("win")
    pairs = []
    for win in range(wins):
        for source, target in (ends, ends[::-1]):
            if 0 <= win + win_step < wins:
                pairs.append((4 * win + source, 4 * (win + win_step) + target))
    return lax.ppermute(value, ("win", "band", "half"), pairs)


def body(model_rhs, obs_rhs, model_var, obs_var, obs_weight, depth):
    rows, width = model_rhs.shape[2:]
    ranks = lax.axis_size("win") * lat_count()
    total_rows = rows * lat_count()
    offset = (GRID_ROWS - total_rows) // 2
    local_rows = lat_index() * rows - rows + lax.broadcasted_iota(jnp.int32, (3 * rows, 128), 0)
    latitude = -jnp.pi / 2 + (local_rows.astype(jnp.float32) + offset + 0.5) * (jnp.pi / GRID_ROWS)
    inside = ((local_rows >= 0) & (local_rows < total_rows)).astype(jnp.float32)
    spin = inside * (mass_rate * spin_rate * jnp.sin(latitude))
    fields = (3, rows, width)

    middle, outer = (1, 2), (0, 3)
    pair, straight, local = run(
        prep_kernel, [(6, rows, width), (4, rows, width), fields],
        model_rhs, obs_rhs, model_var, obs_var, obs_weight, depth,
        scratch=[pltpu.VMEM(model_rhs.shape, jnp.float32)] * 5 + [pltpu.SemaphoreType.DMA((6,))],
        space=pltpu.HBM,
    )
    depth_near = swapped(depth, 0)
    depth_edge = crossed(depth_near, outer, 1)
    pair, straight, local, _ = lax.optimization_barrier((pair, straight, local, depth_near))
    came = shifted(straight, 1)
    relayed = swapped(jnp.concatenate([came[:1], depth_edge]), 0)
    pair_near, pair_far = swapped(pair, 0), crossed(pair, middle)
    known = (pair, pair_near, pair_far, came, relayed, spin, inside)
    local = shifted(local, 1)
    state, back = run(first_adjoint_kernel, [fields, fields], *known, work=4)
    held_state, local = lax.optimization_barrier((state, local))
    back = shifted(back, -1)
    state_far = crossed(held_state, middle)
    (tally,) = run(second_adjoint_kernel, [(4, rows, 128)], *known, local, state)
    state_near = swapped(state, 0)
    lead, sums = run(
        home_kernel, [fields, (8, rows, 128)],
        model_rhs, obs_rhs, model_var, obs_var, obs_weight, tally, back,
    )
    (rest,) = run(inner_forward_kernel, [fields], state, state_near, came, relayed, spin, inside, lead)
    (sent,) = run(
        closing_kernel, [(ranks, 128)], state_far, rest, came, relayed, spin, inside, sums,
        scratch=[pltpu.VMEM(fields, jnp.float32)],
    )
    gathered = lax.all_to_all(sent, ("win", "band", "half"), 0, 0, tiled=True)
    return run(
        combine_kernel, [model_rhs.shape] * 3,
        gathered, model_rhs, obs_rhs, model_var, obs_var, obs_weight, back, target=pltpu.HBM,
        scratch=[pltpu.VMEM(model_rhs.shape, jnp.float32)] * 3 + [pltpu.SemaphoreType.DMA((3,))],
    )


def solution(mesh):
    wins, lats = mesh.devices.shape
    mesh = Mesh(mesh.devices.reshape(wins, lats // 2, 2), ("win", "band", "half"))
    lat = ("band", "half")
    field = P("win", None, lat, None)
    in_specs = (field,) * 5 + (P("win", lat, None),)
    return jax.shard_map(body, mesh=mesh, in_specs=in_specs, out_specs=(field,) * 3, check_vma=False)
```

```python
import jax
import jax.numpy as jnp
from jax import lax
from jax.experimental import pallas as pl
from jax.experimental.pallas import tpu as pltpu
from jax.sharding import Mesh, PartitionSpec as P

GRID_ROWS = 768
STEPS = 4

mass_rate = 0.5
press_rate = 0.5
spin_rate = 0.4


def lon_gap(field):
    width = field.shape[-1]
    return pltpu.roll(field, width - 1, 1) - pltpu.roll(field, 1, 1)


def lat_gap(field):
    rows = field.shape[0]
    return pltpu.roll(field, rows - 1, 0) - pltpu.roll(field, 1, 0)


def even_lat():
    return lax.axis_index("half") == 0


def has_previous():
    return lax.axis_index("win") > 0


def stacked(own, near, far, index):
    even = even_lat()
    low = jnp.where(even, far[index], near[index])
    high = jnp.where(even, near[index], far[index])
    return jnp.concatenate([low, own[index], high], axis=0)


def prep_kernel(p, m, dvar, rvar, hobs, depth, pair, straight, local, pv, mv, dv, rv, hv, sems):
    copies = [
        pltpu.make_async_copy(source, target, sems.at[slot])
        for slot, (source, target) in enumerate(
            ((p, pv), (m, mv), (dvar, dv), (rvar, rv), (hobs, hv), (depth, straight.at[0:1]))
        )
    ]
    for copy in copies:
        copy.start()
    for copy in copies:
        copy.wait()
    for part in range(3):
        up = dv[0, part] * pv[0, part]
        seen = hv[0, part] * mv[0, part]
        pair[part] = pv[0, part]
        pair[3 + part] = up
        straight[1 + part] = pv[0, part] + seen
        local[part] = up + rv[0, part] * seen


def widened(factors, index, width):
    return jnp.concatenate([factors[index]] * (width // 128), axis=1)


def stretched(straight, relayed):
    even = even_lat()
    low = jnp.where(even, relayed[1], relayed[0])
    high = jnp.where(even, relayed[0], relayed[1])
    return 0.25 * jnp.concatenate([low, straight[0], high], axis=0)


def adjoint(pair, pair_near, pair_far, straight, relayed, spin, base):
    depth = stretched(straight, relayed)
    turn, keep = widened(spin, 0, depth.shape[1]), widened(spin, 1, depth.shape[1])
    adj_height, adj_east, adj_north = [stacked(pair, pair_near, pair_far, base + part) for part in range(3)]
    for step in range(STEPS):
        adj_mid = adj_east - turn * adj_north
        adj_height = keep * (adj_height + 0.25 * (lat_gap(adj_north) + lon_gap(adj_mid)))
        adj_north = adj_north + turn * adj_mid + depth * lat_gap(adj_height)
        adj_east = adj_mid + depth * lon_gap(adj_height)
    rows = pair.shape[1]
    return [value[rows:2 * rows] for value in (adj_height, adj_east, adj_north)]


def first_adjoint_kernel(pair, pair_near, pair_far, straight, relayed, spin, state, back):
    swept = adjoint(pair, pair_near, pair_far, straight, relayed, spin, 0)
    link = has_previous()
    for part, value in enumerate(swept):
        back[part] = value
        state[part] = jnp.where(link, straight[1 + part] - value, 0.0)


def second_adjoint_kernel(pair, pair_near, pair_far, straight, relayed, spin, local, state, tally):
    swept = adjoint(pair, pair_near, pair_far, straight, relayed, spin, 3)
    link = has_previous()
    zero = jnp.zeros((pair.shape[1], 128), jnp.float32)
    cross = square = (zero, zero)
    for part, value in enumerate(swept):
        zx = jnp.where(link, local[part] - value, 0.0)
        cross = gathered_in(cross, zx * state[part])
        square = gathered_in(square, zx * zx)
    for slot, value in enumerate(cross + square):
        tally[slot] = value


def lane_sum(value):
    tiles = [value[:, start:start + 128] for start in range(0, value.shape[1], 128)]
    while len(tiles) > 1:
        tiles = [sum(tiles[at:at + 2]) for at in range(0, len(tiles), 2)]
    return tiles[0]


def two_sum(a, b):
    total = a + b
    part = total - a
    return total, (a - (total - part)) + (b - part)


def gathered_in(pair, value):
    total, rest = two_sum(pair[0], lane_sum(value))
    return total, pair[1] + rest


def folded(pair, shift, axis):
    total, rest = two_sum(pair[0], pltpu.roll(pair[0], shift, axis))
    return total, pair[1] + pltpu.roll(pair[1], shift, axis) + rest


def home_kernel(p, m, dvar, rvar, hobs, tally, back, lead, sums):
    last = lax.axis_index("win") == lax.axis_size("win") - 1
    zero = jnp.zeros_like(tally[0])
    m1 = m2 = (zero, zero)
    m3, m4 = (2.0 * tally[0], 2.0 * tally[1]), (tally[2], tally[3])
    for part in range(3):
        dv, rv, hv = dvar[0, part], rvar[0, part], hobs[0, part]
        pv, mv = p[0, part], m[0, part]
        up, um = dv * pv, rv * mv
        ux = pv - back[part] + hv * mv
        lead[part] = dv * up + ux
        zm = rv * um + hv * ux
        zx = jnp.where(last, up + hv * um, 0.0)
        m1 = gathered_in(m1, up * pv + um * mv)
        m2 = gathered_in(m2, up * up + um * um + ux * ux)
        m3 = gathered_in(m3, dv * up * up + rv * um * um + 2.0 * (zx * ux))
        m4 = gathered_in(m4, zm * zm + zx * zx)
    for slot, value in enumerate(m1 + m2 + m3 + m4):
        sums[slot] = value


def forward(height, east, north, depth, turn, keep, gap):
    for step in range(STEPS):
        height = keep * (height - (lon_gap(depth * east) + gap(depth * north)))
        east = east + turn * north - 0.25 * lon_gap(height)
        north = north - turn * east - 0.25 * gap(height)
    return height, east, north


def inner_forward_kernel(state, state_near, straight, relayed, spin, lead, rest):
    depth = stretched(straight, relayed)
    turn, keep = widened(spin, 0, depth.shape[1]), widened(spin, 1, depth.shape[1])
    even = even_lat()
    rows = state.shape[1]
    fields = []
    for part in range(3):
        low = jnp.where(even, 0.0, state_near[part])
        high = jnp.where(even, state_near[part], 0.0)
        fields.append(jnp.concatenate([low, state[part], high], axis=0))
    for part, value in enumerate(forward(*fields, depth, turn, keep, lat_gap)):
        rest[part] = lead[part] - value[rows:2 * rows]


def open_lat_gap(field):
    rows = field.shape[0]
    row = lax.broadcasted_iota(jnp.int32, field.shape, 0)
    above = jnp.where(row < rows - 1, pltpu.roll(field, rows - 1, 0), 0.0)
    below = jnp.where(row > 0, pltpu.roll(field, 1, 0), 0.0)
    return above - below


def closing_kernel(state_far, rest, straight, relayed, spin, sums, sent, remainder):
    even = even_lat()
    rows, width = state_far.shape[1:]
    middle = lax.axis_index("band") != lax.axis_index("half")

    @pl.when(middle)
    def _():
        depth = jnp.where(
            even,
            jnp.concatenate([relayed[1], straight[0]], axis=0),
            jnp.concatenate([straight[0], relayed[1]], axis=0),
        )
        turn, keep = [
            jnp.where(even, factor[:2 * rows], factor[rows:])
            for factor in (widened(spin, 0, width), widened(spin, 1, width))
        ]
        empty = jnp.zeros((rows, width), jnp.float32)
        fields = [
            jnp.where(
                even,
                jnp.concatenate([state_far[part], empty], axis=0),
                jnp.concatenate([empty, state_far[part]], axis=0),
            )
            for part in range(3)
        ]
        for part, value in enumerate(forward(*fields, 0.25 * depth, turn, keep, open_lat_gap)):
            remainder[part] = rest[part] - jnp.where(even, value[rows:], value[:rows])

    @pl.when(jnp.logical_not(middle))
    def _():
        for part in range(3):
            remainder[part] = rest[part]

    moments = [(sums[slot], sums[slot + 1]) for slot in range(0, 8, 2)]
    for part in range(3):
        moments[3] = gathered_in(moments[3], remainder[part] * remainder[part])
    lane = lax.broadcasted_iota(jnp.int32, (rows, 128), 1) // 16
    row = 0.0
    for slot, pair in enumerate(moments):
        for axis, shift in ((0, 4), (0, 2), (0, 1), (1, 64), (1, 32), (1, 16)):
            pair = folded(pair, shift, axis)
        row = jnp.where(lane == slot, pair[0], jnp.where(lane == slot + 4, pair[1], row))
    for start in range(0, sent.shape[0], rows):
        sent[start:start + rows] = row


def split(a):
    wide = 4097.0 * a
    top = wide - (wide - a)
    return top, a - top


def two_product(a, b):
    product = a * b
    a_top, a_low = split(a)
    b_top, b_low = split(b)
    return product, ((a_top * b_top - product) + a_top * b_low + a_low * b_top) + a_low * b_low


def pair_product(a, b):
    product, rest = two_product(a[0], b[0])
    return product, rest + (a[0] * b[1] + a[1] * b[0])


def pair_gap(a, b):
    total, rest = two_sum(a[0], -b[0])
    return total + (rest + (a[1] - b[1]))


def coefficients(gathered):
    pair = gathered[0:8], jnp.zeros((8, 128), jnp.float32)
    for start in range(8, gathered.shape[0], 8):
        total, rest = two_sum(pair[0], gathered[start:start + 8])
        pair = total, pair[1] + rest
    for axis, shift in ((0, 4), (0, 2), (0, 1), (1, 1), (1, 2), (1, 4), (1, 8)):
        pair = folded(pair, shift, axis)
    tops, lows = [], []
    for lane in range(15, 64, 16):
        top, low = [
            jnp.broadcast_to(value[0:1, at:at + 1], (1, 128))
            for value, at in ((pair[0], lane), (pair[1] + pltpu.roll(pair[0], 64, 1), lane))
        ]
        tops.append(top)
        lows.append(low)
    scale = 1.0 / tops[1]
    moments = []
    for value, rest in zip(tops, lows):
        product, error = two_product(value, scale)
        moments.append((product, error + rest * scale))
    m1, m2, m3, m4 = moments
    gap = pair_gap(pair_product(m2, m4), pair_product(m3, m3))
    y1 = pair_gap(pair_product(m1, m4), pair_product(m2, m3)) / gap
    y2 = pair_gap(pair_product(m2, m2), pair_product(m1, m3)) / gap
    return y1, y2


def combine_kernel(gathered, p, m, dvar, rvar, hobs, back, dual_model, dual_obs, increment):
    y1, y2 = coefficients(gathered)
    rows, width = p.shape[2:]
    y1 = jnp.broadcast_to(jnp.concatenate([y1] * (width // 128), axis=1), (rows, width))
    y2 = jnp.broadcast_to(jnp.concatenate([y2] * (width // 128), axis=1), (rows, width))
    for part in range(3):
        pv, mv = p[0, part], m[0, part]
        dual_model[0, part] = (y1 + y2 * dvar[0, part]) * pv
        dual_obs[0, part] = (y1 + y2 * rvar[0, part]) * mv
        increment[0, part] = y2 * (pv - back[part] + hobs[0, part] * mv)


def run(kernel, out_shapes, *operands, scratch=(), space=pltpu.VMEM, target=pltpu.VMEM, work=4):
    shapes = [jax.ShapeDtypeStruct(shape, jnp.float32) for shape in out_shapes]
    size = sum(4 * operand.size for operand in operands) + sum(4 * shape.size for shape in shapes)
    if space is not pltpu.VMEM:
        operands = [pltpu.with_memory_space_constraint(operand, space) for operand in operands]
    return pl.pallas_call(
        kernel,
        out_shape=shapes,
        in_specs=[pl.BlockSpec(memory_space=space)] * len(operands),
        out_specs=[pl.BlockSpec(memory_space=target)] * len(shapes),
        scratch_shapes=scratch,
        compiler_params=pltpu.CompilerParams(vmem_limit_bytes=32 * 1024 * 1024),
        cost_estimate=pl.CostEstimate(flops=work * size // 4, bytes_accessed=work * size // 4, transcendentals=0),
    )(*operands)


def shifted(value, step):
    count = lax.axis_size("win")
    initial, last = (max(0, -step), min(count, count - step))
    return lax.ppermute(value, "win", [(source, source + step) for source in range(initial, last)])


def lat_count():
    return lax.axis_size("band") * lax.axis_size("half")


def lat_index():
    return lax.axis_index("band") * lax.axis_size("half") + lax.axis_index("half")


def swapped(value, first):
    pairs = []
    for lat in range(first, lat_count() - 1, 2):
        pairs += [(lat, lat + 1), (lat + 1, lat)]
    return lax.ppermute(value, ("band", "half"), pairs)


def crossed(value, ends, win_step=0):
    wins = lax.axis_size("win")
    pairs = []
    for win in range(wins):
        for source, target in (ends, ends[::-1]):
            if 0 <= win + win_step < wins:
                pairs.append((4 * win + source, 4 * (win + win_step) + target))
    return lax.ppermute(value, ("win", "band", "half"), pairs)


def body(model_rhs, obs_rhs, model_var, obs_var, obs_weight, depth):
    rows, width = model_rhs.shape[2:]
    ranks = lax.axis_size("win") * lat_count()
    total_rows = rows * lat_count()
    offset = (GRID_ROWS - total_rows) // 2
    local_rows = lat_index() * rows - rows + lax.broadcasted_iota(jnp.int32, (3 * rows, 128), 0)
    latitude = -jnp.pi / 2 + (local_rows.astype(jnp.float32) + offset + 0.5) * (jnp.pi / GRID_ROWS)
    inside = (local_rows >= 0) & (local_rows < total_rows)
    spin = jnp.where(inside, mass_rate * spin_rate * jnp.sin(latitude), 0.0)
    spin = jnp.stack([spin, inside.astype(jnp.float32)])
    fields = (3, rows, width)

    middle, outer = (1, 2), (0, 3)
    pair, straight, local = run(
        prep_kernel, [(6, rows, width), (4, rows, width), fields],
        model_rhs, obs_rhs, model_var, obs_var, obs_weight, depth,
        scratch=[pltpu.VMEM(model_rhs.shape, jnp.float32)] * 5 + [pltpu.SemaphoreType.DMA((6,))],
        space=pltpu.HBM,
    )
    depth_near = swapped(depth, 0)
    depth_edge = crossed(depth_near, outer, 1)
    pair, straight, local, _ = lax.optimization_barrier((pair, straight, local, depth_near))
    came = shifted(straight, 1)
    relayed = swapped(jnp.concatenate([came[:1], depth_edge]), 0)
    pair_near, pair_far = swapped(pair, 0), crossed(pair, middle)
    known = (pair, pair_near, pair_far, came, relayed, spin)
    local = shifted(local, 1)
    state, back = run(first_adjoint_kernel, [fields, fields], *known, work=4)
    held_state, local = lax.optimization_barrier((state, local))
    back = shifted(back, -1)
    state_far = crossed(held_state, middle)
    (tally,) = run(second_adjoint_kernel, [(4, rows, 128)], *known, local, state)
    state_near = swapped(state, 0)
    lead, sums = run(
        home_kernel, [fields, (8, rows, 128)],
        model_rhs, obs_rhs, model_var, obs_var, obs_weight, tally, back,
    )
    (rest,) = run(inner_forward_kernel, [fields], state, state_near, came, relayed, spin, lead)
    (sent,) = run(
        closing_kernel, [(ranks, 128)], state_far, rest, came, relayed, spin, sums,
        scratch=[pltpu.VMEM(fields, jnp.float32)],
    )
    gathered = lax.all_to_all(sent, ("win", "band", "half"), 0, 0, tiled=True)
    return run(
        combine_kernel, [model_rhs.shape] * 3,
        gathered, model_rhs, obs_rhs, model_var, obs_var, obs_weight, back,
    )


def solution(mesh):
    wins, lats = mesh.devices.shape
    mesh = Mesh(mesh.devices.reshape(wins, lats // 2, 2), ("win", "band", "half"))
    lat = ("band", "half")
    field = P("win", None, lat, None)
    in_specs = (field,) * 5 + (P("win", lat, None),)
    return jax.shard_map(body, mesh=mesh, in_specs=in_specs, out_specs=(field,) * 3, check_vma=False)
```

```python
import jax
import jax.numpy as jnp
from jax import lax
from jax.experimental import pallas as pl
from jax.experimental.pallas import tpu as pltpu
from jax.sharding import Mesh, PartitionSpec as P

GRID_ROWS = 768
STEPS = 4

mass_rate = 0.5
press_rate = 0.5
spin_rate = 0.4


def lon_gap(field):
    width = field.shape[-1]
    return pltpu.roll(field, width - 1, 1) - pltpu.roll(field, 1, 1)


def lat_gap(field):
    rows = field.shape[0]
    return pltpu.roll(field, rows - 1, 0) - pltpu.roll(field, 1, 0)


def even_lat():
    return lax.axis_index("half") == 0


def has_previous():
    return lax.axis_index("win") > 0


def stacked(own, near, far, index):
    even = even_lat()
    low = jnp.where(even, far[index], near[index])
    high = jnp.where(even, near[index], far[index])
    return jnp.concatenate([low, own[index], high], axis=0)


def prep_kernel(p, m, dvar, rvar, hobs, depth, pair, straight, local, pv, mv, dv, rv, hv, sems):
    copies = [
        pltpu.make_async_copy(source, target, sems.at[slot])
        for slot, (source, target) in enumerate(
            ((p, pv), (m, mv), (dvar, dv), (rvar, rv), (hobs, hv), (depth, straight.at[0:1]))
        )
    ]
    for copy in copies:
        copy.start()
    for copy in copies:
        copy.wait()
    for part in range(3):
        up = dv[0, part] * pv[0, part]
        seen = hv[0, part] * mv[0, part]
        pair[part] = pv[0, part]
        pair[3 + part] = up
        straight[1 + part] = pv[0, part] + seen
        local[part] = up + rv[0, part] * seen


def widened(tile, width):
    return jnp.concatenate([tile[...]] * (width // 128), axis=1)


def stretched(straight, relayed):
    even = even_lat()
    low = jnp.where(even, relayed[1], relayed[0])
    high = jnp.where(even, relayed[0], relayed[1])
    return 0.25 * jnp.concatenate([low, straight[0], high], axis=0)


def adjoint(pair, pair_near, pair_far, straight, relayed, spin, inside, base):
    depth = stretched(straight, relayed)
    turn, keep = widened(spin, depth.shape[1]), widened(inside, depth.shape[1])
    adj_height, adj_east, adj_north = [stacked(pair, pair_near, pair_far, base + part) for part in range(3)]
    for step in range(STEPS):
        adj_mid = adj_east - turn * adj_north
        adj_height = keep * (adj_height + 0.25 * (lat_gap(adj_north) + lon_gap(adj_mid)))
        adj_north = adj_north + turn * adj_mid + depth * lat_gap(adj_height)
        adj_east = adj_mid + depth * lon_gap(adj_height)
    rows = pair.shape[1]
    return [value[rows:2 * rows] for value in (adj_height, adj_east, adj_north)]


def first_adjoint_kernel(pair, pair_near, pair_far, straight, relayed, spin, inside, state, back):
    swept = adjoint(pair, pair_near, pair_far, straight, relayed, spin, inside, 0)
    link = has_previous()
    for part, value in enumerate(swept):
        back[part] = value
        state[part] = jnp.where(link, straight[1 + part] - value, 0.0)


def second_adjoint_kernel(pair, pair_near, pair_far, straight, relayed, spin, inside, local, state, tally):
    swept = adjoint(pair, pair_near, pair_far, straight, relayed, spin, inside, 3)
    link = has_previous()
    zero = jnp.zeros((pair.shape[1], 128), jnp.float32)
    cross = square = (zero, zero)
    for part, value in enumerate(swept):
        zx = jnp.where(link, local[part] - value, 0.0)
        cross = gathered_in(cross, zx * state[part])
        square = gathered_in(square, zx * zx)
    for slot, value in enumerate(cross + square):
        tally[slot] = value


def lane_sum(value):
    tiles = [value[:, start:start + 128] for start in range(0, value.shape[1], 128)]
    while len(tiles) > 1:
        tiles = [sum(tiles[at:at + 2]) for at in range(0, len(tiles), 2)]
    return tiles[0]


def two_sum(a, b):
    total = a + b
    part = total - a
    return total, (a - (total - part)) + (b - part)


def gathered_in(pair, value):
    total, rest = two_sum(pair[0], lane_sum(value))
    return total, pair[1] + rest


def folded(pair, shift, axis):
    total, rest = two_sum(pair[0], pltpu.roll(pair[0], shift, axis))
    return total, pair[1] + pltpu.roll(pair[1], shift, axis) + rest


def home_kernel(p, m, dvar, rvar, hobs, tally, back, lead, sums):
    last = lax.axis_index("win") == lax.axis_size("win") - 1
    zero = jnp.zeros_like(tally[0])
    m1 = m2 = (zero, zero)
    m3, m4 = (2.0 * tally[0], 2.0 * tally[1]), (tally[2], tally[3])
    for part in range(3):
        dv, rv, hv = dvar[0, part], rvar[0, part], hobs[0, part]
        pv, mv = p[0, part], m[0, part]
        up, um = dv * pv, rv * mv
        ux = pv - back[part] + hv * mv
        lead[part] = dv * up + ux
        zm = rv * um + hv * ux
        zx = jnp.where(last, up + hv * um, 0.0)
        m1 = gathered_in(m1, up * pv + um * mv)
        m2 = gathered_in(m2, up * up + um * um + ux * ux)
        m3 = gathered_in(m3, dv * up * up + rv * um * um + 2.0 * (zx * ux))
        m4 = gathered_in(m4, zm * zm + zx * zx)
    for slot, value in enumerate(m1 + m2 + m3 + m4):
        sums[slot] = value


def forward(height, east, north, depth, turn, keep, gap):
    for step in range(STEPS):
        height = keep * (height - (lon_gap(depth * east) + gap(depth * north)))
        east = east + turn * north - 0.25 * lon_gap(height)
        north = north - turn * east - 0.25 * gap(height)
    return height, east, north


def inner_forward_kernel(state, state_near, straight, relayed, spin, inside, rest):
    depth = stretched(straight, relayed)
    turn, keep = widened(spin, depth.shape[1]), widened(inside, depth.shape[1])
    even = even_lat()
    rows = state.shape[1]
    fields = []
    for part in range(3):
        low = jnp.where(even, 0.0, state_near[part])
        high = jnp.where(even, state_near[part], 0.0)
        fields.append(jnp.concatenate([low, state[part], high], axis=0))
    for part, value in enumerate(forward(*fields, depth, turn, keep, lat_gap)):
        rest[part] = value[rows:2 * rows]


def open_lat_gap(field):
    rows = field.shape[0]
    row = lax.broadcasted_iota(jnp.int32, field.shape, 0)
    above = jnp.where(row < rows - 1, pltpu.roll(field, rows - 1, 0), 0.0)
    below = jnp.where(row > 0, pltpu.roll(field, 1, 0), 0.0)
    return above - below


def closing_kernel(state_far, rest, straight, relayed, spin, inside, lead, sums, sent, remainder):
    even = even_lat()
    rows, width = state_far.shape[1:]
    middle = lax.axis_index("band") != lax.axis_index("half")

    @pl.when(middle)
    def _():
        depth = jnp.where(
            even,
            jnp.concatenate([relayed[1], straight[0]], axis=0),
            jnp.concatenate([straight[0], relayed[1]], axis=0),
        )
        turn, keep = [
            jnp.where(even, factor[:2 * rows], factor[rows:])
            for factor in (widened(spin, width), widened(inside, width))
        ]
        empty = jnp.zeros((rows, width), jnp.float32)
        fields = [
            jnp.where(
                even,
                jnp.concatenate([state_far[part], empty], axis=0),
                jnp.concatenate([empty, state_far[part]], axis=0),
            )
            for part in range(3)
        ]
        for part, value in enumerate(forward(*fields, 0.25 * depth, turn, keep, open_lat_gap)):
            remainder[part] = lead[part] - rest[part] - jnp.where(even, value[rows:], value[:rows])

    @pl.when(jnp.logical_not(middle))
    def _():
        for part in range(3):
            remainder[part] = lead[part] - rest[part]

    moments = [(sums[slot], sums[slot + 1]) for slot in range(0, 8, 2)]
    for part in range(3):
        moments[3] = gathered_in(moments[3], remainder[part] * remainder[part])
    lane = lax.broadcasted_iota(jnp.int32, (rows, 128), 1) // 16
    row = 0.0
    for slot, pair in enumerate(moments):
        for axis, shift in ((0, 4), (0, 2), (0, 1), (1, 64), (1, 32), (1, 16)):
            pair = folded(pair, shift, axis)
        row = jnp.where(lane == slot, pair[0], jnp.where(lane == slot + 4, pair[1], row))
    for start in range(0, sent.shape[0], rows):
        sent[start:start + rows] = row


def split(a):
    wide = 4097.0 * a
    top = wide - (wide - a)
    return top, a - top


def two_product(a, b):
    product = a * b
    a_top, a_low = split(a)
    b_top, b_low = split(b)
    return product, ((a_top * b_top - product) + a_top * b_low + a_low * b_top) + a_low * b_low


def pair_product(a, b):
    product, rest = two_product(a[0], b[0])
    return product, rest + (a[0] * b[1] + a[1] * b[0])


def pair_gap(a, b):
    total, rest = two_sum(a[0], -b[0])
    return total + (rest + (a[1] - b[1]))


def coefficients(gathered):
    pair = gathered[0:8], jnp.zeros((8, 128), jnp.float32)
    for start in range(8, gathered.shape[0], 8):
        total, rest = two_sum(pair[0], gathered[start:start + 8])
        pair = total, pair[1] + rest
    for axis, shift in ((0, 4), (0, 2), (0, 1), (1, 1), (1, 2), (1, 4), (1, 8)):
        pair = folded(pair, shift, axis)
    tops, lows = [], []
    for lane in range(15, 64, 16):
        top, low = [
            jnp.broadcast_to(value[0:1, at:at + 1], (1, 128))
            for value, at in ((pair[0], lane), (pair[1] + pltpu.roll(pair[0], 64, 1), lane))
        ]
        tops.append(top)
        lows.append(low)
    scale = 1.0 / tops[1]
    moments = []
    for value, rest in zip(tops, lows):
        product, error = two_product(value, scale)
        moments.append((product, error + rest * scale))
    m1, m2, m3, m4 = moments
    gap = pair_gap(pair_product(m2, m4), pair_product(m3, m3))
    y1 = pair_gap(pair_product(m1, m4), pair_product(m2, m3)) / gap
    y2 = pair_gap(pair_product(m2, m2), pair_product(m1, m3)) / gap
    return y1, y2


def combine_kernel(gathered, p, m, dvar, rvar, hobs, back, dual_model, dual_obs, increment, first, second, third, sems):
    y1, y2 = coefficients(gathered)
    rows, width = p.shape[2:]
    y1 = jnp.broadcast_to(jnp.concatenate([y1] * (width // 128), axis=1), (rows, width))
    y2 = jnp.broadcast_to(jnp.concatenate([y2] * (width // 128), axis=1), (rows, width))
    copies = [
        pltpu.make_async_copy(source, target, sems.at[slot])
        for slot, (source, target) in enumerate(((first, dual_model), (second, dual_obs), (third, increment)))
    ]
    for part in range(3):
        first[0, part] = (y1 + y2 * dvar[0, part]) * p[0, part]
    copies[0].start()
    for part in range(3):
        second[0, part] = (y1 + y2 * rvar[0, part]) * m[0, part]
    copies[1].start()
    for part in range(3):
        third[0, part] = y2 * (p[0, part] - back[part] + hobs[0, part] * m[0, part])
    copies[2].start()
    for copy in copies:
        copy.wait()


def run(kernel, out_shapes, *operands, scratch=(), space=pltpu.VMEM, target=pltpu.VMEM, work=4):
    shapes = [jax.ShapeDtypeStruct(shape, jnp.float32) for shape in out_shapes]
    size = sum(4 * operand.size for operand in operands) + sum(4 * shape.size for shape in shapes)
    if space is not pltpu.VMEM:
        operands = [pltpu.with_memory_space_constraint(operand, space) for operand in operands]
    return pl.pallas_call(
        kernel,
        out_shape=shapes,
        in_specs=[pl.BlockSpec(memory_space=space)] * len(operands),
        out_specs=[pl.BlockSpec(memory_space=target)] * len(shapes),
        scratch_shapes=scratch,
        compiler_params=pltpu.CompilerParams(vmem_limit_bytes=32 * 1024 * 1024),
        cost_estimate=pl.CostEstimate(flops=work * size // 4, bytes_accessed=work * size // 4, transcendentals=0),
    )(*operands)


def shifted(value, step):
    count = lax.axis_size("win")
    initial, last = (max(0, -step), min(count, count - step))
    return lax.ppermute(value, "win", [(source, source + step) for source in range(initial, last)])


def lat_count():
    return lax.axis_size("band") * lax.axis_size("half")


def lat_index():
    return lax.axis_index("band") * lax.axis_size("half") + lax.axis_index("half")


def swapped(value, first):
    pairs = []
    for lat in range(first, lat_count() - 1, 2):
        pairs += [(lat, lat + 1), (lat + 1, lat)]
    return lax.ppermute(value, ("band", "half"), pairs)


def crossed(value, ends, win_step=0):
    wins = lax.axis_size("win")
    pairs = []
    for win in range(wins):
        for source, target in (ends, ends[::-1]):
            if 0 <= win + win_step < wins:
                pairs.append((4 * win + source, 4 * (win + win_step) + target))
    return lax.ppermute(value, ("win", "band", "half"), pairs)


def body(model_rhs, obs_rhs, model_var, obs_var, obs_weight, depth):
    rows, width = model_rhs.shape[2:]
    ranks = lax.axis_size("win") * lat_count()
    total_rows = rows * lat_count()
    offset = (GRID_ROWS - total_rows) // 2
    local_rows = lat_index() * rows - rows + lax.broadcasted_iota(jnp.int32, (3 * rows, 128), 0)
    latitude = -jnp.pi / 2 + (local_rows.astype(jnp.float32) + offset + 0.5) * (jnp.pi / GRID_ROWS)
    inside = ((local_rows >= 0) & (local_rows < total_rows)).astype(jnp.float32)
    spin = inside * (mass_rate * spin_rate * jnp.sin(latitude))
    fields = (3, rows, width)

    middle, outer = (1, 2), (0, 3)
    pair, straight, local = run(
        prep_kernel, [(6, rows, width), (4, rows, width), fields],
        model_rhs, obs_rhs, model_var, obs_var, obs_weight, depth,
        scratch=[pltpu.VMEM(model_rhs.shape, jnp.float32)] * 5 + [pltpu.SemaphoreType.DMA((6,))],
        space=pltpu.HBM,
    )
    depth_near = swapped(depth, 0)
    depth_edge = crossed(depth_near, outer, 1)
    pair, straight, local, _ = lax.optimization_barrier((pair, straight, local, depth_near))
    came = shifted(straight, 1)
    relayed = swapped(jnp.concatenate([came[:1], depth_edge]), 0)
    pair_near, pair_far = swapped(pair, 0), crossed(pair, middle)
    known = (pair, pair_near, pair_far, came, relayed, spin, inside)
    local = shifted(local, 1)
    state, back = run(first_adjoint_kernel, [fields, fields], *known, work=4)
    held_state, local = lax.optimization_barrier((state, local))
    back = shifted(back, -1)
    state_far = crossed(held_state, middle)
    (tally,) = run(second_adjoint_kernel, [(4, rows, 128)], *known, local, state)
    state_near = swapped(state, 0)
    lead, sums = run(
        home_kernel, [fields, (8, rows, 128)],
        model_rhs, obs_rhs, model_var, obs_var, obs_weight, tally, back,
    )
    (rest,) = run(inner_forward_kernel, [fields], state, state_near, came, relayed, spin, inside)
    (sent,) = run(
        closing_kernel, [(ranks, 128)], state_far, rest, came, relayed, spin, inside, lead, sums,
        scratch=[pltpu.VMEM(fields, jnp.float32)],
    )
    gathered = lax.all_to_all(sent, ("win", "band", "half"), 0, 0, tiled=True)
    return run(
        combine_kernel, [model_rhs.shape] * 3,
        gathered, model_rhs, obs_rhs, model_var, obs_var, obs_weight, back, target=pltpu.HBM,
        scratch=[pltpu.VMEM(model_rhs.shape, jnp.float32)] * 3 + [pltpu.SemaphoreType.DMA((3,))],
    )


def solution(mesh):
    wins, lats = mesh.devices.shape
    mesh = Mesh(mesh.devices.reshape(wins, lats // 2, 2), ("win", "band", "half"))
    lat = ("band", "half")
    field = P("win", None, lat, None)
    in_specs = (field,) * 5 + (P("win", lat, None),)
    return jax.shard_map(body, mesh=mesh, in_specs=in_specs, out_specs=(field,) * 3, check_vma=False)
```
